32 devices in a mesh: fsdp: 8 (over y, x, core), seq: 4 (over z).
Axes of the slice: x: 2, y: 2, z: 4, core: 2. Of those that a mesh axis runs over, the one named last changes fastest.
Arguments:
- block_input: bfloat16 [8, 2048, 2560], P('fsdp', 'seq'), may hold values from -6 to 6
- cont_lengths: int32 [8, 4], P('fsdp'), may hold values from 1 to 384, 1024 in all within a row
- attn_gain: bfloat16 [2560], P('fsdp'), may hold values from 0.099609375 to 1.8984375
- q_down: bfloat16 [2560, 768], P('fsdp'), may hold values from -0.125 to 0.125
- q_gain: bfloat16 [768], P('fsdp'), may hold values from 0.099609375 to 1.8984375
- q_up: bfloat16 [768, 3840], P('fsdp'), may hold values from -0.21875 to 0.21875
- kv_down: bfloat16 [2560, 288], P('fsdp'), may hold values from -0.125 to 0.125
- kv_gain: bfloat16 [256], P('fsdp'), may hold values from 0.099609375 to 1.8984375
- kv_up: bfloat16 [256, 5120], P('fsdp'), may hold values from -0.375 to 0.375
- out_proj: bfloat16 [2560, 2560], P('fsdp'), may hold values from -12 to 12
- mlp_gain: bfloat16 [2560], P('fsdp'), may hold values from 0.099609375 to 1.8984375
- gate_up: bfloat16 [2560, 12800], P('fsdp'), may hold values from -0.125 to 0.125
- down_proj: bfloat16 [6400, 2560], P('fsdp'), may hold values from -0.625 to 0.625
- out_cotangent: bfloat16 [8, 2048, 2560], P('fsdp', 'seq'), may hold values from -6 to 6
Outputs:
- output: bfloat16 [8, 2048, 2560], P('fsdp', 'seq')
- grad_input: float32 [8, 2048, 2560], P('fsdp', 'seq')
- attn_gain_grad: float32 [2560], P('fsdp')
- q_down_grad: float32 [2560, 768], P('fsdp')
- q_gain_grad: float32 [768], P('fsdp')
- q_up_grad: float32 [768, 3840], P('fsdp')
- kv_down_grad: float32 [2560, 288], P('fsdp')
- kv_gain_grad: float32 [256], P('fsdp')
- kv_up_grad: float32 [256, 5120], P('fsdp')
- out_proj_grad: float32 [2560, 2560], P('fsdp')
- mlp_gain_grad: float32 [2560], P('fsdp')
- gate_up_grad: float32 [2560, 12800], P('fsdp')
- down_proj_grad: float32 [6400, 2560], P('fsdp')
The draws below stay inside these ranges and needn't reach their ends.
Inputs may be any that keep to these rules, and one draw needn't show every extreme that they name: `cont_lengths`: each group's 4 continuation lengths sum to 1024, each up to 384; in every group the longest has exactly 384 tokens.
All inputs are finite; a program needn't handle non-finite values.
Results may differ from the reference program's by a relative error of at most 0.02.
Values may be sent and summed in bfloat16 or wider, within the bound.
No kernel may reach another device: no remote copies, remote signals or barrier semaphores. Data moves between devices by JAX's collectives and lax.ppermute only.
A program may use at most 512 MiB of HBM per device.

```python
import math
import jax
import jax.numpy as jnp
import numpy as np
from jax import lax

D = 2560
HEADS = 40
NOPE = 64
ROPE = 32
VDIM = 64
QRANK = 768
KVRANK = 256
FF = 6400
PROMPT = 1024
CONTS = 4
CONT_AVG = 256
CONT_MOST = 384
GROUP = 2048
GROUPS = 8


def block_levels(own_key, shape, cuts, smallest, high):
    def one(dim, blocks):
        heights = jax.random.uniform(jax.random.fold_in(jax.random.fold_in(own_key, 6), dim), (blocks,), jnp.float32, smallest / len(cuts), high / len(cuts))
        return jnp.repeat(jnp.exp(heights), shape[dim] // blocks).reshape((-1,) + (1,) * (len(shape) - dim - 1))

    gain = one(*cuts[0])
    for cut in cuts[1:]:
        gain = gain * one(*cut)
    return gain


def length_profile(number_of, total, bound, lean):
    portions = [(1 << 20) // math.isqrt(grade ** lean) + 1 for grade in range(2, number_of + 1)]
    surplus, holding = total - bound - (number_of - 1), [1] * (number_of - 1)
    while surplus > 0:
        movable = [i for i in range(number_of - 1) if holding[i] < bound]
        pool, budget = sum([portions[i] for i in movable]), surplus
        for i in movable:
            more = min(bound - holding[i], max(1, budget * portions[i] // pool), surplus)
            holding[i] = holding[i] + more
            surplus = surplus - more
    return np.array([bound] + holding)


def ragged_sizes(key, amount, total, reach, slope):
    if amount == 2:
        one = jax.random.randint(key, (), max(1, total - reach), min(reach, total - 1) + 1)
        return jnp.stack([one, total - one])
    sizes = jnp.asarray(length_profile(amount, total, reach, slope), jnp.int32)
    pairs = (amount - 1) // 2
    source_of, taker = sizes[1:1 + 2 * pairs:2], sizes[2:2 + 2 * pairs:2]
    margin = jnp.minimum(source_of - 1, reach - taker)
    moved = jax.random.randint(jax.random.fold_in(key, 1), (pairs,), 0, 1 << 20) % (margin + 1)
    sizes = sizes.at[1:1 + 2 * pairs:2].set(source_of - moved).at[2:2 + 2 * pairs:2].set(taker + moved)
    return sizes[jax.random.permutation(jax.random.fold_in(key, 2), amount)]


def normal_values(key, extent, scale, most, pieces=(), kind=jnp.bfloat16):
    drawn = jax.random.normal(key, extent, jnp.float32) * scale
    if len(pieces) > 0:
        drawn = block_levels(key, extent, pieces, -0.22, 0.18) * drawn
    return jnp.clip(drawn, min=-most, max=most).astype(kind)


def setup_inputs(seed: int = 0) -> dict:
    seeds = jax.random.split(jax.random.key(seed), 15)
    return {
        "block_input": normal_values(seeds[0], (GROUPS, GROUP, D), 1.0, 6.0, ((0, 8), (1, 4))),
        "cont_lengths": jax.vmap(lambda own: ragged_sizes(own, CONTS, CONTS * CONT_AVG, CONT_MOST, 0))(jax.random.split(seeds[1], GROUPS)).reshape((GROUPS, CONTS)).astype(jnp.int32),
        "attn_gain": jnp.clip(1.0 + 0.18 * jax.random.normal(seeds[2], (D,), jnp.float32), 0.099609375, 1.8984375).astype(jnp.bfloat16),
        "q_down": normal_values(seeds[3], (D, QRANK), D ** -0.5, 0.125, ((0, 8),)),
        "q_gain": jnp.clip(1.0 + 0.18 * jax.random.normal(seeds[4], (QRANK,), jnp.float32), 0.099609375, 1.8984375).astype(jnp.bfloat16),
        "q_up": normal_values(seeds[5], (QRANK, HEADS * (NOPE + ROPE)), QRANK ** -0.5, 0.21875, ((0, 8),)),
        "kv_down": normal_values(seeds[6], (D, KVRANK + ROPE), D ** -0.5, 0.125, ((0, 8),)),
        "kv_gain": jnp.clip(1.0 + 0.18 * jax.random.normal(seeds[7], (KVRANK,), jnp.float32), 0.099609375, 1.8984375).astype(jnp.bfloat16),
        "kv_up": normal_values(seeds[8], (KVRANK, HEADS * (NOPE + VDIM)), KVRANK ** -0.5, 0.375, ((0, 8),)),
        "out_proj": normal_values(seeds[9], (HEADS * VDIM, D), 2.0, 12.0, ((0, 8),)),
        "mlp_gain": jnp.clip(1.0 + 0.18 * jax.random.normal(seeds[10], (D,), jnp.float32), 0.099609375, 1.8984375).astype(jnp.bfloat16),
        "gate_up": normal_values(seeds[11], (D, 2 * FF), D ** -0.5, 0.125, ((0, 8),)),
        "down_proj": normal_values(seeds[12], (FF, D), (FF // 64) ** -0.5, 0.625, ((0, 8),)),
        "out_cotangent": normal_values(seeds[13], (GROUPS, GROUP, D), 1.0, 6.0, ((0, 8), (1, 4))),
    }


@jax.custom_vjp
def low(v):
    return lax.optimization_barrier(v.astype(jnp.bfloat16)).astype(jnp.float32)

@jax.custom_vjp
def low_back(v):
    return v

def low_keep(v):
    return (low(v), None)

def low_pass(kept, grad):
    return (grad,)

def back_keep(v):
    return (v, None)

def back_low(kept, grad):
    return (low(grad),)
low.defvjp(low_keep, low_pass)
low_back.defvjp(back_keep, back_low)
variance_eps = 1e-05
depth_scale = 1.4 / math.sqrt(62.0)
masked_score = -1e+30

def matmul_high(left, right):
    return jnp.dot(left, right, precision=lax.Precision.HIGHEST)

def rms_norm(values, gain_vector):
    return values * lax.rsqrt(lax.optimization_barrier(jnp.mean(values * values, axis=-1, keepdims=True)) + variance_eps) * gain_vector

def rotate(values, cosine_table, sine_table):
    half_width = values.shape[-1] // 2
    first_half = values[..., :half_width]
    second = values[..., half_width:]
    return jnp.concatenate([first_half * cosine_table - second * sine_table, second * cosine_table + first_half * sine_table], axis=-1)

def layout(lengths, group_len, prompt_len):
    token_index = jnp.arange(group_len, dtype=jnp.int32)
    cont_ends = (prompt_len + jnp.cumsum(lengths)).astype(jnp.int32)
    starts = (cont_ends - lengths).astype(jnp.int32)
    started = (token_index[:, None] >= starts[None, :]).astype(jnp.int32)
    segment = lax.optimization_barrier(jnp.sum(started, axis=1)).astype(jnp.int32)
    own_start = lax.optimization_barrier(jnp.max(started * starts[None, :], axis=1)).astype(jnp.int32)
    position = jnp.where(segment > 0, prompt_len + token_index - own_start, token_index).astype(jnp.int32)
    return (segment, position)

def rope_tables(position, rope_width):
    steps_half = jnp.arange(rope_width // 2, dtype=jnp.float32)
    frequency = jnp.exp(steps_half * (-2.0 * math.log(10000.0) / rope_width))
    angles = position.astype(jnp.float32)[:, None] * frequency[None, :]
    return (jnp.cos(angles), jnp.sin(angles))

def attend_block(q_block, seg_block, idx_block, key_rows, value_rows, segment, token_index):
    score_scale = (NOPE + ROPE) ** (-0.5)
    raw_scores = jnp.einsum('qhd,khd->hqk', q_block, key_rows, precision=lax.Precision.HIGHEST) * score_scale
    raw_scores = low_back(raw_scores)
    allowed = (token_index[None, :] <= idx_block[:, None]) & ((segment[None, :] == seg_block[:, None]) | (segment[None, :] == 0))
    raw_scores = jnp.where(allowed[None], raw_scores, masked_score)
    row_max = lax.optimization_barrier(jnp.max(raw_scores, axis=-1, keepdims=True))
    unscaled = jnp.exp(raw_scores - row_max)
    attn_probs = low(unscaled / lax.optimization_barrier(jnp.sum(unscaled, axis=-1, keepdims=True)))
    return jnp.einsum('hqk,khd->qhd', attn_probs, value_rows, precision=lax.Precision.HIGHEST)

def attention(queries, key_rows, value_rows, segment):
    block_rows = min(512, GROUP)
    block_count = GROUP // block_rows
    token_index = jnp.arange(GROUP, dtype=jnp.int32)
    blocked = jax.checkpoint(lambda q_block, seg_block, idx_block: attend_block(q_block, seg_block, idx_block, key_rows, value_rows, segment, token_index))
    result = lax.map(lambda inputs: blocked(inputs[0], inputs[1], inputs[2]), (queries.reshape(block_count, block_rows, HEADS, NOPE + ROPE), segment.reshape(block_count, block_rows), token_index.reshape(block_count, block_rows)))
    return result.reshape(GROUP, HEADS, VDIM)

def group_forward(group_input, lengths, weights):
    attn_gain, q_down, q_gain, q_up, kv_down, kv_gain, kv_up, out_proj, mlp_gain, gate_up, down_proj = weights
    segment, position = layout(lengths, GROUP, PROMPT)
    cosine_table, sine_table = rope_tables(position, ROPE)
    normed = low(rms_norm(group_input, attn_gain))
    q_latent = low_back(matmul_high(normed, q_down))
    q_lat_normed = low(rms_norm(q_latent, q_gain))
    q_full = low_back(matmul_high(q_lat_normed, q_up)).reshape(GROUP, HEADS, NOPE + ROPE)
    queries = low_back(low(jnp.concatenate([q_full[..., :NOPE], rotate(q_full[..., NOPE:], cosine_table[:, None], sine_table[:, None])], axis=-1)))
    kv_latent = low_back(matmul_high(normed, kv_down))
    kv_normed = low(rms_norm(kv_latent[:, :KVRANK], kv_gain))
    key_rope = rotate(kv_latent[:, KVRANK:], cosine_table, sine_table)
    kv_full = matmul_high(kv_normed, kv_up).reshape(GROUP, HEADS, NOPE + VDIM)
    key_rows = low_back(low(jnp.concatenate([kv_full[..., :NOPE], jnp.broadcast_to(key_rope[:, None, :], (GROUP, HEADS, ROPE))], axis=-1)))
    value_rows = low_back(low(kv_full[..., NOPE:]))
    attended = low_back(low(attention(queries, key_rows, value_rows, segment)))
    attn_branch = low_back(matmul_high(attended.reshape(GROUP, HEADS * VDIM), out_proj))
    middle = group_input + depth_scale * attn_branch
    mlp_normed = low(rms_norm(middle, mlp_gain))
    gate_up_out = low_back(matmul_high(mlp_normed, gate_up))
    activated = low(jax.nn.silu(gate_up_out[:, :FF]) * gate_up_out[:, FF:])
    mlp_branch = low_back(matmul_high(activated, down_proj))
    return middle + depth_scale * mlp_branch

def reference(block_input, cont_lengths, attn_gain, q_down, q_gain, q_up, kv_down, kv_gain, kv_up, out_proj, mlp_gain, gate_up, down_proj, out_cotangent):
    weights = tuple((weight.astype(jnp.float32) for weight in (attn_gain, q_down, q_gain, q_up, kv_down, kv_gain, kv_up, out_proj, mlp_gain, gate_up, down_proj)))
    input_float = block_input.astype(jnp.float32)

    def forward_all(inputs_all, weight_set):
        group_fn = jax.checkpoint(group_forward)

        def scan_step(carried, group_items):
            return (carried, group_fn(group_items[0], group_items[1], weight_set))
        unused, outputs = lax.scan(scan_step, jnp.zeros((), jnp.float32), (inputs_all, cont_lengths))
        return outputs
    outputs, pullback = jax.vjp(forward_all, input_float, weights)
    grad_input, grad_weights = pullback(out_cotangent.astype(jnp.float32))
    return (outputs.astype(jnp.bfloat16), grad_input, grad_weights[0], grad_weights[1], grad_weights[2], grad_weights[3], grad_weights[4], grad_weights[5], grad_weights[6], grad_weights[7], grad_weights[8], grad_weights[9], grad_weights[10])
```

```python
import functools, math
import jax
import jax.numpy as jnp
from jax import lax
from jax.experimental import pallas as pl
from jax.experimental.pallas import tpu as pltpu
from jax.sharding import PartitionSpec as P

HEADS = 40
NOPE = 64
ROPE = 32
PROMPT = 1024
LANES = 128
NEG = -1e30
SCALE = (NOPE + ROPE) ** -0.5
LOG2E = math.log2(math.e)
LN2 = math.log(2.0)


def dot(a, b, ca, cb):
    return lax.dot_general(a, b, (((ca,), (cb,)), ((), ())), preferred_element_type=jnp.float32)


def fwd_kernel(bounds, qlat, qup, kvn, kvup, krope, cos, sin_r, sin_l, start, out, q_out, lse_out, m_scr, acc_scr, *, full_rows, mask_rows):
    rows = qlat.shape[0]
    lane = lax.broadcasted_iota(jnp.int32, (1, LANES), 1)
    low_half = lane < NOPE
    raw = dot(qlat[...], qup[...], 1, 0)
    for h in range(2):
        u = raw[:, h * LANES:(h + 1) * LANES]
        turned = u * cos[...] + pltpu.roll(u, 16, 1) * sin_r[...] + pltpu.roll(u, LANES - 16, 1) * sin_l[...]
        q_out[:, h * LANES:(h + 1) * LANES] = turned.astype(jnp.bfloat16)
    m_scr[...] = jnp.full_like(m_scr, NEG)
    acc_scr[...] = jnp.zeros_like(acc_scr)

    def block(first, size, masked):
        span = pl.ds(first, size)
        kv = dot(kvn[span, :], kvup[...], 1, 0).astype(jnp.bfloat16)
        rope_rows = krope[span, :]
        if masked:
            key_index = first + lax.broadcasted_iota(jnp.int32, (size, rows), 0)
            own = bounds[3] + lax.broadcasted_iota(jnp.int32, (size, rows), 1)
            allowed = (key_index <= own) & ((key_index >= start[...]) | (key_index < PROMPT))
        for h in range(2):
            kv_h = kv[:, h * LANES:(h + 1) * LANES]
            key = jnp.where(low_half, kv_h, rope_rows)
            val = jnp.where(low_half, jnp.ones_like(kv_h), kv_h)
            s = dot(key, q_out[:, h * LANES:(h + 1) * LANES], 1, 1)
            if masked:
                s = jnp.where(allowed, s, NEG)
            m_old = m_scr[h:h + 1, :]
            m_new = jnp.maximum(m_old, jnp.max(s, axis=0, keepdims=True))
            p = jnp.exp2(s - m_new)
            m_scr[h:h + 1, :] = m_new
            acc_scr[h] = acc_scr[h] * jnp.exp2(m_old - m_new) + dot(val, p.astype(jnp.bfloat16), 0, 0)

    lax.fori_loop(0, bounds[0], lambda i, c: (block(pl.multiple_of(i * full_rows, full_rows), full_rows, False), c)[1], 0)
    lax.fori_loop(bounds[1], bounds[2], lambda i, c: (block(pl.multiple_of(i * mask_rows, mask_rows), mask_rows, True), c)[1], 0)
    parts = []
    for h in range(2):
        total = acc_scr[h, 0:1, :]
        parts.append(acc_scr[h, NOPE:, :] / total)
        lse_out[h:h + 1, :] = m_scr[h:h + 1, :] + jnp.log2(total)
    out[...] = jnp.concatenate(parts, axis=0).T.astype(jnp.bfloat16)


def attend_forward(bounds, qlat, qup, kvn, kvup, krope, cos, sin_r, sin_l, start, full_rows=512, mask_rows=256):
    rows, rank = qlat.shape
    keys = kvn.shape[0]
    whole = lambda *_: (0, 0)
    col = lambda i, b: (0, i)
    pairs = HEADS // 2
    flops = pairs * 2 * 2 * rows * 1536 * LANES * 2
    return pl.pallas_call(
        functools.partial(fwd_kernel, full_rows=full_rows, mask_rows=mask_rows),
        grid_spec=pltpu.PrefetchScalarGridSpec(
            num_scalar_prefetch=1,
            grid=(pairs,),
            in_specs=[
                pl.BlockSpec((rows, rank), whole),
                pl.BlockSpec((rank, 2 * LANES), col),
                pl.BlockSpec(kvn.shape, whole),
                pl.BlockSpec((kvn.shape[1], 2 * LANES), col),
                pl.BlockSpec(krope.shape, whole),
                pl.BlockSpec(cos.shape, whole),
                pl.BlockSpec(cos.shape, whole),
                pl.BlockSpec(cos.shape, whole),
                pl.BlockSpec((1, rows), whole),
            ],
            out_specs=[
                pl.BlockSpec((rows, LANES), col),
                pl.BlockSpec((rows, 2 * LANES), col),
                pl.BlockSpec((8, rows), lambda i, b: (i, 0)),
            ],
            scratch_shapes=[pltpu.VMEM((8, rows), jnp.float32), pltpu.VMEM((2, LANES, rows), jnp.float32)],
        ),
        out_shape=[
            jax.ShapeDtypeStruct((rows, HEADS * NOPE), jnp.bfloat16),
            jax.ShapeDtypeStruct((rows, HEADS * LANES), jnp.bfloat16),
            jax.ShapeDtypeStruct((pairs * 8, rows), jnp.float32),
        ],
        compiler_params=pltpu.CompilerParams(vmem_limit_bytes=48 << 20),
        cost_estimate=pl.CostEstimate(flops=flops, bytes_accessed=30 << 20, transcendentals=HEADS * rows * 1536),
        name="attend_forward",
    )(bounds, qlat, qup, kvn, kvup, krope, cos, sin_r, sin_l, start)


def bwd_kernel(bounds, q, kvn, kvn_t, kvup, krope, grad_out, out, lse, cos, sin_r, sin_l, start, dq_out, dkvup, dkvn, drope, go_scr, dq_scr, delta_scr, *, full_rows, mask_rows):
    rows = q.shape[0]
    lane = lax.broadcasted_iota(jnp.int32, (1, LANES), 1)
    low_half = lane < NOPE

    @pl.when(pl.program_id(0) == 0)
    def _():
        dkvn[...] = jnp.zeros_like(dkvn)
        drope[...] = jnp.zeros_like(drope)

    go = grad_out[...].astype(jnp.float32)
    prod_t = (go * out[...].astype(jnp.float32)).T
    delta_scr[0:1, :] = jnp.sum(prod_t[:NOPE], axis=0, keepdims=True)
    delta_scr[1:2, :] = jnp.sum(prod_t[NOPE:], axis=0, keepdims=True)
    zero = jnp.zeros_like(go)
    go_scr[0] = jnp.where(low_half, zero, pltpu.roll(go, NOPE, 1)).astype(jnp.bfloat16)
    go_scr[1] = jnp.where(low_half, zero, go).astype(jnp.bfloat16)
    dq_scr[...] = jnp.zeros_like(dq_scr)
    dkvup[...] = jnp.zeros_like(dkvup)

    def block(first, size, masked):
        span = pl.ds(first, size)
        kv = dot(kvn[span, :], kvup[...], 1, 0).astype(jnp.bfloat16)
        rope_rows = krope[span, :]
        if masked:
            key_index = first + lax.broadcasted_iota(jnp.int32, (size, rows), 0)
            own = bounds[3] + lax.broadcasted_iota(jnp.int32, (size, rows), 1)
            allowed = (key_index <= own) & ((key_index >= start[...]) | (key_index < PROMPT))
        pieces = []
        rope_sum = None
        for h in range(2):
            kv_h = kv[:, h * LANES:(h + 1) * LANES]
            q_h = q[:, h * LANES:(h + 1) * LANES]
            key = jnp.where(low_half, kv_h, rope_rows)
            p = jnp.exp2(dot(key, q_h, 1, 1) - lse[h:h + 1, :])
            if masked:
                p = jnp.where(allowed, p, 0.0)
            ds = (p * (dot(kv_h, go_scr[h], 1, 1) - delta_scr[h:h + 1, :])).astype(jnp.bfloat16)
            dk = dot(ds, q_h, 1, 0) * LN2
            dv = dot(p.astype(jnp.bfloat16), go_scr[h], 1, 0)
            dq_scr[h] += dot(key, ds, 0, 0)
            pieces.append(jnp.where(low_half, dk, dv).astype(jnp.bfloat16))
            rope_sum = dk if rope_sum is None else rope_sum + dk
        dkv = jnp.concatenate(pieces, axis=1)
        drope[span, :] += rope_sum
        dkvn[span, :] += dot(dkv, kvup[...], 1, 1)
        dkvup[...] += dot(kvn_t[:, span], dkv, 1, 0)

    lax.fori_loop(0, bounds[0], lambda i, c: (block(pl.multiple_of(i * full_rows, full_rows), full_rows, False), c)[1], 0)
    lax.fori_loop(bounds[1], bounds[2], lambda i, c: (block(pl.multiple_of(i * mask_rows, mask_rows), mask_rows, True), c)[1], 0)
    for h in range(2):
        u = dq_scr[h].T * SCALE
        turned = u * cos[...] - pltpu.roll(u, 16, 1) * sin_r[...] - pltpu.roll(u, LANES - 16, 1) * sin_l[...]
        dq_out[:, h * LANES:(h + 1) * LANES] = turned.astype(jnp.bfloat16)


def attend_backward(bounds, q, kvn, kvn_t, kvup, krope, grad_out, out, lse, cos, sin_r, sin_l, start, full_rows=512, mask_rows=256):
    rows = q.shape[0]
    keys, rank = kvn.shape
    whole = lambda *_: (0, 0)
    col = lambda i, b: (0, i)
    pairs = HEADS // 2
    flops = pairs * 2 * 5 * rows * 1536 * LANES * 2
    return pl.pallas_call(
        functools.partial(bwd_kernel, full_rows=full_rows, mask_rows=mask_rows),
        grid_spec=pltpu.PrefetchScalarGridSpec(
            num_scalar_prefetch=1,
            grid=(pairs,),
            in_specs=[
                pl.BlockSpec((rows, 2 * LANES), col),
                pl.BlockSpec(kvn.shape, whole),
                pl.BlockSpec(kvn_t.shape, whole),
                pl.BlockSpec((rank, 2 * LANES), col),
                pl.BlockSpec(krope.shape, whole),
                pl.BlockSpec((rows, LANES), col),
                pl.BlockSpec((rows, LANES), col),
                pl.BlockSpec((8, rows), lambda i, b: (i, 0)),
                pl.BlockSpec(cos.shape, whole),
                pl.BlockSpec(cos.shape, whole),
                pl.BlockSpec(cos.shape, whole),
                pl.BlockSpec((1, rows), whole),
            ],
            out_specs=[
                pl.BlockSpec((rows, 2 * LANES), col),
                pl.BlockSpec((rank, 2 * LANES), col),
                pl.BlockSpec((keys, rank), whole),
                pl.BlockSpec((keys, LANES), whole),
            ],
            scratch_shapes=[
                pltpu.VMEM((2, rows, LANES), jnp.bfloat16),
                pltpu.VMEM((2, LANES, rows), jnp.float32),
                pltpu.VMEM((8, rows), jnp.float32),
            ],
        ),
        out_shape=[
            jax.ShapeDtypeStruct((rows, HEADS * LANES), jnp.bfloat16),
            jax.ShapeDtypeStruct((rank, HEADS * LANES), jnp.float32),
            jax.ShapeDtypeStruct((keys, rank), jnp.float32),
            jax.ShapeDtypeStruct((keys, LANES), jnp.float32),
        ],
        compiler_params=pltpu.CompilerParams(vmem_limit_bytes=48 << 20),
        cost_estimate=pl.CostEstimate(flops=flops, bytes_accessed=40 << 20, transcendentals=HEADS * rows * 1536),
        name="attend_backward",
    )(bounds, q, kvn, kvn_t, kvup, krope, grad_out, out, lse, cos, sin_r, sin_l, start)


D = 2560
FF = 6400
CONTS = 4
variance_eps = 1e-05
depth_scale = 1.4 / math.sqrt(62.0)
BF16 = jnp.bfloat16
F32 = jnp.float32


def rms_forward(values, gain_vector):
    inverse = lax.rsqrt(jnp.mean(values * values, axis=-1, keepdims=True) + variance_eps)
    return (values * inverse * gain_vector, inverse)


def rms_backward(values, inverse, gain_vector, upstream):
    scaled = upstream * gain_vector
    inner_mean = jnp.mean(scaled * values, axis=-1, keepdims=True)
    grad_values = inverse * scaled - values * inverse * inverse * inverse * inner_mean
    grad_gain = jnp.sum(upstream * values * inverse, axis=0)
    return (grad_values, grad_gain)


def segment_starts(lengths, index):
    own = jnp.zeros_like(index)
    begin = jnp.int32(PROMPT)
    for c in range(CONTS):
        own = jnp.where(index >= begin, begin, own)
        begin = begin + lengths[c]
    return own


def rope_tables(position):
    frequency = jnp.exp(jnp.arange(ROPE // 2, dtype=F32) * (-2.0 * math.log(10000.0) / ROPE))
    angles = position.astype(F32)[:, None] * frequency[None, :]
    cosine, sine = jnp.cos(angles), jnp.sin(angles)
    rows = position.shape[0]
    zeros = lambda n: jnp.zeros((rows, n), F32)
    return (
        jnp.concatenate([jnp.ones((rows, NOPE), F32), cosine, cosine, zeros(32)], axis=1),
        jnp.concatenate([zeros(80), sine, zeros(32)], axis=1),
        jnp.concatenate([zeros(64), -sine, zeros(48)], axis=1),
        cosine,
        sine,
    )


def rotate(values, cosine, sine):
    first, second = values[:, : ROPE // 2], values[:, ROPE // 2 :]
    return jnp.concatenate([first * cosine - second * sine, second * cosine + first * sine], axis=1)


def swap(tensor, bit, n):
    return lax.ppermute(tensor, "fsdp", [(i, i ^ bit) for i in range(n)])


def bit_orders(n):
    bits = []
    bit = 2
    while bit < n:
        bits.append(bit)
        bit *= 2
    return [bits, bits[::-1]]


def chip_gather(tensor, n):
    half = tensor.shape[0] // 2
    gathered = []
    for part, order in enumerate(bit_orders(n)):
        blocks = {0: tensor[part * half : (part + 1) * half]}
        for bit in order:
            blocks.update({r | bit: swap(block, bit, n) for r, block in list(blocks.items())})
        gathered.append(blocks)
    return [gathered[part][r] for r in range(0, n, 2) for part in range(2)]


def chip_scatter(pieces, n):
    sums = []
    for part, order in enumerate(bit_orders(n)):
        blocks = {r: pieces[r + part] for r in range(0, n, 2)}
        for bit in order[::-1]:
            kept = {r: block for r, block in blocks.items() if not r & bit}
            for r in kept:
                arrived = swap(blocks[r | bit].astype(BF16), bit, n)
                kept[r] = kept[r].astype(F32) + arrived.astype(F32)
            blocks = kept
        sums.append(blocks[0].astype(F32))
    return jnp.concatenate(sums, axis=0)


def body(
    n,
    block_input,
    cont_lengths,
    attn_gain,
    q_down,
    q_gain,
    q_up,
    kv_down,
    kv_gain,
    kv_up,
    out_proj,
    mlp_gain,
    gate_up,
    down_proj,
    out_cotangent,
):
    rows = block_input.shape[1]
    chips = n // 2
    ff_chip = FF // chips
    group_len = rows * lax.axis_size("seq")
    device = lax.axis_index("fsdp")
    core = device % 2
    same_core = [[2 * c + k for c in range(chips)] for k in range(2)]
    pairs = [[2 * c, 2 * c + 1] for c in range(chips)]
    rank_q, rank_kv = q_up.shape[0] * n, kv_up.shape[0] * n
    first_row = lax.axis_index("seq") * rows
    index = first_row + jnp.arange(rows, dtype=jnp.int32)
    own_start = segment_starts(cont_lengths[0], index)
    position = jnp.where(own_start > 0, PROMPT + index - own_start, index)
    cos, sin_r, sin_l, cosine, sine = rope_tables(position)
    fold = SCALE * LOG2E
    start_row = own_start[None, :]
    full_rows, mask_rows = 512, 256
    full_blocks = jnp.minimum(first_row, PROMPT) // full_rows
    bounds = jnp.stack([
        full_blocks,
        jnp.where(first_row < PROMPT, full_blocks * (full_rows // mask_rows), own_start[0] // mask_rows),
        (first_row + rows) // mask_rows,
        first_row,
    ]).astype(jnp.int32)

    gains = lax.all_gather(jnp.concatenate([attn_gain, mlp_gain, q_gain, kv_gain]), "fsdp", axis=0)
    widths = [v.shape[0] for v in (attn_gain, mlp_gain, q_gain, kv_gain)]
    gain_list = []
    at = 0
    for width in widths:
        gain_list.append(gains[:, at : at + width].reshape(-1).astype(F32))
        at += width
    attn_gain_all, mlp_gain_all, q_gain_all, kv_gain_all = gain_list

    down_all = lax.all_gather(jnp.concatenate([q_down, kv_down], axis=1), "fsdp", axis=0, tiled=True)
    q_up_wide = jnp.pad(q_up.reshape(-1, HEADS, NOPE + ROPE), ((0, 0), (0, 0), (0, ROPE))).reshape(-1, HEADS * LANES)
    q_up_all = lax.all_gather(q_up_wide, "fsdp", axis=0, tiled=True)
    kv_up_all = lax.all_gather(kv_up, "fsdp", axis=0, tiled=True)
    out_proj_all = lax.all_gather(out_proj, "fsdp", axis=0, tiled=True)

    token_rows = block_input[0].astype(F32)
    normed_float, attn_inverse = rms_forward(token_rows, attn_gain_all)
    normed = normed_float.astype(BF16)
    latent = jnp.dot(normed, down_all, preferred_element_type=F32)
    q_latent, kv_latent, rope_latent = jnp.split(latent, [rank_q, rank_q + rank_kv], axis=1)
    q_lat_float, q_inverse = rms_forward(q_latent, q_gain_all)
    q_lat_normed = q_lat_float.astype(BF16)
    kv_float, kv_inverse = rms_forward(kv_latent, kv_gain_all)
    key_rope = jnp.pad(rotate(rope_latent, cosine, sine), ((0, 0), (NOPE, LANES - NOPE - ROPE)))
    kv_own = jnp.concatenate([kv_float, key_rope], axis=1).astype(BF16)
    kv_all = lax.all_gather(kv_own, "seq", axis=0, tiled=True)
    kv_normed, key_rope_all = kv_all[:, :rank_kv], kv_all[:, rank_kv:]

    attended, queries, log_total = attend_forward(
        bounds, q_lat_normed, q_up_all, kv_normed, kv_up_all, key_rope_all,
        cos * fold, sin_r * fold, sin_l * fold, start_row, full_rows, mask_rows,
    )
    attn_branch = jnp.dot(attended, out_proj_all, preferred_element_type=F32)
    middle = token_rows + depth_scale * attn_branch
    mlp_float, mlp_inverse = rms_forward(middle, mlp_gain_all)

    hidden = gate_up.reshape(-1, 2, chips, ff_chip)
    hidden = lax.all_to_all(hidden, "fsdp", 2, 0, axis_index_groups=same_core)
    hidden = lax.all_gather(hidden.reshape(chips, -1, 2, ff_chip), "fsdp", axis=1, axis_index_groups=pairs)
    gate_w = hidden[:, :, :, 0].reshape(D, ff_chip)
    up_w = hidden[:, :, :, 1].reshape(D, ff_chip)
    down_w = lax.all_gather(down_proj, "fsdp", axis=0, tiled=True, axis_index_groups=pairs)

    cotangent = out_cotangent[0].astype(F32)
    grad_mlp = jnp.concatenate(chip_gather((depth_scale * cotangent).astype(BF16), n), axis=0)
    grad_act = dot(grad_mlp, down_w, 1, 1)
    mlp_normed = jnp.concatenate(chip_gather(mlp_float.astype(BF16), n), axis=0)
    gate_part = jnp.dot(mlp_normed, gate_w, preferred_element_type=F32)
    up_part = jnp.dot(mlp_normed, up_w, preferred_element_type=F32)
    gate_sigmoid = jax.nn.sigmoid(gate_part)
    silu_gate = gate_part * gate_sigmoid
    activated = (silu_gate * up_part).astype(BF16)
    grad_gate = (grad_act * up_part * gate_sigmoid * (1.0 + gate_part * (1.0 - gate_sigmoid))).astype(BF16)
    grad_up = (grad_act * silu_gate).astype(BF16)

    def pieces(whole):
        half = rows // 2
        return [whole[i * half : (i + 1) * half] for i in range(n)]

    grad_mlp_normed = chip_scatter(pieces((dot(grad_gate, gate_w, 1, 1) + dot(grad_up, up_w, 1, 1)).astype(BF16)), n)
    mlp_branch = chip_scatter(pieces(jnp.dot(activated, down_w, preferred_element_type=F32).astype(BF16)), n)
    output = (middle + depth_scale * mlp_branch).astype(BF16).reshape(block_input.shape)

    def keep_half(split):
        mine = lax.dynamic_index_in_dim(split, core, 1, keepdims=False)
        other = lax.dynamic_index_in_dim(split, 1 - core, 1, keepdims=False).astype(BF16)
        return (mine.astype(F32) + swap(other, 1, n).astype(F32)).astype(BF16)

    down_part = keep_half(dot(activated, grad_mlp, 0, 0).astype(BF16).reshape(1, 2, ff_chip // 2, D))[0]
    hidden_part = keep_half(
        jnp.stack([dot(mlp_normed, grad_gate, 0, 0).astype(BF16), dot(mlp_normed, grad_up, 0, 0).astype(BF16)], axis=1)
        .reshape(chips, 2, D // n, 2, ff_chip)
    )
    down_grad = lax.psum(down_part, "seq").astype(F32)
    hidden_part = lax.all_to_all(hidden_part, "fsdp", 0, 2, axis_index_groups=same_core)
    gate_up_grad = lax.psum(hidden_part.reshape(D // n, 2 * FF), "seq").astype(F32)

    grad_mid_norm, mlp_gain_part = rms_backward(middle, mlp_inverse, mlp_gain_all, grad_mlp_normed)
    grad_middle = cotangent + grad_mid_norm
    grad_attn = (depth_scale * grad_middle).astype(BF16)
    out_proj_part = dot(attended, grad_attn, 0, 0)
    grad_attended = dot(grad_attn, out_proj_all, 1, 1).astype(BF16)
    grad_q_full, kv_up_part, grad_kv_all, grad_rope_all = attend_backward(
        bounds, queries, kv_normed, kv_normed.T, kv_up_all, key_rope_all, grad_attended, attended, log_total,
        cos, sin_r, sin_l, start_row, full_rows, mask_rows,
    )
    q_up_part = dot(q_lat_normed, grad_q_full, 0, 0)
    grad_q_float, q_gain_part = rms_backward(q_latent, q_inverse, q_gain_all, dot(grad_q_full, q_up_all, 1, 1))
    grad_kv = lax.psum_scatter(
        jnp.concatenate([grad_kv_all, grad_rope_all], axis=1).astype(BF16), "seq", scatter_dimension=0, tiled=True
    ).astype(F32)
    grad_kv_first, kv_gain_part = rms_backward(kv_latent, kv_inverse, kv_gain_all, grad_kv[:, :rank_kv])
    grad_rope = rotate(grad_kv[:, rank_kv + NOPE : rank_kv + NOPE + ROPE], cosine, -sine)
    grad_latent = jnp.concatenate([grad_q_float, grad_kv_first, grad_rope], axis=1).astype(BF16)
    down_all_part = dot(normed, grad_latent, 0, 0)
    grad_normed = dot(grad_latent, down_all, 1, 1)
    grad_in_norm, attn_gain_part = rms_backward(token_rows, attn_inverse, attn_gain_all, grad_normed)
    grad_input = (grad_middle + grad_in_norm).reshape(block_input.shape)

    def reduced(part):
        share = lax.psum_scatter(part.astype(BF16), "fsdp", scatter_dimension=0, tiled=True)
        return lax.psum(share, "seq").astype(F32)

    down_all_grad = reduced(down_all_part)
    q_up_grad = reduced(q_up_part).reshape(-1, HEADS, LANES)[..., : NOPE + ROPE].reshape(-1, HEADS * (NOPE + ROPE))
    kv_up_grad = reduced(kv_up_part)
    out_proj_grad = reduced(out_proj_part)
    gain_parts = [v.reshape(n, -1) for v in (attn_gain_part, mlp_gain_part, q_gain_part, kv_gain_part)]
    gain_sum = reduced(jnp.concatenate(gain_parts, axis=1)).reshape(-1)
    attn_gain_grad, mlp_gain_grad, q_gain_grad, kv_gain_grad = jnp.split(
        gain_sum, [widths[0], widths[0] + widths[1], widths[0] + widths[1] + widths[2]]
    )
    return (
        output,
        grad_input,
        attn_gain_grad,
        down_all_grad[:, :rank_q],
        q_gain_grad,
        q_up_grad,
        down_all_grad[:, rank_q:],
        kv_gain_grad,
        kv_up_grad,
        out_proj_grad,
        mlp_gain_grad,
        gate_up_grad,
        down_grad,
    )


def solution(mesh):
    tokens, matrix, vector = P("fsdp", "seq", None), P("fsdp", None), P("fsdp")
    return jax.shard_map(
        functools.partial(body, mesh.shape["fsdp"]),
        mesh=mesh,
        in_specs=(tokens, matrix, vector, matrix, vector, matrix, matrix, vector, matrix, matrix, vector, matrix, matrix, tokens),
        out_specs=(tokens, tokens, vector, matrix, vector, matrix, matrix, vector, matrix, matrix, vector, matrix, matrix),
        check_vma=False,
    )
```

```python
import functools, math
import jax
import jax.numpy as jnp
from jax import lax
from jax.experimental import pallas as pl
from jax.experimental.pallas import tpu as pltpu
from jax.sharding import PartitionSpec as P

HEADS = 40
NOPE = 64
ROPE = 32
PROMPT = 1024
LANES = 128
NEG = -1e30
SCALE = (NOPE + ROPE) ** -0.5
LOG2E = math.log2(math.e)
LN2 = math.log(2.0)


LIGHT = pl.CostEstimate(flops=1 << 20, bytes_accessed=1 << 16, transcendentals=0)


def dot(a, b, ca, cb):
    return lax.dot_general(a, b, (((ca,), (cb,)), ((), ())), preferred_element_type=jnp.float32)


def flat(ref):
    return ref[...].reshape(-1, ref.shape[-1])


def fwd_kernel(bounds, qlat, qup_ref, kvn, kvup_ref, krope, cos, sin_r, sin_l, start, *rest, full_rows, mask_rows):
    out, q_out, lse_out, m_scr, acc_scr = rest[-5:]
    rows = qlat.shape[0]
    lane = lax.broadcasted_iota(jnp.int32, (1, LANES), 1)
    low_half = lane < NOPE
    raw = dot(qlat[...], flat(qup_ref), 1, 0)
    kvup = flat(kvup_ref)
    for h in range(2):
        u = raw[:, h * LANES:(h + 1) * LANES]
        turned = u * cos[...] + pltpu.roll(u, 16, 1) * sin_r[...] + pltpu.roll(u, LANES - 16, 1) * sin_l[...]
        q_out[:, h * LANES:(h + 1) * LANES] = turned.astype(jnp.bfloat16)
    m_scr[...] = jnp.full_like(m_scr, NEG)
    acc_scr[...] = jnp.zeros_like(acc_scr)

    def block(first, size, masked):
        span = pl.ds(first, size)
        kv = dot(kvn[span, :], kvup, 1, 0).astype(jnp.bfloat16)
        rope_rows = krope[span, :]
        if masked:
            key_index = first + lax.broadcasted_iota(jnp.int32, (size, rows), 0)
            own = bounds[3] + lax.broadcasted_iota(jnp.int32, (size, rows), 1)
            allowed = (key_index <= own) & ((key_index >= start[...]) | (key_index < PROMPT))
        for h in range(2):
            kv_h = kv[:, h * LANES:(h + 1) * LANES]
            key = jnp.where(low_half, kv_h, rope_rows)
            val = jnp.where(low_half, jnp.ones_like(kv_h), kv_h)
            s = dot(key, q_out[:, h * LANES:(h + 1) * LANES], 1, 1)
            if masked:
                s = jnp.where(allowed, s, NEG)
            m_old = m_scr[h:h + 1, :]
            m_new = jnp.maximum(m_old, jnp.max(s, axis=0, keepdims=True))
            p = jnp.exp2(s - m_new)
            m_scr[h:h + 1, :] = m_new
            acc_scr[h] = acc_scr[h] * jnp.exp2(m_old - m_new) + dot(val, p.astype(jnp.bfloat16), 0, 0)

    lax.fori_loop(0, bounds[0], lambda i, c: (block(pl.multiple_of(i * full_rows, full_rows), full_rows, False), c)[1], 0)
    lax.fori_loop(bounds[1], bounds[2], lambda i, c: (block(pl.multiple_of(i * mask_rows, mask_rows), mask_rows, True), c)[1], 0)
    parts = []
    for h in range(2):
        total = acc_scr[h, 0:1, :]
        parts.append(acc_scr[h, NOPE:, :] / total)
        lse_out[h:h + 1, :] = m_scr[h:h + 1, :] + jnp.log2(total)
    out[...] = jnp.concatenate(parts, axis=0).T.astype(jnp.bfloat16)


def attend_forward(part, prev, deps, bounds, qlat, up, kvn, krope, cos, sin_r, sin_l, start, full_rows, mask_rows):
    rows, rank = qlat.shape
    q_rows, kv_rows = rank // up.shape[0], kvn.shape[1] // up.shape[0]
    whole = lambda *_: (0, 0)
    first_pair, pairs = part
    col = lambda i, b: (0, i + first_pair)
    return pl.pallas_call(
        functools.partial(fwd_kernel, full_rows=full_rows, mask_rows=mask_rows),
        grid_spec=pltpu.PrefetchScalarGridSpec(
            num_scalar_prefetch=1,
            grid=(pairs,),
            in_specs=[
                pl.BlockSpec((rows, rank), whole),
                pl.BlockSpec((up.shape[0], q_rows, 2 * LANES), lambda i, b: (0, 0, i + first_pair)),
                pl.BlockSpec(kvn.shape, whole),
                pl.BlockSpec((up.shape[0], kv_rows, 2 * LANES), lambda i, b: (0, q_rows // kv_rows, i + first_pair)),
                pl.BlockSpec(krope.shape, whole),
                pl.BlockSpec(cos.shape, whole),
                pl.BlockSpec(cos.shape, whole),
                pl.BlockSpec(cos.shape, whole),
                pl.BlockSpec((1, rows), whole),
            ] + [pl.BlockSpec(memory_space=pl.ANY)] * (len(prev) + len(deps)),
            out_specs=[
                pl.BlockSpec((rows, LANES), col),
                pl.BlockSpec((rows, 2 * LANES), col),
                pl.BlockSpec((8, rows), lambda i, b: (i + first_pair, 0)),
            ],
            scratch_shapes=[pltpu.VMEM((8, rows), jnp.float32), pltpu.VMEM((2, LANES, rows), jnp.float32)],
        ),
        out_shape=[
            jax.ShapeDtypeStruct((rows, HEADS * NOPE), jnp.bfloat16),
            jax.ShapeDtypeStruct((rows, HEADS * LANES), jnp.bfloat16),
            jax.ShapeDtypeStruct((HEADS // 2 * 8, rows), jnp.float32),
        ],
        compiler_params=pltpu.CompilerParams(vmem_limit_bytes=48 << 20),
        cost_estimate=LIGHT,
        input_output_aliases={10 + i: i for i in range(len(prev))},
        name="attend_forward",
    )(bounds, qlat, up, kvn, up, krope, cos, sin_r, sin_l, start, *prev, *deps)


def bwd_kernel(bounds, qlat_t, qup_ref, q, kvn, kvn_t, kvup_ref, krope, grad_out, out, lse, cos, sin_r, sin_l, start, *rest, full_rows, mask_rows, resumes):
    dqup_out, dkvup_out, dkvn, drope, dqlat, go_scr, dq_scr, delta_scr, dkvup = rest[-9:]
    kvup = flat(kvup_ref)
    rows = q.shape[0]
    lane = lax.broadcasted_iota(jnp.int32, (1, LANES), 1)
    low_half = lane < NOPE

    @pl.when(pl.program_id(0) == 0)
    def _():
        dkvn[...] = rest[-12][...] if resumes else jnp.zeros_like(dkvn)
        drope[...] = rest[-11][...] if resumes else jnp.zeros_like(drope)
        dqlat[...] = rest[-10][...] if resumes else jnp.zeros_like(dqlat)

    go = grad_out[...].astype(jnp.float32)
    prod_t = (go * out[...].astype(jnp.float32)).T
    delta_scr[0:1, :] = jnp.sum(prod_t[:NOPE], axis=0, keepdims=True)
    delta_scr[1:2, :] = jnp.sum(prod_t[NOPE:], axis=0, keepdims=True)
    zero = jnp.zeros_like(go)
    go_scr[0] = jnp.where(low_half, zero, pltpu.roll(go, NOPE, 1)).astype(jnp.bfloat16)
    go_scr[1] = jnp.where(low_half, zero, go).astype(jnp.bfloat16)
    dq_scr[...] = jnp.zeros_like(dq_scr)
    dkvup[...] = jnp.zeros_like(dkvup)

    def block(first, size, masked):
        span = pl.ds(first, size)
        kv = dot(kvn[span, :], kvup, 1, 0).astype(jnp.bfloat16)
        rope_rows = krope[span, :]
        if masked:
            key_index = first + lax.broadcasted_iota(jnp.int32, (size, rows), 0)
            own = bounds[3] + lax.broadcasted_iota(jnp.int32, (size, rows), 1)
            allowed = (key_index <= own) & ((key_index >= start[...]) | (key_index < PROMPT))
        pieces = []
        rope_sum = None
        for h in range(2):
            kv_h = kv[:, h * LANES:(h + 1) * LANES]
            q_h = q[:, h * LANES:(h + 1) * LANES]
            key = jnp.where(low_half, kv_h, rope_rows)
            p = jnp.exp2(dot(key, q_h, 1, 1) - lse[h:h + 1, :])
            if masked:
                p = jnp.where(allowed, p, 0.0)
            ds = (p * (dot(kv_h, go_scr[h], 1, 1) - delta_scr[h:h + 1, :])).astype(jnp.bfloat16)
            dk = dot(ds, q_h, 1, 0) * LN2
            dv = dot(p.astype(jnp.bfloat16), go_scr[h], 1, 0)
            dq_scr[h] += dot(key, ds, 0, 0)
            pieces.append(jnp.where(low_half, dk, dv).astype(jnp.bfloat16))
            rope_sum = dk if rope_sum is None else rope_sum + dk
        dkv = jnp.concatenate(pieces, axis=1)
        drope[span, :] += rope_sum
        dkvn[span, :] += dot(dkv, kvup, 1, 1)
        dkvup[...] += dot(kvn_t[:, span], dkv, 1, 0)

    lax.fori_loop(0, bounds[0], lambda i, c: (block(pl.multiple_of(i * full_rows, full_rows), full_rows, False), c)[1], 0)
    lax.fori_loop(bounds[1], bounds[2], lambda i, c: (block(pl.multiple_of(i * mask_rows, mask_rows), mask_rows, True), c)[1], 0)
    turned = []
    for h in range(2):
        u = dq_scr[h].T * SCALE
        turned.append(u * cos[...] - pltpu.roll(u, 16, 1) * sin_r[...] - pltpu.roll(u, LANES - 16, 1) * sin_l[...])
    dq = jnp.concatenate(turned, axis=1).astype(jnp.bfloat16)
    dqlat[...] += dot(dq, flat(qup_ref), 1, 1)
    dqup_out[...] = dot(qlat_t[...], dq, 1, 0).astype(jnp.bfloat16).reshape(dqup_out.shape)
    dkvup_out[...] = dkvup[...].astype(jnp.bfloat16).reshape(dkvup_out.shape)


def attend_backward(part, prev, deps, bounds, qlat_t, up, q, kvn, kvn_t, krope, grad_out, out, lse, cos, sin_r, sin_l, start, full_rows, mask_rows):
    rows = q.shape[0]
    keys, rank = kvn.shape
    devices = up.shape[0]
    q_rows, kv_rows = qlat_t.shape[0] // devices, rank // devices
    up_block = lambda i, b: (0, 0, i + first_pair)
    whole = lambda *_: (0, 0)
    first_pair, pairs = part
    col = lambda i, b: (0, i + first_pair)
    return pl.pallas_call(
        functools.partial(bwd_kernel, full_rows=full_rows, mask_rows=mask_rows, resumes=bool(prev)),
        grid_spec=pltpu.PrefetchScalarGridSpec(
            num_scalar_prefetch=1,
            grid=(pairs,),
            in_specs=[
                pl.BlockSpec(qlat_t.shape, whole),
                pl.BlockSpec((devices, q_rows, 2 * LANES), up_block),
                pl.BlockSpec((rows, 2 * LANES), col),
                pl.BlockSpec(kvn.shape, whole),
                pl.BlockSpec(kvn_t.shape, whole),
                pl.BlockSpec((devices, kv_rows, 2 * LANES), lambda i, b: (0, q_rows // kv_rows, i + first_pair)),
                pl.BlockSpec(krope.shape, whole),
                pl.BlockSpec((rows, LANES), col),
                pl.BlockSpec((rows, LANES), col),
                pl.BlockSpec((8, rows), lambda i, b: (i + first_pair, 0)),
                pl.BlockSpec(cos.shape, whole),
                pl.BlockSpec(cos.shape, whole),
                pl.BlockSpec(cos.shape, whole),
                pl.BlockSpec((1, rows), whole),
            ] + [pl.BlockSpec(memory_space=pl.ANY)] * (len(prev[:2]) + len(deps)) + [pl.BlockSpec(v.shape, whole) for v in prev[2:]],
            out_specs=[
                pl.BlockSpec((devices, q_rows, 2 * LANES), up_block),
                pl.BlockSpec((devices, kv_rows, 2 * LANES), up_block),
                pl.BlockSpec((keys, rank), whole),
                pl.BlockSpec((keys, LANES), whole),
                pl.BlockSpec((rows, qlat_t.shape[0]), whole),
            ],
            scratch_shapes=[
                pltpu.VMEM((2, rows, LANES), jnp.bfloat16),
                pltpu.VMEM((2, LANES, rows), jnp.float32),
                pltpu.VMEM((8, rows), jnp.float32),
                pltpu.VMEM((rank, 2 * LANES), jnp.float32),
            ],
        ),
        out_shape=[
            jax.ShapeDtypeStruct((devices, q_rows, HEADS * LANES), jnp.bfloat16),
            jax.ShapeDtypeStruct((devices, kv_rows, HEADS * LANES), jnp.bfloat16),
            jax.ShapeDtypeStruct((keys, rank), jnp.float32),
            jax.ShapeDtypeStruct((keys, LANES), jnp.float32),
            jax.ShapeDtypeStruct((rows, qlat_t.shape[0]), jnp.float32),
        ],
        compiler_params=pltpu.CompilerParams(vmem_limit_bytes=48 << 20),
        cost_estimate=LIGHT,
        input_output_aliases={15 + i: i for i in range(len(prev[:2]))},
        name="attend_backward",
    )(bounds, qlat_t, up, q, kvn, kvn_t, up, krope, grad_out, out, lse, cos, sin_r, sin_l, start, *prev[:2], *deps, *prev[2:])


def hidden_kernel(*refs, count):
    normed, grads, (gate_w, up_w, down_w) = refs[:count], refs[count : 2 * count], refs[2 * count : 2 * count + 3]
    active, grad_gate, grad_up = refs[-3:]
    height = normed[0].shape[0]
    for i in range(count):
        rows = slice(i * height, (i + 1) * height)
        x = normed[i][...]
        gate = dot(x, gate_w[...], 1, 0)
        upper = dot(x, up_w[...], 1, 0)
        grad = dot(grads[i][...], down_w[...], 1, 1)
        sigmoid = jax.nn.sigmoid(gate)
        silu = gate * sigmoid
        active[rows, :] = (silu * upper).astype(jnp.bfloat16)
        grad_gate[rows, :] = (grad * upper * sigmoid * (1.0 + gate * (1.0 - sigmoid))).astype(jnp.bfloat16)
        grad_up[rows, :] = (grad * silu).astype(jnp.bfloat16)


def hidden_units(first_row, all_rows, prev, normed, grads, gate_w, up_w, down_w):
    count = len(normed)
    height, width = normed[0].shape
    rows, hidden = count * height, gate_w.shape[1]
    tile = 2 * LANES
    whole = lambda j: (0, 0)
    at = first_row // rows
    return pl.pallas_call(
        functools.partial(hidden_kernel, count=count),
        grid=(pl.cdiv(hidden, tile),),
        in_specs=[pl.BlockSpec((height, width), whole)] * (2 * count)
        + [pl.BlockSpec((width, tile), lambda j: (0, j))] * 2
        + [pl.BlockSpec((tile, width), lambda j: (j, 0))]
        + [pl.BlockSpec(memory_space=pl.ANY)] * len(prev),
        out_specs=[pl.BlockSpec((rows, tile), lambda j: (at, j))] * 3,
        out_shape=[jax.ShapeDtypeStruct((all_rows, hidden), jnp.bfloat16)] * 3,
        input_output_aliases={2 * count + 3 + i: i for i in range(len(prev))},
        compiler_params=pltpu.CompilerParams(vmem_limit_bytes=48 << 20),
        cost_estimate=LIGHT,
        name="hidden_units",
    )(*normed, *grads, gate_w, up_w, down_w, *prev)


def back_kernel(*refs, terms, contract):
    left, right, outs = refs[:terms], refs[terms : 2 * terms], refs[2 * terms :]
    height = outs[0].shape[0]
    for i, out in enumerate(outs):
        rows = slice(i * height, (i + 1) * height)
        total = dot(left[0][rows, :], right[0][...], 1, contract)
        for a, b in zip(left[1:], right[1:]):
            total = total + dot(a[rows, :], b[...], 1, contract)
        out[...] = total.astype(jnp.bfloat16)


def to_tokens(first_row, height, count, left, right, contract):
    hidden = left[0].shape[1]
    width = right[0].shape[1 - contract]
    rows = height * count
    tile = 2 * LANES
    at = first_row // rows
    if contract:
        right_spec = pl.BlockSpec((tile, hidden), lambda j: (j, 0))
    else:
        right_spec = pl.BlockSpec((hidden, tile), lambda j: (0, j))
    return pl.pallas_call(
        functools.partial(back_kernel, terms=len(left), contract=contract),
        grid=(width // tile,),
        in_specs=[pl.BlockSpec((rows, hidden), lambda j: (at, 0))] * len(left) + [right_spec] * len(left),
        out_specs=[pl.BlockSpec((height, tile), lambda j: (0, j))] * count,
        out_shape=[jax.ShapeDtypeStruct((height, width), jnp.bfloat16)] * count,
        compiler_params=pltpu.CompilerParams(vmem_limit_bytes=48 << 20),
        cost_estimate=LIGHT,
        name="to_tokens",
    )(*left, *right)


def blank(shape):
    return pl.pallas_call(
        lambda out: None,
        out_specs=pl.BlockSpec(memory_space=pl.ANY),
        out_shape=jax.ShapeDtypeStruct(shape, jnp.bfloat16),
        cost_estimate=LIGHT,
        name="blank",
    )()


D = 2560
FF = 6400
CONTS = 4
variance_eps = 1e-05
depth_scale = 1.4 / math.sqrt(62.0)
BF16 = jnp.bfloat16
F32 = jnp.float32


def rms_forward(values, gain_vector):
    inverse = lax.rsqrt(jnp.mean(values * values, axis=-1, keepdims=True) + variance_eps)
    return (values * inverse * gain_vector, inverse)


def rms_backward(values, inverse, gain_vector, upstream):
    scaled = upstream * gain_vector
    inner_mean = jnp.mean(scaled * values, axis=-1, keepdims=True)
    grad_values = inverse * scaled - values * inverse * inverse * inverse * inner_mean
    grad_gain = jnp.sum(upstream * values * inverse, axis=0)
    return (grad_values, grad_gain)


def segment_starts(lengths, index):
    own = jnp.zeros_like(index)
    begin = jnp.int32(PROMPT)
    for c in range(CONTS):
        own = jnp.where(index >= begin, begin, own)
        begin = begin + lengths[c]
    return own


def rope_tables(position):
    frequency = jnp.exp(jnp.arange(ROPE // 2, dtype=F32) * (-2.0 * math.log(10000.0) / ROPE))
    angles = position.astype(F32)[:, None] * frequency[None, :]
    cosine, sine = jnp.cos(angles), jnp.sin(angles)
    rows = position.shape[0]
    zeros = lambda n: jnp.zeros((rows, n), F32)
    return (
        jnp.concatenate([jnp.ones((rows, NOPE), F32), cosine, cosine, zeros(32)], axis=1),
        jnp.concatenate([zeros(80), sine, zeros(32)], axis=1),
        jnp.concatenate([zeros(64), -sine, zeros(48)], axis=1),
        cosine,
        sine,
    )


def rotate(values, cosine, sine):
    first, second = values[:, : ROPE // 2], values[:, ROPE // 2 :]
    return jnp.concatenate([first * cosine - second * sine, second * cosine + first * sine], axis=1)


def swap(tensor, bit, n):
    return lax.ppermute(tensor, "fsdp", [(i, i ^ bit) for i in range(n)])


def bit_orders(n):
    bits = []
    bit = 2
    while bit < n:
        bits.append(bit)
        bit *= 2
    return [bits, bits[::-1]]


def arrivals(n):
    orders = bit_orders(n)
    steps = [[(0, part) for part in range(2)]]
    for at in range(len(orders[0])):
        steps.append([
            (r | order[at], part)
            for part, order in enumerate(orders)
            for r in range(0, n, 2)
            if not r & ~sum(order[:at])
        ])
    return steps


ATTEND_PARTS = ((0, 4), (4, 5), (9, 6), (15, HEADS // 2 - 15))


def own_blocks(tensor):
    half = tensor.shape[0] // 2
    return {(0, part): tensor[part * half : (part + 1) * half] for part in range(2)}


def gather_step(blocks, n, at):
    return {
        (r | order[at], p): swap(block, order[at], n)
        for part, order in enumerate(bit_orders(n))
        for (r, p), block in blocks.items()
        if p == part
    }


def scatter_step(blocks, n, at, hold=None):
    arrived = {}
    for part, order in enumerate(bit_orders(n)):
        bit = order[at]
        for r, p in blocks:
            if p == part and not r & bit:
                arrived[r, p] = swap(blocks[r | bit, p].astype(BF16), bit, n)
    if hold is not None:
        hold, arrived = tie(hold, arrived)
    return {key: blocks[key].astype(F32) + block.astype(F32) for key, block in arrived.items()}, hold


def chip_scatter(blocks, n):
    for at in range(len(bit_orders(n)[0]))[::-1]:
        blocks, _ = scatter_step(blocks, n, at)
    return jnp.concatenate([blocks[0, part] for part in range(2)])


def tie(*trees):
    return lax.optimization_barrier(trees)


def ring(shift, count):
    return [(i, (i + shift) % count) for i in range(count)]


def seq_gather(share, layer, layers):
    whole = jnp.zeros((layers, *share.shape), share.dtype)
    for shift in range(layers):
        block = lax.ppermute(share, "seq", ring(shift, layers)) if shift else share
        whole = lax.dynamic_update_index_in_dim(whole, block, (layer - shift) % layers, 0)
    return whole.reshape(-1, *share.shape[1:])


def seq_scatter(whole, layer, layers):
    shares = whole.reshape(layers, -1, *whole.shape[1:])
    total = pick(shares, layer).astype(F32)
    for shift in range(1, layers):
        total = total + lax.ppermute(pick(shares, (layer + shift) % layers), "seq", ring(shift, layers)).astype(F32)
    return total


def pick(tensor, at, axis=0):
    return lax.dynamic_index_in_dim(tensor, at, axis, keepdims=False)


def core_scatter(split, core, n, axis=0):
    arrived = swap(pick(split, 1 - core, axis).astype(BF16), 1, n)
    return pick(split, core, axis).astype(F32) + arrived.astype(F32)


def core_shares(part, n):
    return jnp.swapaxes(part.astype(BF16).reshape(n // 2, 2, part.shape[0] // n, part.shape[1]), 0, 1)


def chip_blocks(mine, chip, n):
    half = mine.shape[1] // 2
    blocks = {}
    for r in range(0, n, 2):
        own = pick(mine, chip ^ (r // 2))
        for p in range(2):
            blocks[r, p] = own[p * half : (p + 1) * half]
    return blocks


def fsdp_scatter(part, core, chip, n):
    return chip_scatter(chip_blocks(core_scatter(core_shares(part, n), core, n).astype(BF16), chip, n), n)


def body(
    n,
    block_input,
    cont_lengths,
    attn_gain,
    q_down,
    q_gain,
    q_up,
    kv_down,
    kv_gain,
    kv_up,
    out_proj,
    mlp_gain,
    gate_up,
    down_proj,
    out_cotangent,
):
    rows = block_input.shape[1]
    chips = n // 2
    ff_chip = FF // chips
    ff_sent = -(-ff_chip // LANES) * LANES
    ff_wide = ff_sent
    group_len = rows * lax.axis_size("seq")
    device = lax.axis_index("fsdp")
    core, chip = device % 2, device // 2
    layers = lax.axis_size("seq")
    layer = lax.axis_index("seq")
    rank_q, rank_kv = q_up.shape[0] * n, kv_up.shape[0] * n
    first_row = lax.axis_index("seq") * rows
    index = first_row + jnp.arange(rows, dtype=jnp.int32)
    own_start = segment_starts(cont_lengths[0], index)
    position = jnp.where(own_start > 0, PROMPT + index - own_start, index)
    cos, sin_r, sin_l, cosine, sine = rope_tables(position)
    fold = SCALE * LOG2E
    start_row = own_start[None, :]
    full_rows, mask_rows = 1024, 512
    full_blocks = jnp.minimum(first_row, PROMPT) // full_rows
    bounds = jnp.stack([
        full_blocks,
        jnp.where(first_row < PROMPT, full_blocks * (full_rows // mask_rows), own_start[0] // mask_rows),
        (first_row + rows + mask_rows - 1) // mask_rows,
        first_row,
    ]).astype(jnp.int32)

    gains = lax.all_gather(jnp.concatenate([attn_gain, mlp_gain, q_gain, kv_gain]), "fsdp", axis=0)
    widths = [v.shape[0] for v in (attn_gain, mlp_gain, q_gain, kv_gain)]
    gain_list = []
    at = 0
    for width in widths:
        gain_list.append(gains[:, at : at + width].reshape(-1).astype(F32))
        at += width
    attn_gain_all, mlp_gain_all, q_gain_all, kv_gain_all = gain_list

    down_all = lax.all_gather(jnp.concatenate([q_down, kv_down], axis=1), "fsdp", axis=0, tiled=True)
    q_up_wide = jnp.pad(q_up.reshape(-1, HEADS, NOPE + ROPE), ((0, 0), (0, 0), (0, ROPE))).reshape(-1, HEADS * LANES)
    q_rows = q_up.shape[0]
    up_all = lax.all_gather(jnp.concatenate([q_up_wide, kv_up], axis=0), "fsdp", axis=0)
    out_proj_all = lax.all_gather(out_proj, "fsdp", axis=0, tiled=True)

    steps = arrivals(n)
    fetch = (D // n) // layers
    half_down = swap(down_proj, 1, n)
    down_w = jnp.concatenate([
        jnp.where(core == 0, down_proj, half_down),
        jnp.where(core == 0, half_down, down_proj),
        jnp.zeros((ff_wide - ff_chip, D), BF16),
    ])
    own_fetch = lax.dynamic_slice_in_dim(gate_up, layer * fetch, fetch, 0)
    widen = lambda v: jnp.pad(v, ((0, 0), (0, ff_sent - ff_chip)))
    own_fetch = jnp.stack([
        jnp.stack([widen(own_fetch[:, at + c * ff_chip : at + (c + 1) * ff_chip]) for at in (0, FF)]) for c in range(chips)
    ])
    own_fetch = [pick(own_fetch, chip ^ (r // 2)) for r in range(0, n, 2)]
    tables = (cos * fold, sin_r * fold, sin_l * fold, cos, sin_r, sin_l)
    down_all, tables, down_w, own_fetch = tie(down_all, tables, down_w, own_fetch)

    token_rows = block_input[0].astype(F32)
    normed_float, attn_inverse = rms_forward(token_rows, attn_gain_all)
    normed = normed_float.astype(BF16)
    latent = jnp.dot(normed, down_all, preferred_element_type=F32)
    q_latent, kv_latent, rope_latent = jnp.split(latent, [rank_q, rank_q + rank_kv], axis=1)
    q_lat_float, q_inverse = rms_forward(q_latent, q_gain_all)
    q_lat_normed = q_lat_float.astype(BF16)
    kv_float, kv_inverse = rms_forward(kv_latent, kv_gain_all)
    key_rope = jnp.pad(rotate(rope_latent, cosine, sine), ((0, 0), (NOPE, LANES - NOPE - ROPE)))
    kv_own = jnp.concatenate([kv_float, key_rope], axis=1).astype(BF16)
    kv_all = seq_gather(kv_own, layer, layers)
    cotangent = out_cotangent[0].astype(F32)
    grad_low = (depth_scale * cotangent).astype(BF16)
    up_all, kv_all, own_fetch, grad_low = tie(up_all, kv_all, own_fetch, grad_low)
    kv_normed, key_rope_all = kv_all[:, :rank_kv], kv_all[:, rank_kv:]
    forward_args = (
        bounds, q_lat_normed, up_all, kv_normed, key_rope_all,
        *tables[:3], start_row, full_rows, mask_rows,
    )

    fetched_blocks = [swap(block, 2 * r, n) if r else block for r, block in enumerate(own_fetch)]
    outputs = attend_forward(ATTEND_PARTS[0], [], [], *forward_args)
    outputs, fetched_blocks, grad_low = tie(outputs, fetched_blocks, grad_low)
    fetched = blank((2, chips, fetch, ff_sent))
    for r, block in enumerate(fetched_blocks):
        fetched = lax.dynamic_update_slice(fetched, block[:, None], (0, chip ^ r, 0, 0))
    grad_blocks = own_blocks(grad_low)
    passed = [(fetched, fetched)]
    for step in range(1, layers):
        link = (
            lax.ppermute(passed[-1][0], "seq", [(i, i + 1) for i in range(layers - 1)]),
            lax.ppermute(passed[-1][1], "seq", [(i + 1, i) for i in range(layers - 1)]),
        )
        moved = gather_step(grad_blocks, n, step - 1) if step < len(steps) else {}
        if step < len(ATTEND_PARTS):
            outputs = attend_forward(ATTEND_PARTS[step], outputs, [], *forward_args)
            outputs, link, moved = tie(outputs, link, moved)
        passed.append(link)
        grad_blocks = {**grad_blocks, **moved}
    for part in ATTEND_PARTS[layers:]:
        outputs = attend_forward(part, outputs, [], *forward_args)
    attended, queries, log_total = outputs
    attn_branch = jnp.dot(attended, out_proj_all, preferred_element_type=F32)
    middle = token_rows + depth_scale * attn_branch
    mlp_float, mlp_inverse = rms_forward(middle, mlp_gain_all)
    normed_blocks = own_blocks(mlp_float.astype(BF16))
    normed_blocks = {**normed_blocks, **gather_step(normed_blocks, n, 0)}
    normed_blocks, passed, grad_blocks = tie(normed_blocks, passed, grad_blocks)
    layer_blocks = [jnp.where(layer >= shift, passed[shift][0], passed[layers - shift][1]) for shift in range(1, layers)]
    for at in range(1, len(steps) - 1):
        normed_blocks = {**normed_blocks, **gather_step(normed_blocks, n, at)}
    hidden = [blank((chips, 2, layers, fetch, ff_wide)) for _ in range(2)]
    for shift in range(layers):
        block = layer_blocks[shift - 1] if shift else fetched
        source = (layer - shift) % layers
        for owner, arrived in ((core, block), (1 - core, swap(block, 1, n))):
            hidden = [
                lax.dynamic_update_slice(whole, v[:, None, None], (0, owner, source, 0, 0)) for whole, v in zip(hidden, arrived)
            ]
    gate_w, up_w = (v.reshape(D, ff_wide) for v in hidden)
    half = rows // 2
    first_rows = [sum(len(step) for step in steps[:i]) * half for i in range(len(steps))]
    kept = []
    for step, at in zip(steps, first_rows):
        kept = hidden_units(
            at, n * half, kept, [normed_blocks[key] for key in step], [grad_blocks[key] for key in step], gate_w, up_w, down_w
        )
    active, grad_gate, grad_up = kept
    all_normed = jnp.concatenate([normed_blocks[key] for step in steps for key in step])
    all_grad = jnp.concatenate([grad_blocks[key] for step in steps for key in step])

    back = lambda i, hidden: dict(zip(steps[i], to_tokens(first_rows[i], half, len(steps[i]), hidden, [gate_w, up_w], 1)))
    down_whole = dot(active, all_grad, 0, 0).astype(BF16)
    down_whole, grad_gate, grad_up = tie(down_whole, grad_gate, grad_up)
    last_blocks = back(-1, [grad_gate, grad_up])
    last_blocks, earlier = tie(last_blocks, [grad_gate, grad_up])
    half_ff = ff_chip // 2
    half_of = lambda at: lax.dynamic_slice_in_dim(down_whole, at * half_ff, half_ff, 0)
    down_part = (half_of(core).astype(F32) + swap(half_of(1 - core), 1, n).astype(F32)).astype(BF16)
    last_blocks, down_part, earlier = tie(last_blocks, down_part, [grad_gate, grad_up])
    down_share = lax.psum_scatter(down_part, "seq", scatter_dimension=0, tiled=True)
    early_blocks = {}
    for i in range(len(steps) - 1)[::-1]:
        early_blocks.update(back(i, earlier))
    blocks, _ = scatter_step({**last_blocks, **early_blocks}, n, len(steps) - 2)
    blocks, all_normed = tie(blocks, all_normed)
    hidden_parts, hidden_shares, crossing = [], [], []
    for grads in (grad_gate, grad_up):
        whole = dot(all_normed, grads, 0, 0).astype(BF16).reshape(chips, 2, layers, fetch, ff_wide)
        crossing.append((pick(whole, core, 1), swap(pick(whole, 1 - core, 1), 1, n)))
    for at in range(len(steps) - 2)[::-1]:
        blocks, _ = scatter_step(blocks, n, at)

    def over_layers(crossed):
        part = (crossed[0].astype(F32) + crossed[1].astype(F32)).astype(BF16).transpose(1, 0, 2, 3)
        hidden_parts.append(part)
        hidden_shares.append(lax.psum_scatter(part, "seq", scatter_dimension=0, tiled=True)[0])

    blocks, crossing[0], down_share = tie(blocks, crossing[0], down_share)
    over_layers(crossing[0])
    grad_mlp_normed = jnp.concatenate([blocks[0, part] for part in range(2)]).astype(F32)
    grad_mid_norm, mlp_gain_part = rms_backward(middle, mlp_inverse, mlp_gain_all, grad_mlp_normed)
    grad_middle = cotangent + grad_mid_norm
    grad_attn = (depth_scale * grad_middle).astype(BF16)
    out_proj_part = dot(attended, grad_attn, 0, 0).astype(BF16)
    grad_attended = dot(grad_attn, out_proj_all, 1, 1).astype(BF16)
    grad_attended, crossing[1] = tie(grad_attended, crossing[1])
    over_layers(crossing[1])
    backward_args = (
        bounds, q_lat_normed.T, up_all, queries, kv_normed, kv_normed.T, key_rope_all, grad_attended, attended, log_total,
        *tables[3:], start_row, full_rows, mask_rows,
    )
    out_shares = core_shares(out_proj_part, n)
    out_arrived = swap(pick(out_shares, 1 - core), 1, n)
    thirds = ((0, 12), (12, 4), (16, HEADS // 2 - 16))
    first = attend_backward(thirds[0], [], [*hidden_parts, out_proj_part], *backward_args)
    first, out_arrived = tie(first, out_arrived)
    out_mine = (pick(out_shares, core).astype(F32) + out_arrived.astype(F32)).astype(BF16)
    down_low = lax.all_gather(down_share, "seq", axis=0, tiled=True)
    second = attend_backward(thirds[1], first, [down_share, *hidden_shares], *backward_args)
    hidden_share = jnp.stack(hidden_shares)
    hidden_blocks = []
    for r in range(0, n, 2):
        block = pick(hidden_share, chip ^ (r // 2), 1)
        hidden_blocks.append(swap(block, r, n) if r else block)
    second, hidden_blocks = tie(second, hidden_blocks)
    hidden_blocks = jnp.stack(hidden_blocks)
    hidden_blocks = [pick(hidden_blocks, chip ^ c)[..., :ff_chip] for c in range(chips)]
    placed = jnp.concatenate([block[at] for at in range(2) for block in hidden_blocks], axis=1)
    out_blocks, second = scatter_step(chip_blocks(out_mine, chip, n), n, len(steps) - 2, second)
    third = attend_backward(thirds[2], second, [placed], *backward_args)
    for at in range(len(steps) - 2)[::-1]:
        out_blocks, third = scatter_step(out_blocks, n, at, third)
    out_share = jnp.concatenate([out_blocks[0, part] for part in range(2)]).astype(BF16)
    gate_up_low = lax.all_gather(placed, "seq", axis=0, tiled=True)
    q_up_part, kv_up_part, grad_kv_all, grad_rope_all, grad_q_lat = third
    grad_q_float, q_gain_part = rms_backward(q_latent, q_inverse, q_gain_all, grad_q_lat)
    grad_kv = seq_scatter(jnp.concatenate([grad_kv_all, grad_rope_all], axis=1).astype(BF16), layer, layers)
    up_parts = jnp.concatenate([q_up_part, kv_up_part], axis=1).reshape(-1, HEADS * LANES)
    up_share = fsdp_scatter(up_parts, core, chip, n).astype(BF16)
    grad_kv, active_last = tie(grad_kv, active)
    branch = {}
    for step, at in zip(steps, first_rows):
        branch.update(zip(step, to_tokens(at, half, len(step), [active_last], [down_w], 0)))
    grad_kv, up_share, out_share, down_low, gate_up_low, branch = tie(
        grad_kv, up_share, out_share, down_low, gate_up_low, branch
    )
    up_grad, out_proj_grad = lax.psum((up_share, out_share), "seq")
    down_grad, gate_up_grad = down_low.astype(F32), gate_up_low.astype(F32)
    grad_kv_first, kv_gain_part = rms_backward(kv_latent, kv_inverse, kv_gain_all, grad_kv[:, :rank_kv])
    grad_rope = rotate(grad_kv[:, rank_kv + NOPE : rank_kv + NOPE + ROPE], cosine, -sine)
    grad_latent = jnp.concatenate([grad_q_float, grad_kv_first, grad_rope], axis=1).astype(BF16)
    down_all_part = dot(normed, grad_latent, 0, 0)
    grad_normed = dot(grad_latent, down_all, 1, 1)
    grad_in_norm, attn_gain_part = rms_backward(token_rows, attn_inverse, attn_gain_all, grad_normed)
    grad_input = (grad_middle + grad_in_norm).reshape(block_input.shape)

    gain_parts = [v.reshape(n, -1) for v in (attn_gain_part, mlp_gain_part, q_gain_part, kv_gain_part)]
    gain_rows = jnp.concatenate(gain_parts, axis=1)
    gain_rows = jnp.pad(gain_rows[:, None], ((0, 0), (0, 15), (0, latent.shape[1] - gain_rows.shape[1])))
    down_rows = D // n
    down_all_part = jnp.concatenate([down_all_part.reshape(n, down_rows, -1), gain_rows], axis=1)
    down_all_share = fsdp_scatter(down_all_part.reshape(-1, latent.shape[1]), core, chip, n).astype(BF16)
    branch, down_all_share = scatter_step(branch, n, len(steps) - 2, down_all_share)
    for at in range(len(steps) - 2)[::-1]:
        branch, _ = scatter_step(branch, n, at)
    mlp_branch = jnp.concatenate([branch[0, part] for part in range(2)])
    output = (middle + depth_scale * mlp_branch).astype(BF16).reshape(block_input.shape)
    up_grad, out_proj_grad, down_all_share = tie(up_grad, out_proj_grad, down_all_share)
    down_all_grad = lax.psum(down_all_share, "seq").astype(F32)
    up_grad, out_proj_grad = up_grad.astype(F32), out_proj_grad.astype(F32)
    gain_sum = down_all_grad[down_rows]
    down_all_grad = down_all_grad[:down_rows]
    q_up_grad = up_grad[:q_rows].reshape(-1, HEADS, LANES)[..., : NOPE + ROPE].reshape(-1, HEADS * (NOPE + ROPE))
    kv_up_grad = up_grad[q_rows:]
    ends = [sum(widths[: i + 1]) for i in range(4)]
    attn_gain_grad, mlp_gain_grad, q_gain_grad, kv_gain_grad = jnp.split(gain_sum[: ends[3]], ends[:3])
    return (
        output,
        grad_input,
        attn_gain_grad,
        down_all_grad[:, :rank_q],
        q_gain_grad,
        q_up_grad,
        down_all_grad[:, rank_q:],
        kv_gain_grad,
        kv_up_grad,
        out_proj_grad,
        mlp_gain_grad,
        gate_up_grad,
        down_grad,
    )


def solution(mesh):
    tokens, matrix, vector = P("fsdp", "seq", None), P("fsdp", None), P("fsdp")
    return jax.shard_map(
        functools.partial(body, mesh.shape["fsdp"]),
        mesh=mesh,
        in_specs=(tokens, matrix, vector, matrix, vector, matrix, matrix, vector, matrix, matrix, vector, matrix, matrix, tokens),
        out_specs=(tokens, tokens, vector, matrix, vector, matrix, matrix, vector, matrix, matrix, vector, matrix, matrix),
        check_vma=False,
    )
```

```python
import functools, math
import jax
import jax.numpy as jnp
from jax import lax
from jax.experimental import pallas as pl
from jax.experimental.pallas import tpu as pltpu
from jax.sharding import PartitionSpec as P

HEADS = 40
NOPE = 64
ROPE = 32
PROMPT = 1024
LANES = 128
NEG = -1e30
SCALE = (NOPE + ROPE) ** -0.5
LOG2E = math.log2(math.e)
LN2 = math.log(2.0)


LIGHT = pl.CostEstimate(flops=1 << 20, bytes_accessed=1 << 16, transcendentals=0)


def dot(a, b, ca, cb):
    return lax.dot_general(a, b, (((ca,), (cb,)), ((), ())), preferred_element_type=jnp.float32)


def flat(ref):
    return ref[...].reshape(-1, ref.shape[-1])


def fwd_kernel(bounds, qlat, qup_ref, kvn, kvup_ref, krope, cos, sin_r, sin_l, start, *rest, full_rows, mask_rows):
    out, q_out, lse_out, m_scr, acc_scr = rest[-5:]
    rows = qlat.shape[0]
    lane = lax.broadcasted_iota(jnp.int32, (1, LANES), 1)
    low_half = lane < NOPE
    raw = dot(qlat[...], flat(qup_ref), 1, 0)
    kvup = flat(kvup_ref)
    for h in range(2):
        u = raw[:, h * LANES:(h + 1) * LANES]
        turned = u * cos[...] + pltpu.roll(u, 16, 1) * sin_r[...] + pltpu.roll(u, LANES - 16, 1) * sin_l[...]
        q_out[:, h * LANES:(h + 1) * LANES] = turned.astype(jnp.bfloat16)
    m_scr[...] = jnp.full_like(m_scr, NEG)
    acc_scr[...] = jnp.zeros_like(acc_scr)

    def block(first, size, masked):
        span = pl.ds(first, size)
        kv = dot(kvn[span, :], kvup, 1, 0).astype(jnp.bfloat16)
        rope_rows = krope[span, :]
        if masked:
            key_index = first + lax.broadcasted_iota(jnp.int32, (size, rows), 0)
            own = bounds[3] + lax.broadcasted_iota(jnp.int32, (size, rows), 1)
            allowed = (key_index <= own) & ((key_index >= start[...]) | (key_index < PROMPT))
        scores, vals = [], []
        for h in range(2):
            kv_h = kv[:, h * LANES:(h + 1) * LANES]
            key = jnp.where(low_half, kv_h, rope_rows)
            vals.append(jnp.where(low_half, jnp.ones_like(kv_h), kv_h))
            s = dot(key, q_out[:, h * LANES:(h + 1) * LANES], 1, 1)
            scores.append(jnp.where(allowed, s, NEG) if masked else s)
        for h in range(2):
            m_old = m_scr[h:h + 1, :]
            m_new = jnp.maximum(m_old, jnp.max(scores[h], axis=0, keepdims=True))
            m_scr[h:h + 1, :] = m_new
            p = jnp.exp2(scores[h] - m_new).astype(jnp.bfloat16)
            acc_scr[h] = acc_scr[h] * jnp.exp2(m_old - m_new) + dot(vals[h], p, 0, 0)

    lax.fori_loop(0, bounds[0], lambda i, c: (block(pl.multiple_of(i * full_rows, full_rows), full_rows, False), c)[1], 0)
    lax.fori_loop(bounds[1], bounds[2], lambda i, c: (block(pl.multiple_of(i * mask_rows, mask_rows), mask_rows, True), c)[1], 0)
    parts = []
    for h in range(2):
        total = acc_scr[h, 0:1, :]
        parts.append(acc_scr[h, NOPE:, :] / total)
        lse_out[h:h + 1, :] = m_scr[h:h + 1, :] + jnp.log2(total)
    out[...] = jnp.concatenate(parts, axis=0).T.astype(jnp.bfloat16)


def attend_forward(part, prev, deps, bounds, qlat, up, kvn, krope, cos, sin_r, sin_l, start, full_rows, mask_rows):
    rows, rank = qlat.shape
    q_rows, kv_rows = rank // up.shape[0], kvn.shape[1] // up.shape[0]
    whole = lambda *_: (0, 0)
    first_pair, pairs = part
    col = lambda i, b: (0, i + first_pair)
    return pl.pallas_call(
        functools.partial(fwd_kernel, full_rows=full_rows, mask_rows=mask_rows),
        grid_spec=pltpu.PrefetchScalarGridSpec(
            num_scalar_prefetch=1,
            grid=(pairs,),
            in_specs=[
                pl.BlockSpec((rows, rank), whole),
                pl.BlockSpec((up.shape[0], q_rows, 2 * LANES), lambda i, b: (0, 0, i + first_pair)),
                pl.BlockSpec(kvn.shape, whole),
                pl.BlockSpec((up.shape[0], kv_rows, 2 * LANES), lambda i, b: (0, q_rows // kv_rows, i + first_pair)),
                pl.BlockSpec(krope.shape, whole),
                pl.BlockSpec(cos.shape, whole),
                pl.BlockSpec(cos.shape, whole),
                pl.BlockSpec(cos.shape, whole),
                pl.BlockSpec((1, rows), whole),
            ] + [pl.BlockSpec(memory_space=pl.ANY)] * (len(prev) + len(deps)),
            out_specs=[
                pl.BlockSpec((rows, LANES), col),
                pl.BlockSpec((rows, 2 * LANES), col),
                pl.BlockSpec((8, rows), lambda i, b: (i + first_pair, 0)),
            ],
            scratch_shapes=[pltpu.VMEM((8, rows), jnp.float32), pltpu.VMEM((2, LANES, rows), jnp.float32)],
        ),
        out_shape=[
            jax.ShapeDtypeStruct((rows, HEADS * NOPE), jnp.bfloat16),
            jax.ShapeDtypeStruct((rows, HEADS * LANES), jnp.bfloat16),
            jax.ShapeDtypeStruct((HEADS // 2 * 8, rows), jnp.float32),
        ],
        compiler_params=pltpu.CompilerParams(vmem_limit_bytes=48 << 20),
        cost_estimate=LIGHT,
        input_output_aliases={10 + i: i for i in range(len(prev))},
        name="attend_forward",
    )(bounds, qlat, up, kvn, up, krope, cos, sin_r, sin_l, start, *prev, *deps)


def bwd_kernel(bounds, qlat_t, qup_ref, q, kvn, kvn_t, kvup_ref, krope, grad_out, out, lse, cos, sin_r, sin_l, start, *rest, full_rows, mask_rows, resumes):
    dqup_out, dkvup_out, dkvn, drope, dqlat, go_scr, dq_scr, delta_scr, dkvup = rest[-9:]
    kvup = flat(kvup_ref)
    rows = q.shape[0]
    lane = lax.broadcasted_iota(jnp.int32, (1, LANES), 1)
    low_half = lane < NOPE

    @pl.when(pl.program_id(0) == 0)
    def _():
        dkvn[...] = rest[-12][...] if resumes else jnp.zeros_like(dkvn)
        drope[...] = rest[-11][...] if resumes else jnp.zeros_like(drope)
        dqlat[...] = rest[-10][...] if resumes else jnp.zeros_like(dqlat)

    go = grad_out[...].astype(jnp.float32)
    prod_t = (go * out[...].astype(jnp.float32)).T
    delta_scr[0:1, :] = jnp.sum(prod_t[:NOPE], axis=0, keepdims=True)
    delta_scr[1:2, :] = jnp.sum(prod_t[NOPE:], axis=0, keepdims=True)
    zero = jnp.zeros_like(go)
    go_scr[0] = jnp.where(low_half, zero, pltpu.roll(go, NOPE, 1)).astype(jnp.bfloat16)
    go_scr[1] = jnp.where(low_half, zero, go).astype(jnp.bfloat16)
    dq_scr[...] = jnp.zeros_like(dq_scr)
    dkvup[...] = jnp.zeros_like(dkvup)

    def block(first, size, masked):
        span = pl.ds(first, size)
        kv = dot(kvn[span, :], kvup, 1, 0).astype(jnp.bfloat16)
        rope_rows = krope[span, :]
        if masked:
            key_index = first + lax.broadcasted_iota(jnp.int32, (size, rows), 0)
            own = bounds[3] + lax.broadcasted_iota(jnp.int32, (size, rows), 1)
            allowed = (key_index <= own) & ((key_index >= start[...]) | (key_index < PROMPT))
        pieces = []
        rope_sum = None
        for h in range(2):
            kv_h = kv[:, h * LANES:(h + 1) * LANES]
            q_h = q[:, h * LANES:(h + 1) * LANES]
            key = jnp.where(low_half, kv_h, rope_rows)
            p = jnp.exp2(dot(key, q_h, 1, 1) - lse[h:h + 1, :])
            if masked:
                p = jnp.where(allowed, p, 0.0)
            ds = (p * (dot(kv_h, go_scr[h], 1, 1) - delta_scr[h:h + 1, :])).astype(jnp.bfloat16)
            dk = dot(ds, q_h, 1, 0) * LN2
            dv = dot(p.astype(jnp.bfloat16), go_scr[h], 1, 0)
            dq_scr[h] += dot(key, ds, 0, 0)
            pieces.append(jnp.where(low_half, dk, dv).astype(jnp.bfloat16))
            rope_sum = dk if rope_sum is None else rope_sum + dk
        dkv = jnp.concatenate(pieces, axis=1)
        drope[span, :] += rope_sum
        dkvn[span, :] += dot(dkv, kvup, 1, 1)
        dkvup[...] += dot(kvn_t[:, span], dkv, 1, 0)

    lax.fori_loop(0, bounds[0], lambda i, c: (block(pl.multiple_of(i * full_rows, full_rows), full_rows, False), c)[1], 0)
    lax.fori_loop(bounds[1], bounds[2], lambda i, c: (block(pl.multiple_of(i * mask_rows, mask_rows), mask_rows, True), c)[1], 0)
    turned = []
    for h in range(2):
        u = dq_scr[h].T * SCALE
        turned.append(u * cos[...] - pltpu.roll(u, 16, 1) * sin_r[...] - pltpu.roll(u, LANES - 16, 1) * sin_l[...])
    dq = jnp.concatenate(turned, axis=1).astype(jnp.bfloat16)
    dqlat[...] += dot(dq, flat(qup_ref), 1, 1)
    dqup_out[...] = dot(qlat_t[...], dq, 1, 0).astype(jnp.bfloat16).reshape(dqup_out.shape)
    dkvup_out[...] = dkvup[...].astype(jnp.bfloat16).reshape(dkvup_out.shape)


def attend_backward(part, prev, deps, bounds, qlat_t, up, q, kvn, kvn_t, krope, grad_out, out, lse, cos, sin_r, sin_l, start, full_rows, mask_rows):
    rows = q.shape[0]
    keys, rank = kvn.shape
    devices = up.shape[0]
    q_rows, kv_rows = qlat_t.shape[0] // devices, rank // devices
    up_block = lambda i, b: (0, 0, i + first_pair)
    whole = lambda *_: (0, 0)
    first_pair, pairs = part
    col = lambda i, b: (0, i + first_pair)
    return pl.pallas_call(
        functools.partial(bwd_kernel, full_rows=full_rows, mask_rows=mask_rows, resumes=bool(prev)),
        grid_spec=pltpu.PrefetchScalarGridSpec(
            num_scalar_prefetch=1,
            grid=(pairs,),
            in_specs=[
                pl.BlockSpec(qlat_t.shape, whole),
                pl.BlockSpec((devices, q_rows, 2 * LANES), up_block),
                pl.BlockSpec((rows, 2 * LANES), col),
                pl.BlockSpec(kvn.shape, whole),
                pl.BlockSpec(kvn_t.shape, whole),
                pl.BlockSpec((devices, kv_rows, 2 * LANES), lambda i, b: (0, q_rows // kv_rows, i + first_pair)),
                pl.BlockSpec(krope.shape, whole),
                pl.BlockSpec((rows, LANES), col),
                pl.BlockSpec((rows, LANES), col),
                pl.BlockSpec((8, rows), lambda i, b: (i + first_pair, 0)),
                pl.BlockSpec(cos.shape, whole),
                pl.BlockSpec(cos.shape, whole),
                pl.BlockSpec(cos.shape, whole),
                pl.BlockSpec((1, rows), whole),
            ] + [pl.BlockSpec(memory_space=pl.ANY)] * (len(prev[:2]) + len(deps)) + [pl.BlockSpec(v.shape, whole) for v in prev[2:]],
            out_specs=[
                pl.BlockSpec((devices, q_rows, 2 * LANES), up_block),
                pl.BlockSpec((devices, kv_rows, 2 * LANES), up_block),
                pl.BlockSpec((keys, rank), whole),
                pl.BlockSpec((keys, LANES), whole),
                pl.BlockSpec((rows, qlat_t.shape[0]), whole),
            ],
            scratch_shapes=[
                pltpu.VMEM((2, rows, LANES), jnp.bfloat16),
                pltpu.VMEM((2, LANES, rows), jnp.float32),
                pltpu.VMEM((8, rows), jnp.float32),
                pltpu.VMEM((rank, 2 * LANES), jnp.float32),
            ],
        ),
        out_shape=[
            jax.ShapeDtypeStruct((devices, q_rows, HEADS * LANES), jnp.bfloat16),
            jax.ShapeDtypeStruct((devices, kv_rows, HEADS * LANES), jnp.bfloat16),
            jax.ShapeDtypeStruct((keys, rank), jnp.float32),
            jax.ShapeDtypeStruct((keys, LANES), jnp.float32),
            jax.ShapeDtypeStruct((rows, qlat_t.shape[0]), jnp.float32),
        ],
        compiler_params=pltpu.CompilerParams(vmem_limit_bytes=48 << 20),
        cost_estimate=LIGHT,
        input_output_aliases={15 + i: i for i in range(len(prev[:2]))},
        name="attend_backward",
    )(bounds, qlat_t, up, q, kvn, kvn_t, up, krope, grad_out, out, lse, cos, sin_r, sin_l, start, *prev[:2], *deps, *prev[2:])


def hidden_kernel(*refs, count):
    normed, grads, (gate_w, up_w, down_w) = refs[:count], refs[count : 2 * count], refs[2 * count : 2 * count + 3]
    active, grad_gate, grad_up = refs[-3:]
    height = normed[0].shape[0]
    for i in range(count):
        rows = slice(i * height, (i + 1) * height)
        x = normed[i][...]
        gate = dot(x, gate_w[...], 1, 0)
        upper = dot(x, up_w[...], 1, 0)
        grad = dot(grads[i][...], down_w[...], 1, 1)
        sigmoid = jax.nn.sigmoid(gate)
        silu = gate * sigmoid
        active[rows, :] = (silu * upper).astype(jnp.bfloat16)
        grad_gate[rows, :] = (grad * upper * sigmoid * (1.0 + gate * (1.0 - sigmoid))).astype(jnp.bfloat16)
        grad_up[rows, :] = (grad * silu).astype(jnp.bfloat16)


def hidden_units(first_row, all_rows, prev, normed, grads, gate_w, up_w, down_w):
    count = len(normed)
    height, width = normed[0].shape
    rows, hidden = count * height, gate_w.shape[1]
    tile = 2 * LANES
    whole = lambda j: (0, 0)
    at = first_row // rows
    return pl.pallas_call(
        functools.partial(hidden_kernel, count=count),
        grid=(pl.cdiv(hidden, tile),),
        in_specs=[pl.BlockSpec((height, width), whole)] * (2 * count)
        + [pl.BlockSpec((width, tile), lambda j: (0, j))] * 2
        + [pl.BlockSpec((tile, width), lambda j: (j, 0))]
        + [pl.BlockSpec(memory_space=pl.ANY)] * len(prev),
        out_specs=[pl.BlockSpec((rows, tile), lambda j: (at, j))] * 3,
        out_shape=[jax.ShapeDtypeStruct((all_rows, hidden), jnp.bfloat16)] * 3,
        input_output_aliases={2 * count + 3 + i: i for i in range(len(prev))},
        compiler_params=pltpu.CompilerParams(vmem_limit_bytes=48 << 20),
        cost_estimate=pl.CostEstimate(
            flops=6 * rows * width * hidden, bytes_accessed=6 * width * hidden + 8 * rows * width, transcendentals=0
        ),
        name="hidden_units",
    )(*normed, *grads, gate_w, up_w, down_w, *prev)


def back_kernel(*refs, terms, contract):
    left, right, outs = refs[:terms], refs[terms : 2 * terms], refs[2 * terms :]
    height = outs[0].shape[0]
    for i, out in enumerate(outs):
        rows = slice(i * height, (i + 1) * height)
        total = dot(left[0][rows, :], right[0][...], 1, contract)
        for a, b in zip(left[1:], right[1:]):
            total = total + dot(a[rows, :], b[...], 1, contract)
        out[...] = total.astype(jnp.bfloat16)


def to_tokens(first_row, height, count, left, right, contract):
    hidden = left[0].shape[1]
    width = right[0].shape[1 - contract]
    rows = height * count
    tile = 2 * LANES
    at = first_row // rows
    if contract:
        right_spec = pl.BlockSpec((tile, hidden), lambda j: (j, 0))
    else:
        right_spec = pl.BlockSpec((hidden, tile), lambda j: (0, j))
    return pl.pallas_call(
        functools.partial(back_kernel, terms=len(left), contract=contract),
        grid=(width // tile,),
        in_specs=[pl.BlockSpec((rows, hidden), lambda j: (at, 0))] * len(left) + [right_spec] * len(left),
        out_specs=[pl.BlockSpec((height, tile), lambda j: (0, j))] * count,
        out_shape=[jax.ShapeDtypeStruct((height, width), jnp.bfloat16)] * count,
        compiler_params=pltpu.CompilerParams(vmem_limit_bytes=48 << 20),
        cost_estimate=LIGHT,
        name="to_tokens",
    )(*left, *right)


def blank(shape):
    return pl.pallas_call(
        lambda out: None,
        out_specs=pl.BlockSpec(memory_space=pl.ANY),
        out_shape=jax.ShapeDtypeStruct(shape, jnp.bfloat16),
        cost_estimate=LIGHT,
        name="blank",
    )()


D = 2560
FF = 6400
CONTS = 4
variance_eps = 1e-05
depth_scale = 1.4 / math.sqrt(62.0)
BF16 = jnp.bfloat16
F32 = jnp.float32


def rms_forward(values, gain_vector):
    inverse = lax.rsqrt(jnp.mean(values * values, axis=-1, keepdims=True) + variance_eps)
    return (values * inverse * gain_vector, inverse)


def rms_backward(values, inverse, gain_vector, upstream):
    scaled = upstream * gain_vector
    inner_mean = jnp.mean(scaled * values, axis=-1, keepdims=True)
    grad_values = inverse * scaled - values * inverse * inverse * inverse * inner_mean
    grad_gain = jnp.sum(upstream * values * inverse, axis=0)
    return (grad_values, grad_gain)


def segment_starts(lengths, index):
    own = jnp.zeros_like(index)
    begin = jnp.int32(PROMPT)
    for c in range(CONTS):
        own = jnp.where(index >= begin, begin, own)
        begin = begin + lengths[c]
    return own


def rope_tables(position):
    frequency = jnp.exp(jnp.arange(ROPE // 2, dtype=F32) * (-2.0 * math.log(10000.0) / ROPE))
    angles = position.astype(F32)[:, None] * frequency[None, :]
    cosine, sine = jnp.cos(angles), jnp.sin(angles)
    rows = position.shape[0]
    zeros = lambda n: jnp.zeros((rows, n), F32)
    return (
        jnp.concatenate([jnp.ones((rows, NOPE), F32), cosine, cosine, zeros(32)], axis=1),
        jnp.concatenate([zeros(80), sine, zeros(32)], axis=1),
        jnp.concatenate([zeros(64), -sine, zeros(48)], axis=1),
        cosine,
        sine,
    )


def rotate(values, cosine, sine):
    first, second = values[:, : ROPE // 2], values[:, ROPE // 2 :]
    return jnp.concatenate([first * cosine - second * sine, second * cosine + first * sine], axis=1)


def swap(tensor, bit, n):
    return lax.ppermute(tensor, "fsdp", [(i, i ^ bit) for i in range(n)])


def bit_orders(n):
    bits = []
    bit = 2
    while bit < n:
        bits.append(bit)
        bit *= 2
    return [bits, bits[::-1]]


def arrivals(n):
    orders = bit_orders(n)
    steps = [[(0, part) for part in range(2)]]
    for at in range(len(orders[0])):
        steps.append([
            (r | order[at], part)
            for part, order in enumerate(orders)
            for r in range(0, n, 2)
            if not r & ~sum(order[:at])
        ])
    return steps


BACK_PARTS = ((0, 12), (12, 4), (16, HEADS // 2 - 16))
ATTEND_PARTS = ((0, 4), (4, 7), (11, 7), (18, HEADS // 2 - 18))


def own_blocks(tensor):
    half = tensor.shape[0] // 2
    return {(0, part): tensor[part * half : (part + 1) * half] for part in range(2)}


def gather_step(blocks, n, at):
    return {
        (r | order[at], p): swap(block, order[at], n)
        for part, order in enumerate(bit_orders(n))
        for (r, p), block in blocks.items()
        if p == part
    }


def scatter_step(blocks, n, at, hold=None):
    arrived = {}
    for part, order in enumerate(bit_orders(n)):
        bit = order[at]
        for r, p in blocks:
            if p == part and not r & bit:
                arrived[r, p] = swap(blocks[r | bit, p].astype(BF16), bit, n)
    if hold is not None:
        hold, arrived = tie(hold, arrived)
    return {key: blocks[key].astype(F32) + block.astype(F32) for key, block in arrived.items()}, hold


def chip_scatter(blocks, n):
    for at in range(len(bit_orders(n)[0]))[::-1]:
        blocks, _ = scatter_step(blocks, n, at)
    return jnp.concatenate([blocks[0, part] for part in range(2)])


def tie(*trees):
    return lax.optimization_barrier(trees)


def ring(shift, count):
    return [(i, (i + shift) % count) for i in range(count)]


def seq_gather(share, layer, layers):
    whole = jnp.zeros((layers, *share.shape), share.dtype)
    for shift in range(layers):
        block = lax.ppermute(share, "seq", ring(shift, layers)) if shift else share
        whole = lax.dynamic_update_index_in_dim(whole, block, (layer - shift) % layers, 0)
    return whole.reshape(-1, *share.shape[1:])


def seq_scatter(whole, layer, layers):
    shares = whole.reshape(layers, -1, *whole.shape[1:])
    total = pick(shares, layer).astype(F32)
    for shift in range(1, layers):
        total = total + lax.ppermute(pick(shares, (layer + shift) % layers), "seq", ring(shift, layers)).astype(F32)
    return total


def pick(tensor, at, axis=0):
    return lax.dynamic_index_in_dim(tensor, at, axis, keepdims=False)


def core_scatter(split, core, n, axis=0):
    arrived = swap(pick(split, 1 - core, axis).astype(BF16), 1, n)
    return pick(split, core, axis).astype(F32) + arrived.astype(F32)


def core_shares(part, n):
    return jnp.swapaxes(part.astype(BF16).reshape(n // 2, 2, part.shape[0] // n, part.shape[1]), 0, 1)


def chip_blocks(mine, chip, n):
    half = mine.shape[1] // 2
    blocks = {}
    for r in range(0, n, 2):
        own = pick(mine, chip ^ (r // 2))
        for p in range(2):
            blocks[r, p] = own[p * half : (p + 1) * half]
    return blocks


def fsdp_scatter(part, core, chip, n):
    return chip_scatter(chip_blocks(core_scatter(core_shares(part, n), core, n).astype(BF16), chip, n), n)


def body(
    n,
    block_input,
    cont_lengths,
    attn_gain,
    q_down,
    q_gain,
    q_up,
    kv_down,
    kv_gain,
    kv_up,
    out_proj,
    mlp_gain,
    gate_up,
    down_proj,
    out_cotangent,
):
    rows = block_input.shape[1]
    chips = n // 2
    ff_chip = FF // chips
    ff_sent = -(-ff_chip // LANES) * LANES
    ff_wide = ff_sent
    group_len = rows * lax.axis_size("seq")
    device = lax.axis_index("fsdp")
    core, chip = device % 2, device // 2
    layers = lax.axis_size("seq")
    layer = lax.axis_index("seq")
    rank_q, rank_kv = q_up.shape[0] * n, kv_up.shape[0] * n
    first_row = lax.axis_index("seq") * rows
    index = first_row + jnp.arange(rows, dtype=jnp.int32)
    own_start = segment_starts(cont_lengths[0], index)
    position = jnp.where(own_start > 0, PROMPT + index - own_start, index)
    cos, sin_r, sin_l, cosine, sine = rope_tables(position)
    fold = SCALE * LOG2E
    start_row = own_start[None, :]
    full_rows, mask_rows = 1024, 512
    full_blocks = jnp.minimum(first_row, PROMPT) // full_rows
    bounds = jnp.stack([
        full_blocks,
        jnp.where(first_row < PROMPT, full_blocks * (full_rows // mask_rows), own_start[0] // mask_rows),
        (first_row + rows + mask_rows - 1) // mask_rows,
        first_row,
    ]).astype(jnp.int32)

    gains = lax.all_gather(jnp.concatenate([attn_gain, mlp_gain, q_gain, kv_gain]), "fsdp", axis=0)
    widths = [v.shape[0] for v in (attn_gain, mlp_gain, q_gain, kv_gain)]
    gain_list = []
    at = 0
    for width in widths:
        gain_list.append(gains[:, at : at + width].reshape(-1).astype(F32))
        at += width
    attn_gain_all, mlp_gain_all, q_gain_all, kv_gain_all = gain_list

    down_all = lax.all_gather(jnp.concatenate([q_down, kv_down], axis=1), "fsdp", axis=0, tiled=True)
    q_up_wide = jnp.pad(q_up.reshape(-1, HEADS, NOPE + ROPE), ((0, 0), (0, 0), (0, ROPE))).reshape(-1, HEADS * LANES)
    q_rows = q_up.shape[0]
    up_all = lax.all_gather(jnp.concatenate([q_up_wide, kv_up], axis=0), "fsdp", axis=0)
    out_proj_all = lax.all_gather(out_proj, "fsdp", axis=0, tiled=True)

    steps = arrivals(n)
    fetch = (D // n) // layers
    half_down = swap(down_proj, 1, n)
    down_w = jnp.concatenate([
        jnp.where(core == 0, down_proj, half_down),
        jnp.where(core == 0, half_down, down_proj),
        jnp.zeros((ff_wide - ff_chip, D), BF16),
    ])
    own_fetch = lax.dynamic_slice_in_dim(gate_up, layer * fetch, fetch, 0)
    widen = lambda v: jnp.pad(v, ((0, 0), (0, ff_sent - ff_chip)))
    own_fetch = jnp.stack([
        jnp.stack([widen(own_fetch[:, at + c * ff_chip : at + (c + 1) * ff_chip]) for at in (0, FF)]) for c in range(chips)
    ])
    own_fetch = [pick(own_fetch, chip ^ (r // 2)) for r in range(0, n, 2)]
    tables = (cos * fold, sin_r * fold, sin_l * fold, cos, sin_r, sin_l)
    down_all, tables, down_w, own_fetch = tie(down_all, tables, down_w, own_fetch)

    token_rows = block_input[0].astype(F32)
    normed_float, attn_inverse = rms_forward(token_rows, attn_gain_all)
    normed = normed_float.astype(BF16)
    latent = jnp.dot(normed, down_all, preferred_element_type=F32)
    q_latent, kv_latent, rope_latent = jnp.split(latent, [rank_q, rank_q + rank_kv], axis=1)
    q_lat_float, q_inverse = rms_forward(q_latent, q_gain_all)
    q_lat_normed = q_lat_float.astype(BF16)
    kv_float, kv_inverse = rms_forward(kv_latent, kv_gain_all)
    key_rope = jnp.pad(rotate(rope_latent, cosine, sine), ((0, 0), (NOPE, LANES - NOPE - ROPE)))
    kv_own = jnp.concatenate([kv_float, key_rope], axis=1).astype(BF16)
    kv_all = seq_gather(kv_own, layer, layers)
    cotangent = out_cotangent[0].astype(F32)
    grad_low = (depth_scale * cotangent).astype(BF16)
    up_all, kv_all, own_fetch, grad_low = tie(up_all, kv_all, own_fetch, grad_low)
    kv_normed, key_rope_all = kv_all[:, :rank_kv], kv_all[:, rank_kv:]
    forward_args = (
        bounds, q_lat_normed, up_all, kv_normed, key_rope_all,
        *tables[:3], start_row, full_rows, mask_rows,
    )

    fetched_blocks = [swap(block, 2 * r, n) if r else block for r, block in enumerate(own_fetch)]
    outputs = attend_forward(ATTEND_PARTS[0], [], [], *forward_args)
    grad_blocks = own_blocks(grad_low)
    moved = gather_step(grad_blocks, n, 0)
    outputs, fetched_blocks = tie(outputs, fetched_blocks)
    fetched = blank((2, chips, fetch, ff_sent))
    for r, block in enumerate(fetched_blocks):
        fetched = lax.dynamic_update_slice(fetched, block[:, None], (0, chip ^ r, 0, 0))
    passed = [(fetched, fetched)]
    for step in range(1, layers):
        link = (
            lax.ppermute(passed[-1][0], "seq", [(i, i + 1) for i in range(layers - 1)]),
            lax.ppermute(passed[-1][1], "seq", [(i + 1, i) for i in range(layers - 1)]),
        )
        if step < len(ATTEND_PARTS):
            outputs = attend_forward(ATTEND_PARTS[step], outputs, [], *forward_args)
            if step < layers - 1:
                outputs, link = tie(outputs, link)
            if step == 1:
                outputs, moved = tie(outputs, moved)
                grad_blocks = {**grad_blocks, **moved}
        passed.append(link)
    for part in ATTEND_PARTS[layers:]:
        outputs = attend_forward(part, outputs, [], *forward_args)
    attended, queries, log_total = outputs
    for at in range(1, len(steps) - 1):
        grad_blocks = {**grad_blocks, **gather_step(grad_blocks, n, at)}
    attn_branch = jnp.dot(attended, out_proj_all, preferred_element_type=F32)
    attn_branch, grad_blocks = tie(attn_branch, grad_blocks)
    middle = token_rows + depth_scale * attn_branch
    mlp_float, mlp_inverse = rms_forward(middle, mlp_gain_all)
    normed_blocks = own_blocks(mlp_float.astype(BF16))
    normed_blocks = {**normed_blocks, **gather_step(normed_blocks, n, 0)}
    normed_blocks, passed = tie(normed_blocks, passed)
    layer_blocks = [jnp.where(layer >= shift, passed[shift][0], passed[layers - shift][1]) for shift in range(1, layers)]
    for at in range(1, len(steps) - 1):
        normed_blocks = {**normed_blocks, **gather_step(normed_blocks, n, at)}
    hidden = [blank((chips, 2, layers, fetch, ff_wide)) for _ in range(2)]
    for shift in range(layers):
        block = layer_blocks[shift - 1] if shift else fetched
        source = (layer - shift) % layers
        for owner, arrived in ((core, block), (1 - core, swap(block, 1, n))):
            hidden = [
                lax.dynamic_update_slice(whole, v[:, None, None], (0, owner, source, 0, 0)) for whole, v in zip(hidden, arrived)
            ]
    gate_w, up_w = (v.reshape(D, ff_wide) for v in hidden)
    half = rows // 2
    first_rows = [sum(len(step) for step in steps[:i]) * half for i in range(len(steps))]
    kept = []
    for step, at in zip(steps, first_rows):
        kept = hidden_units(
            at, n * half, kept, [normed_blocks[key] for key in step], [grad_blocks[key] for key in step], gate_w, up_w, down_w
        )
    active, grad_gate, grad_up = kept
    all_normed = jnp.concatenate([normed_blocks[key] for step in steps for key in step])
    all_grad = jnp.concatenate([grad_blocks[key] for step in steps for key in step])

    back = lambda i, hidden: dict(zip(steps[i], to_tokens(first_rows[i], half, len(steps[i]), hidden, [gate_w, up_w], 1)))
    last_blocks = back(-1, [grad_gate, grad_up])
    last_blocks, active_late, earlier = tie(last_blocks, active, [grad_gate, grad_up])
    down_whole = dot(active_late, all_grad, 0, 0).astype(BF16)
    last_blocks, earlier = tie(last_blocks, [grad_gate, grad_up])
    half_ff = ff_chip // 2
    half_of = lambda at: lax.dynamic_slice_in_dim(down_whole, at * half_ff, half_ff, 0)
    down_part = (half_of(core).astype(F32) + swap(half_of(1 - core), 1, n).astype(F32)).astype(BF16)
    early_blocks = {}
    for i in range(len(steps) - 1)[::-1]:
        early_blocks.update(back(i, earlier))
    blocks, _ = scatter_step({**last_blocks, **early_blocks}, n, len(steps) - 2)
    blocks, all_normed, down_part = tie(blocks, all_normed, down_part)
    down_share = lax.psum_scatter(down_part, "seq", scatter_dimension=0, tiled=True)
    hidden_parts, hidden_shares, crossing = [], [], []
    for grads in (grad_gate, grad_up):
        whole = dot(all_normed, grads, 0, 0).astype(BF16).reshape(chips, 2, layers, fetch, ff_wide)
        crossing.append((pick(whole, core, 1), swap(pick(whole, 1 - core, 1), 1, n)))
    for at in range(len(steps) - 2)[::-1]:
        blocks, _ = scatter_step(blocks, n, at)

    def over_layers(crossed):
        part = (crossed[0].astype(F32) + crossed[1].astype(F32)).astype(BF16).transpose(1, 0, 2, 3)
        hidden_parts.append(part)
        hidden_shares.append(lax.psum_scatter(part, "seq", scatter_dimension=0, tiled=True)[0])

    blocks, crossing[0], down_share = tie(blocks, crossing[0], down_share)
    over_layers(crossing[0])
    grad_mlp_normed = jnp.concatenate([blocks[0, part] for part in range(2)]).astype(F32)
    grad_mid_norm, mlp_gain_part = rms_backward(middle, mlp_inverse, mlp_gain_all, grad_mlp_normed)
    grad_middle = cotangent + grad_mid_norm
    grad_attn = (depth_scale * grad_middle).astype(BF16)
    out_proj_part = dot(attended, grad_attn, 0, 0).astype(BF16)
    grad_attended = dot(grad_attn, out_proj_all, 1, 1).astype(BF16)
    grad_attended, crossing[1] = tie(grad_attended, crossing[1])
    over_layers(crossing[1])
    backward_args = (
        bounds, q_lat_normed.T, up_all, queries, kv_normed, kv_normed.T, key_rope_all, grad_attended, attended, log_total,
        *tables[3:], start_row, full_rows, mask_rows,
    )
    out_shares = core_shares(out_proj_part, n)
    out_arrived = swap(pick(out_shares, 1 - core), 1, n)
    first = attend_backward(BACK_PARTS[0], [], [*hidden_parts, out_proj_part], *backward_args)
    down_low = lax.all_gather(down_share, "seq", axis=0, tiled=True)
    first, hidden_shares, down_share, out_arrived = tie(first, hidden_shares, down_share, out_arrived)
    out_mine = (pick(out_shares, core).astype(F32) + out_arrived.astype(F32)).astype(BF16)
    first, out_mine = tie(first, out_mine)
    hidden_share = jnp.stack(hidden_shares)
    hidden_blocks = [pick(hidden_share, chip ^ (r // 2), 1) for r in range(0, n, 2)]
    hidden_blocks = [swap(block, 2 * r, n) if r else block for r, block in enumerate(hidden_blocks)]
    second = attend_backward(BACK_PARTS[1], first, [down_share], *backward_args)
    second, hidden_blocks = tie(second, hidden_blocks)
    hidden_blocks = jnp.stack(hidden_blocks)
    hidden_blocks = [pick(hidden_blocks, chip ^ c)[..., :ff_chip] for c in range(chips)]
    placed = [jnp.concatenate([block[at] for block in hidden_blocks], axis=1) for at in range(2)]
    gate_low, up_low = (lax.all_gather(v, "seq", axis=0, tiled=True) for v in placed)
    third = attend_backward(BACK_PARTS[2], second, placed, *backward_args)
    out_blocks, third = scatter_step(chip_blocks(out_mine, chip, n), n, len(steps) - 2, third)
    for at in range(len(steps) - 2)[::-1]:
        out_blocks, _ = scatter_step(out_blocks, n, at)
    out_share = jnp.concatenate([out_blocks[0, part] for part in range(2)]).astype(BF16)
    q_up_part, kv_up_part, grad_kv_all, grad_rope_all, grad_q_lat = third
    grad_q_float, q_gain_part = rms_backward(q_latent, q_inverse, q_gain_all, grad_q_lat)
    grad_kv = seq_scatter(jnp.concatenate([grad_kv_all, grad_rope_all], axis=1).astype(BF16), layer, layers)
    grad_kv, gate_low, down_low = tie(grad_kv, gate_low, down_low)
    up_parts = jnp.concatenate([q_up_part, kv_up_part], axis=1).reshape(-1, HEADS * LANES)
    up_share = fsdp_scatter(up_parts, core, chip, n).astype(BF16)
    grad_kv_first, kv_gain_part = rms_backward(kv_latent, kv_inverse, kv_gain_all, grad_kv[:, :rank_kv])
    grad_rope = rotate(grad_kv[:, rank_kv + NOPE : rank_kv + NOPE + ROPE], cosine, -sine)
    grad_latent = jnp.concatenate([grad_q_float, grad_kv_first, grad_rope], axis=1).astype(BF16)
    down_all_part = dot(normed, grad_latent, 0, 0)
    grad_normed = dot(grad_latent, down_all, 1, 1)
    grad_in_norm, attn_gain_part = rms_backward(token_rows, attn_inverse, attn_gain_all, grad_normed)
    grad_input = (grad_middle + grad_in_norm).reshape(block_input.shape)

    gain_parts = [v.reshape(n, -1) for v in (attn_gain_part, mlp_gain_part, q_gain_part, kv_gain_part)]
    gain_rows = jnp.concatenate(gain_parts, axis=1)
    gain_rows = jnp.pad(gain_rows[:, None], ((0, 0), (0, 15), (0, latent.shape[1] - gain_rows.shape[1])))
    down_rows = D // n
    down_all_part = jnp.concatenate([down_all_part.reshape(n, down_rows, -1), gain_rows], axis=1)
    down_all_share = fsdp_scatter(down_all_part.reshape(-1, latent.shape[1]), core, chip, n).astype(BF16)
    up_share, out_share, down_all_share, up_low, active_last = tie(up_share, out_share, down_all_share, up_low, active)
    up_grad, out_proj_grad, down_all_grad = (v.astype(F32) for v in lax.psum((up_share, out_share, down_all_share), "seq"))
    branch = {}
    for step, at in zip(steps, first_rows):
        branch.update(zip(step, to_tokens(at, half, len(step), [active_last], [down_w], 0)))
    down_grad = down_low.astype(F32)
    gate_up_grad = jnp.concatenate([gate_low, up_low], axis=1).astype(F32)
    output = (middle + depth_scale * chip_scatter(branch, n)).astype(BF16).reshape(block_input.shape)
    gain_sum = down_all_grad[down_rows]
    down_all_grad = down_all_grad[:down_rows]
    q_up_grad = up_grad[:q_rows].reshape(-1, HEADS, LANES)[..., : NOPE + ROPE].reshape(-1, HEADS * (NOPE + ROPE))
    kv_up_grad = up_grad[q_rows:]
    ends = [sum(widths[: i + 1]) for i in range(4)]
    attn_gain_grad, mlp_gain_grad, q_gain_grad, kv_gain_grad = jnp.split(gain_sum[: ends[3]], ends[:3])
    return (
        output,
        grad_input,
        attn_gain_grad,
        down_all_grad[:, :rank_q],
        q_gain_grad,
        q_up_grad,
        down_all_grad[:, rank_q:],
        kv_gain_grad,
        kv_up_grad,
        out_proj_grad,
        mlp_gain_grad,
        gate_up_grad,
        down_grad,
    )


def solution(mesh):
    tokens, matrix, vector = P("fsdp", "seq", None), P("fsdp", None), P("fsdp")
    return jax.shard_map(
        functools.partial(body, mesh.shape["fsdp"]),
        mesh=mesh,
        in_specs=(tokens, matrix, vector, matrix, vector, matrix, matrix, vector, matrix, matrix, vector, matrix, matrix, tokens),
        out_specs=(tokens, tokens, vector, matrix, vector, matrix, matrix, vector, matrix, matrix, vector, matrix, matrix),
        check_vma=False,
    )
```

```python
import functools, math
import jax
import jax.numpy as jnp
from jax import lax
from jax.experimental import pallas as pl
from jax.experimental.pallas import tpu as pltpu
from jax.sharding import PartitionSpec as P

HEADS = 40
NOPE = 64
ROPE = 32
PROMPT = 1024
LANES = 128
NEG = -1e30
SCALE = (NOPE + ROPE) ** -0.5
LOG2E = math.log2(math.e)
LN2 = math.log(2.0)


LIGHT = pl.CostEstimate(flops=1 << 20, bytes_accessed=1 << 16, transcendentals=0)


def dot(a, b, ca, cb):
    return lax.dot_general(a, b, (((ca,), (cb,)), ((), ())), preferred_element_type=jnp.float32)


def flat(ref):
    return ref[...].reshape(-1, ref.shape[-1])


def fwd_kernel(bounds, qlat, qup_ref, kvn, kvup_ref, krope, cos, sin_r, sin_l, start, *rest, full_rows, mask_rows):
    out, q_out, lse_out, m_scr, acc_scr = rest[-5:]
    rows = qlat.shape[0]
    lane = lax.broadcasted_iota(jnp.int32, (1, LANES), 1)
    low_half = lane < NOPE
    raw = dot(qlat[...], flat(qup_ref), 1, 0)
    kvup = flat(kvup_ref)
    for h in range(2):
        u = raw[:, h * LANES:(h + 1) * LANES]
        turned = u * cos[...] + pltpu.roll(u, 16, 1) * sin_r[...] + pltpu.roll(u, LANES - 16, 1) * sin_l[...]
        q_out[:, h * LANES:(h + 1) * LANES] = turned.astype(jnp.bfloat16)
    m_scr[...] = jnp.full_like(m_scr, NEG)
    acc_scr[...] = jnp.zeros_like(acc_scr)

    def block(first, size, masked):
        span = pl.ds(first, size)
        kv = dot(kvn[span, :], kvup, 1, 0).astype(jnp.bfloat16)
        rope_rows = krope[span, :]
        if masked:
            key_index = first + lax.broadcasted_iota(jnp.int32, (size, rows), 0)
            own = bounds[3] + lax.broadcasted_iota(jnp.int32, (size, rows), 1)
            allowed = (key_index <= own) & ((key_index >= start[...]) | (key_index < PROMPT))
        scores, vals = [], []
        for h in range(2):
            kv_h = kv[:, h * LANES:(h + 1) * LANES]
            key = jnp.where(low_half, kv_h, rope_rows)
            vals.append(jnp.where(low_half, jnp.ones_like(kv_h), kv_h))
            s = dot(key, q_out[:, h * LANES:(h + 1) * LANES], 1, 1)
            scores.append(jnp.where(allowed, s, NEG) if masked else s)
        for h in range(2):
            m_old = m_scr[h:h + 1, :]
            m_new = jnp.maximum(m_old, jnp.max(scores[h], axis=0, keepdims=True))
            m_scr[h:h + 1, :] = m_new
            p = jnp.exp2(scores[h] - m_new).astype(jnp.bfloat16)
            acc_scr[h] = acc_scr[h] * jnp.exp2(m_old - m_new) + dot(vals[h], p, 0, 0)

    lax.fori_loop(0, bounds[0], lambda i, c: (block(pl.multiple_of(i * full_rows, full_rows), full_rows, False), c)[1], 0)
    lax.fori_loop(bounds[1], bounds[2], lambda i, c: (block(pl.multiple_of(i * mask_rows, mask_rows), mask_rows, True), c)[1], 0)
    parts = []
    for h in range(2):
        total = acc_scr[h, 0:1, :]
        parts.append(acc_scr[h, NOPE:, :] / total)
        lse_out[h:h + 1, :] = m_scr[h:h + 1, :] + jnp.log2(total)
    out[...] = jnp.concatenate(parts, axis=0).T.astype(jnp.bfloat16)


def attend_forward(part, prev, deps, bounds, qlat, up, kvn, krope, cos, sin_r, sin_l, start, full_rows, mask_rows):
    rows, rank = qlat.shape
    q_rows, kv_rows = rank // up.shape[0], kvn.shape[1] // up.shape[0]
    whole = lambda *_: (0, 0)
    first_pair, pairs = part
    col = lambda i, b: (0, i + first_pair)
    return pl.pallas_call(
        functools.partial(fwd_kernel, full_rows=full_rows, mask_rows=mask_rows),
        grid_spec=pltpu.PrefetchScalarGridSpec(
            num_scalar_prefetch=1,
            grid=(pairs,),
            in_specs=[
                pl.BlockSpec((rows, rank), whole),
                pl.BlockSpec((up.shape[0], q_rows, 2 * LANES), lambda i, b: (0, 0, i + first_pair)),
                pl.BlockSpec(kvn.shape, whole),
                pl.BlockSpec((up.shape[0], kv_rows, 2 * LANES), lambda i, b: (0, q_rows // kv_rows, i + first_pair)),
                pl.BlockSpec(krope.shape, whole),
                pl.BlockSpec(cos.shape, whole),
                pl.BlockSpec(cos.shape, whole),
                pl.BlockSpec(cos.shape, whole),
                pl.BlockSpec((1, rows), whole),
            ] + [pl.BlockSpec(memory_space=pl.ANY)] * (len(prev) + len(deps)),
            out_specs=[
                pl.BlockSpec((rows, LANES), col),
                pl.BlockSpec((rows, 2 * LANES), col),
                pl.BlockSpec((8, rows), lambda i, b: (i + first_pair, 0)),
            ],
            scratch_shapes=[pltpu.VMEM((8, rows), jnp.float32), pltpu.VMEM((2, LANES, rows), jnp.float32)],
        ),
        out_shape=[
            jax.ShapeDtypeStruct((rows, HEADS * NOPE), jnp.bfloat16),
            jax.ShapeDtypeStruct((rows, HEADS * LANES), jnp.bfloat16),
            jax.ShapeDtypeStruct((HEADS // 2 * 8, rows), jnp.float32),
        ],
        compiler_params=pltpu.CompilerParams(vmem_limit_bytes=48 << 20),
        cost_estimate=LIGHT,
        input_output_aliases={10 + i: i for i in range(len(prev))},
        name="attend_forward",
    )(bounds, qlat, up, kvn, up, krope, cos, sin_r, sin_l, start, *prev, *deps)


def bwd_kernel(bounds, qlat_t, qup_ref, q, kvn, kvn_t, kvup_ref, krope, grad_out, out, lse, cos, sin_r, sin_l, start, *rest, full_rows, mask_rows, resumes):
    dqup_out, dkvup_out, dkvn, drope, dqlat, go_scr, dq_scr, delta_scr, dkvup = rest[-9:]
    kvup = flat(kvup_ref)
    rows = q.shape[0]
    lane = lax.broadcasted_iota(jnp.int32, (1, LANES), 1)
    low_half = lane < NOPE

    @pl.when(pl.program_id(0) == 0)
    def _():
        dkvn[...] = rest[-12][...] if resumes else jnp.zeros_like(dkvn)
        drope[...] = rest[-11][...] if resumes else jnp.zeros_like(drope)
        dqlat[...] = rest[-10][...] if resumes else jnp.zeros_like(dqlat)

    go = grad_out[...].astype(jnp.float32)
    prod_t = (go * out[...].astype(jnp.float32)).T
    delta_scr[0:1, :] = jnp.sum(prod_t[:NOPE], axis=0, keepdims=True)
    delta_scr[1:2, :] = jnp.sum(prod_t[NOPE:], axis=0, keepdims=True)
    zero = jnp.zeros_like(go)
    go_scr[0] = jnp.where(low_half, zero, pltpu.roll(go, NOPE, 1)).astype(jnp.bfloat16)
    go_scr[1] = jnp.where(low_half, zero, go).astype(jnp.bfloat16)
    dq_scr[...] = jnp.zeros_like(dq_scr)
    dkvup[...] = jnp.zeros_like(dkvup)

    def block(first, size, masked):
        span = pl.ds(first, size)
        kv = dot(kvn[span, :], kvup, 1, 0).astype(jnp.bfloat16)
        rope_rows = krope[span, :]
        if masked:
            key_index = first + lax.broadcasted_iota(jnp.int32, (size, rows), 0)
            own = bounds[3] + lax.broadcasted_iota(jnp.int32, (size, rows), 1)
            allowed = (key_index <= own) & ((key_index >= start[...]) | (key_index < PROMPT))
        pieces = []
        rope_sum = None
        for h in range(2):
            kv_h = kv[:, h * LANES:(h + 1) * LANES]
            q_h = q[:, h * LANES:(h + 1) * LANES]
            key = jnp.where(low_half, kv_h, rope_rows)
            p = jnp.exp2(dot(key, q_h, 1, 1) - lse[h:h + 1, :])
            if masked:
                p = jnp.where(allowed, p, 0.0)
            ds = (p * (dot(kv_h, go_scr[h], 1, 1) - delta_scr[h:h + 1, :])).astype(jnp.bfloat16)
            dk = dot(ds, q_h, 1, 0) * LN2
            dv = dot(p.astype(jnp.bfloat16), go_scr[h], 1, 0)
            dq_scr[h] += dot(key, ds, 0, 0)
            pieces.append(jnp.where(low_half, dk, dv).astype(jnp.bfloat16))
            rope_sum = dk if rope_sum is None else rope_sum + dk
        dkv = jnp.concatenate(pieces, axis=1)
        drope[span, :] += rope_sum
        dkvn[span, :] += dot(dkv, kvup, 1, 1)
        dkvup[...] += dot(kvn_t[:, span], dkv, 1, 0)

    lax.fori_loop(0, bounds[0], lambda i, c: (block(pl.multiple_of(i * full_rows, full_rows), full_rows, False), c)[1], 0)
    lax.fori_loop(bounds[1], bounds[2], lambda i, c: (block(pl.multiple_of(i * mask_rows, mask_rows), mask_rows, True), c)[1], 0)
    turned = []
    for h in range(2):
        u = dq_scr[h].T * SCALE
        turned.append(u * cos[...] - pltpu.roll(u, 16, 1) * sin_r[...] - pltpu.roll(u, LANES - 16, 1) * sin_l[...])
    dq = jnp.concatenate(turned, axis=1).astype(jnp.bfloat16)
    dqlat[...] += dot(dq, flat(qup_ref), 1, 1)
    dqup_out[...] = dot(qlat_t[...], dq, 1, 0).astype(jnp.bfloat16).reshape(dqup_out.shape)
    dkvup_out[...] = dkvup[...].astype(jnp.bfloat16).reshape(dkvup_out.shape)


def attend_backward(part, prev, deps, bounds, qlat_t, up, q, kvn, kvn_t, krope, grad_out, out, lse, cos, sin_r, sin_l, start, full_rows, mask_rows):
    rows = q.shape[0]
    keys, rank = kvn.shape
    devices = up.shape[0]
    q_rows, kv_rows = qlat_t.shape[0] // devices, rank // devices
    up_block = lambda i, b: (0, 0, i + first_pair)
    whole = lambda *_: (0, 0)
    first_pair, pairs = part
    col = lambda i, b: (0, i + first_pair)
    return pl.pallas_call(
        functools.partial(bwd_kernel, full_rows=full_rows, mask_rows=mask_rows, resumes=bool(prev)),
        grid_spec=pltpu.PrefetchScalarGridSpec(
            num_scalar_prefetch=1,
            grid=(pairs,),
            in_specs=[
                pl.BlockSpec(qlat_t.shape, whole),
                pl.BlockSpec((devices, q_rows, 2 * LANES), up_block),
                pl.BlockSpec((rows, 2 * LANES), col),
                pl.BlockSpec(kvn.shape, whole),
                pl.BlockSpec(kvn_t.shape, whole),
                pl.BlockSpec((devices, kv_rows, 2 * LANES), lambda i, b: (0, q_rows // kv_rows, i + first_pair)),
                pl.BlockSpec(krope.shape, whole),
                pl.BlockSpec((rows, LANES), col),
                pl.BlockSpec((rows, LANES), col),
                pl.BlockSpec((8, rows), lambda i, b: (i + first_pair, 0)),
                pl.BlockSpec(cos.shape, whole),
                pl.BlockSpec(cos.shape, whole),
                pl.BlockSpec(cos.shape, whole),
                pl.BlockSpec((1, rows), whole),
            ] + [pl.BlockSpec(memory_space=pl.ANY)] * (len(prev[:2]) + len(deps)) + [pl.BlockSpec(v.shape, whole) for v in prev[2:]],
            out_specs=[
                pl.BlockSpec((devices, q_rows, 2 * LANES), up_block),
                pl.BlockSpec((devices, kv_rows, 2 * LANES), up_block),
                pl.BlockSpec((keys, rank), whole),
                pl.BlockSpec((keys, LANES), whole),
                pl.BlockSpec((rows, qlat_t.shape[0]), whole),
            ],
            scratch_shapes=[
                pltpu.VMEM((2, rows, LANES), jnp.bfloat16),
                pltpu.VMEM((2, LANES, rows), jnp.float32),
                pltpu.VMEM((8, rows), jnp.float32),
                pltpu.VMEM((rank, 2 * LANES), jnp.float32),
            ],
        ),
        out_shape=[
            jax.ShapeDtypeStruct((devices, q_rows, HEADS * LANES), jnp.bfloat16),
            jax.ShapeDtypeStruct((devices, kv_rows, HEADS * LANES), jnp.bfloat16),
            jax.ShapeDtypeStruct((keys, rank), jnp.float32),
            jax.ShapeDtypeStruct((keys, LANES), jnp.float32),
            jax.ShapeDtypeStruct((rows, qlat_t.shape[0]), jnp.float32),
        ],
        compiler_params=pltpu.CompilerParams(vmem_limit_bytes=48 << 20),
        cost_estimate=LIGHT,
        input_output_aliases={15 + i: i for i in range(len(prev[:2]))},
        name="attend_backward",
    )(bounds, qlat_t, up, q, kvn, kvn_t, up, krope, grad_out, out, lse, cos, sin_r, sin_l, start, *prev[:2], *deps, *prev[2:])


def hidden_kernel(*refs, count):
    normed, grads, (gate_w, up_w, down_w) = refs[:count], refs[count : 2 * count], refs[2 * count : 2 * count + 3]
    active, grad_gate, grad_up = refs[-3:]
    height = normed[0].shape[0]
    for i in range(count):
        rows = slice(i * height, (i + 1) * height)
        x = normed[i][...]
        gate = dot(x, gate_w[...], 1, 0)
        upper = dot(x, up_w[...], 1, 0)
        grad = dot(grads[i][...], down_w[...], 1, 1)
        sigmoid = jax.nn.sigmoid(gate)
        silu = gate * sigmoid
        active[rows, :] = (silu * upper).astype(jnp.bfloat16)
        grad_gate[rows, :] = (grad * upper * sigmoid * (1.0 + gate * (1.0 - sigmoid))).astype(jnp.bfloat16)
        grad_up[rows, :] = (grad * silu).astype(jnp.bfloat16)


def hidden_units(first_row, all_rows, prev, normed, grads, gate_w, up_w, down_w):
    count = len(normed)
    height, width = normed[0].shape
    rows, hidden = count * height, gate_w.shape[1]
    tile = 2 * LANES
    whole = lambda j: (0, 0)
    at = first_row // rows
    return pl.pallas_call(
        functools.partial(hidden_kernel, count=count),
        grid=(pl.cdiv(hidden, tile),),
        in_specs=[pl.BlockSpec((height, width), whole)] * (2 * count)
        + [pl.BlockSpec((width, tile), lambda j: (0, j))] * 2
        + [pl.BlockSpec((tile, width), lambda j: (j, 0))]
        + [pl.BlockSpec(memory_space=pl.ANY)] * len(prev),
        out_specs=[pl.BlockSpec((rows, tile), lambda j: (at, j))] * 3,
        out_shape=[jax.ShapeDtypeStruct((all_rows, hidden), jnp.bfloat16)] * 3,
        input_output_aliases={2 * count + 3 + i: i for i in range(len(prev))},
        compiler_params=pltpu.CompilerParams(vmem_limit_bytes=48 << 20),
        cost_estimate=pl.CostEstimate(
            flops=6 * rows * width * hidden, bytes_accessed=6 * width * hidden + 8 * rows * width, transcendentals=0
        ),
        name="hidden_units",
    )(*normed, *grads, gate_w, up_w, down_w, *prev)


def back_kernel(*refs, terms, contract):
    left, right, outs = refs[:terms], refs[terms : 2 * terms], refs[2 * terms :]
    height = outs[0].shape[0]
    for i, out in enumerate(outs):
        rows = slice(i * height, (i + 1) * height)
        total = dot(left[0][rows, :], right[0][...], 1, contract)
        for a, b in zip(left[1:], right[1:]):
            total = total + dot(a[rows, :], b[...], 1, contract)
        out[...] = total.astype(jnp.bfloat16)


def to_tokens(first_row, height, count, left, right, contract):
    hidden = left[0].shape[1]
    width = right[0].shape[1 - contract]
    rows = height * count
    tile = 2 * LANES
    at = first_row // rows
    if contract:
        right_spec = pl.BlockSpec((tile, hidden), lambda j: (j, 0))
    else:
        right_spec = pl.BlockSpec((hidden, tile), lambda j: (0, j))
    return pl.pallas_call(
        functools.partial(back_kernel, terms=len(left), contract=contract),
        grid=(width // tile,),
        in_specs=[pl.BlockSpec((rows, hidden), lambda j: (at, 0))] * len(left) + [right_spec] * len(left),
        out_specs=[pl.BlockSpec((height, tile), lambda j: (0, j))] * count,
        out_shape=[jax.ShapeDtypeStruct((height, width), jnp.bfloat16)] * count,
        compiler_params=pltpu.CompilerParams(vmem_limit_bytes=48 << 20),
        cost_estimate=LIGHT,
        name="to_tokens",
    )(*left, *right)


def blank(shape):
    return pl.pallas_call(
        lambda out: None,
        out_specs=pl.BlockSpec(memory_space=pl.ANY),
        out_shape=jax.ShapeDtypeStruct(shape, jnp.bfloat16),
        cost_estimate=LIGHT,
        name="blank",
    )()


D = 2560
FF = 6400
CONTS = 4
variance_eps = 1e-05
depth_scale = 1.4 / math.sqrt(62.0)
BF16 = jnp.bfloat16
F32 = jnp.float32


def rms_forward(values, gain_vector):
    inverse = lax.rsqrt(jnp.mean(values * values, axis=-1, keepdims=True) + variance_eps)
    return (values * inverse * gain_vector, inverse)


def rms_backward(values, inverse, gain_vector, upstream):
    scaled = upstream * gain_vector
    inner_mean = jnp.mean(scaled * values, axis=-1, keepdims=True)
    grad_values = inverse * scaled - values * inverse * inverse * inverse * inner_mean
    grad_gain = jnp.sum(upstream * values * inverse, axis=0)
    return (grad_values, grad_gain)


def segment_starts(lengths, index):
    own = jnp.zeros_like(index)
    begin = jnp.int32(PROMPT)
    for c in range(CONTS):
        own = jnp.where(index >= begin, begin, own)
        begin = begin + lengths[c]
    return own


def rope_tables(position):
    frequency = jnp.exp(jnp.arange(ROPE // 2, dtype=F32) * (-2.0 * math.log(10000.0) / ROPE))
    angles = position.astype(F32)[:, None] * frequency[None, :]
    cosine, sine = jnp.cos(angles), jnp.sin(angles)
    rows = position.shape[0]
    zeros = lambda n: jnp.zeros((rows, n), F32)
    return (
        jnp.concatenate([jnp.ones((rows, NOPE), F32), cosine, cosine, zeros(32)], axis=1),
        jnp.concatenate([zeros(80), sine, zeros(32)], axis=1),
        jnp.concatenate([zeros(64), -sine, zeros(48)], axis=1),
        cosine,
        sine,
    )


def rotate(values, cosine, sine):
    first, second = values[:, : ROPE // 2], values[:, ROPE // 2 :]
    return jnp.concatenate([first * cosine - second * sine, second * cosine + first * sine], axis=1)


def swap(tensor, bit, n):
    return lax.ppermute(tensor, "fsdp", [(i, i ^ bit) for i in range(n)])


def bit_orders(n):
    bits = []
    bit = 2
    while bit < n:
        bits.append(bit)
        bit *= 2
    return [bits, bits[::-1]]


def arrivals(n):
    orders = bit_orders(n)
    steps = [[(0, part) for part in range(2)]]
    for at in range(len(orders[0])):
        steps.append([
            (r | order[at], part)
            for part, order in enumerate(orders)
            for r in range(0, n, 2)
            if not r & ~sum(order[:at])
        ])
    return steps


BACK_PARTS = ((0, 12), (12, 4), (16, HEADS // 2 - 16))
ATTEND_PARTS = ((0, 4), (4, 7), (11, 5), (16, HEADS // 2 - 16))


def own_blocks(tensor):
    half = tensor.shape[0] // 2
    return {(0, part): tensor[part * half : (part + 1) * half] for part in range(2)}


def gather_step(blocks, n, at):
    return {
        (r | order[at], p): swap(block, order[at], n)
        for part, order in enumerate(bit_orders(n))
        for (r, p), block in blocks.items()
        if p == part
    }


def scatter_step(blocks, n, at, hold=None):
    arrived = {}
    for part, order in enumerate(bit_orders(n)):
        bit = order[at]
        for r, p in blocks:
            if p == part and not r & bit:
                arrived[r, p] = swap(blocks[r | bit, p].astype(BF16), bit, n)
    if hold is not None:
        hold, arrived = tie(hold, arrived)
    return {key: blocks[key].astype(F32) + block.astype(F32) for key, block in arrived.items()}, hold


def chip_scatter(blocks, n):
    for at in range(len(bit_orders(n)[0]))[::-1]:
        blocks, _ = scatter_step(blocks, n, at)
    return jnp.concatenate([blocks[0, part] for part in range(2)])


def tie(*trees):
    return lax.optimization_barrier(trees)


def ring(shift, count):
    return [(i, (i + shift) % count) for i in range(count)]


def seq_gather(share, layer, layers):
    whole = jnp.zeros((layers, *share.shape), share.dtype)
    for shift in range(layers):
        block = lax.ppermute(share, "seq", ring(shift, layers)) if shift else share
        whole = lax.dynamic_update_index_in_dim(whole, block, (layer - shift) % layers, 0)
    return whole.reshape(-1, *share.shape[1:])


def seq_scatter(whole, layer, layers):
    shares = whole.reshape(layers, -1, *whole.shape[1:])
    total = pick(shares, layer).astype(F32)
    for shift in range(1, layers):
        total = total + lax.ppermute(pick(shares, (layer + shift) % layers), "seq", ring(shift, layers)).astype(F32)
    return total


def pick(tensor, at, axis=0):
    return lax.dynamic_index_in_dim(tensor, at, axis, keepdims=False)


def core_scatter(split, core, n, axis=0):
    arrived = swap(pick(split, 1 - core, axis).astype(BF16), 1, n)
    return pick(split, core, axis).astype(F32) + arrived.astype(F32)


def core_shares(part, n):
    return jnp.swapaxes(part.astype(BF16).reshape(n // 2, 2, part.shape[0] // n, part.shape[1]), 0, 1)


def chip_blocks(mine, chip, n):
    half = mine.shape[1] // 2
    blocks = {}
    for r in range(0, n, 2):
        own = pick(mine, chip ^ (r // 2))
        for p in range(2):
            blocks[r, p] = own[p * half : (p + 1) * half]
    return blocks


def fsdp_scatter(part, core, chip, n):
    return chip_scatter(chip_blocks(core_scatter(core_shares(part, n), core, n).astype(BF16), chip, n), n)


def body(
    n,
    block_input,
    cont_lengths,
    attn_gain,
    q_down,
    q_gain,
    q_up,
    kv_down,
    kv_gain,
    kv_up,
    out_proj,
    mlp_gain,
    gate_up,
    down_proj,
    out_cotangent,
):
    rows = block_input.shape[1]
    chips = n // 2
    ff_chip = FF // chips
    ff_sent = -(-ff_chip // LANES) * LANES
    ff_wide = ff_sent
    group_len = rows * lax.axis_size("seq")
    device = lax.axis_index("fsdp")
    core, chip = device % 2, device // 2
    layers = lax.axis_size("seq")
    layer = lax.axis_index("seq")
    rank_q, rank_kv = q_up.shape[0] * n, kv_up.shape[0] * n
    first_row = lax.axis_index("seq") * rows
    index = first_row + jnp.arange(rows, dtype=jnp.int32)
    own_start = segment_starts(cont_lengths[0], index)
    position = jnp.where(own_start > 0, PROMPT + index - own_start, index)
    cos, sin_r, sin_l, cosine, sine = rope_tables(position)
    fold = SCALE * LOG2E
    start_row = own_start[None, :]
    full_rows, mask_rows = 1024, 512
    full_blocks = jnp.minimum(first_row, PROMPT) // full_rows
    bounds = jnp.stack([
        full_blocks,
        jnp.where(first_row < PROMPT, full_blocks * (full_rows // mask_rows), own_start[0] // mask_rows),
        (first_row + rows + mask_rows - 1) // mask_rows,
        first_row,
    ]).astype(jnp.int32)

    gains = lax.all_gather(jnp.concatenate([attn_gain, mlp_gain, q_gain, kv_gain]), "fsdp", axis=0)
    widths = [v.shape[0] for v in (attn_gain, mlp_gain, q_gain, kv_gain)]
    gain_list = []
    at = 0
    for width in widths:
        gain_list.append(gains[:, at : at + width].reshape(-1).astype(F32))
        at += width
    attn_gain_all, mlp_gain_all, q_gain_all, kv_gain_all = gain_list

    down_all = lax.all_gather(jnp.concatenate([q_down, kv_down], axis=1), "fsdp", axis=0, tiled=True)
    q_up_wide = jnp.pad(q_up.reshape(-1, HEADS, NOPE + ROPE), ((0, 0), (0, 0), (0, ROPE))).reshape(-1, HEADS * LANES)
    q_rows = q_up.shape[0]
    up_all = lax.all_gather(jnp.concatenate([q_up_wide, kv_up], axis=0), "fsdp", axis=0)
    out_proj_all = lax.all_gather(out_proj, "fsdp", axis=0, tiled=True)

    steps = arrivals(n)
    fetch = (D // n) // layers
    half_down = swap(down_proj, 1, n)
    down_w = jnp.concatenate([
        jnp.where(core == 0, down_proj, half_down),
        jnp.where(core == 0, half_down, down_proj),
        jnp.zeros((ff_wide - ff_chip, D), BF16),
    ])
    own_fetch = lax.dynamic_slice_in_dim(gate_up, layer * fetch, fetch, 0)
    widen = lambda v: jnp.pad(v, ((0, 0), (0, ff_sent - ff_chip)))
    own_fetch = jnp.stack([
        jnp.stack([widen(own_fetch[:, at + c * ff_chip : at + (c + 1) * ff_chip]) for at in (0, FF)]) for c in range(chips)
    ])
    own_fetch = [pick(own_fetch, chip ^ (r // 2)) for r in range(0, n, 2)]
    tables = (cos * fold, sin_r * fold, sin_l * fold, cos, sin_r, sin_l)
    down_all, tables, down_w, own_fetch = tie(down_all, tables, down_w, own_fetch)

    token_rows = block_input[0].astype(F32)
    normed_float, attn_inverse = rms_forward(token_rows, attn_gain_all)
    normed = normed_float.astype(BF16)
    latent = jnp.dot(normed, down_all, preferred_element_type=F32)
    q_latent, kv_latent, rope_latent = jnp.split(latent, [rank_q, rank_q + rank_kv], axis=1)
    q_lat_float, q_inverse = rms_forward(q_latent, q_gain_all)
    q_lat_normed = q_lat_float.astype(BF16)
    kv_float, kv_inverse = rms_forward(kv_latent, kv_gain_all)
    key_rope = jnp.pad(rotate(rope_latent, cosine, sine), ((0, 0), (NOPE, LANES - NOPE - ROPE)))
    kv_own = jnp.concatenate([kv_float, key_rope], axis=1).astype(BF16)
    kv_all = seq_gather(kv_own, layer, layers)
    cotangent = out_cotangent[0].astype(F32)
    grad_low = (depth_scale * cotangent).astype(BF16)
    up_all, kv_all, own_fetch, grad_low = tie(up_all, kv_all, own_fetch, grad_low)
    kv_normed, key_rope_all = kv_all[:, :rank_kv], kv_all[:, rank_kv:]
    forward_args = (
        bounds, q_lat_normed, up_all, kv_normed, key_rope_all,
        *tables[:3], start_row, full_rows, mask_rows,
    )

    fetched_blocks = [swap(block, 2 * r, n) if r else block for r, block in enumerate(own_fetch)]
    outputs = attend_forward(ATTEND_PARTS[0], [], [], *forward_args)
    grad_blocks = own_blocks(grad_low)
    moved = gather_step(grad_blocks, n, 0)
    outputs, fetched_blocks = tie(outputs, fetched_blocks)
    fetched = blank((2, chips, fetch, ff_sent))
    for r, block in enumerate(fetched_blocks):
        fetched = lax.dynamic_update_slice(fetched, block[:, None], (0, chip ^ r, 0, 0))
    passed = [(fetched, fetched)]
    for step in range(1, layers):
        link = (
            lax.ppermute(passed[-1][0], "seq", [(i, i + 1) for i in range(layers - 1)]),
            lax.ppermute(passed[-1][1], "seq", [(i + 1, i) for i in range(layers - 1)]),
        )
        if step < len(ATTEND_PARTS):
            outputs = attend_forward(ATTEND_PARTS[step], outputs, [], *forward_args)
            if step < layers - 1:
                outputs, link = tie(outputs, link)
            if step == 1:
                outputs, moved = tie(outputs, moved)
                grad_blocks = {**grad_blocks, **moved}
        passed.append(link)
    for part in ATTEND_PARTS[layers:]:
        outputs = attend_forward(part, outputs, [], *forward_args)
    attended, queries, log_total = outputs
    for at in range(1, len(steps) - 1):
        grad_blocks = {**grad_blocks, **gather_step(grad_blocks, n, at)}
    attn_branch = jnp.dot(attended, out_proj_all, preferred_element_type=F32)
    attn_branch, grad_blocks, passed = tie(attn_branch, grad_blocks, passed)
    middle = token_rows + depth_scale * attn_branch
    mlp_float, mlp_inverse = rms_forward(middle, mlp_gain_all)
    normed_blocks = own_blocks(mlp_float.astype(BF16))
    normed_blocks = {**normed_blocks, **gather_step(normed_blocks, n, 0)}
    layer_blocks = [jnp.where(layer >= shift, passed[shift][0], passed[layers - shift][1]) for shift in range(1, layers)]
    for at in range(1, len(steps) - 1):
        normed_blocks = {**normed_blocks, **gather_step(normed_blocks, n, at)}
    hidden = [blank((chips, 2, layers, fetch, ff_wide)) for _ in range(2)]
    for shift in range(layers):
        block = layer_blocks[shift - 1] if shift else fetched
        source = (layer - shift) % layers
        for owner, arrived in ((core, block), (1 - core, swap(block, 1, n))):
            hidden = [
                lax.dynamic_update_slice(whole, v[:, None, None], (0, owner, source, 0, 0)) for whole, v in zip(hidden, arrived)
            ]
    gate_w, up_w = (v.reshape(D, ff_wide) for v in hidden)
    half = rows // 2
    first_rows = [sum(len(step) for step in steps[:i]) * half for i in range(len(steps))]
    kept = []
    for step, at in zip(steps, first_rows):
        kept = hidden_units(
            at, n * half, kept, [normed_blocks[key] for key in step], [grad_blocks[key] for key in step], gate_w, up_w, down_w
        )
    active, grad_gate, grad_up = kept
    all_normed = jnp.concatenate([normed_blocks[key] for step in steps for key in step])
    all_grad = jnp.concatenate([grad_blocks[key] for step in steps for key in step])

    back = lambda i, hidden: dict(zip(steps[i], to_tokens(first_rows[i], half, len(steps[i]), hidden, [gate_w, up_w], 1)))
    last_blocks = back(-1, [grad_gate, grad_up])
    last_blocks, active_late, earlier = tie(last_blocks, active, [grad_gate, grad_up])
    down_whole = dot(active_late, all_grad, 0, 0).astype(BF16)
    last_blocks, earlier = tie(last_blocks, [grad_gate, grad_up])
    half_ff = ff_chip // 2
    half_of = lambda at: lax.dynamic_slice_in_dim(down_whole, at * half_ff, half_ff, 0)
    down_part = (half_of(core).astype(F32) + swap(half_of(1 - core), 1, n).astype(F32)).astype(BF16)
    early_blocks = {}
    for i in range(len(steps) - 1)[::-1]:
        early_blocks.update(back(i, earlier))
    blocks, _ = scatter_step({**last_blocks, **early_blocks}, n, len(steps) - 2)
    blocks, all_normed, down_part = tie(blocks, all_normed, down_part)
    down_share = lax.psum_scatter(down_part, "seq", scatter_dimension=0, tiled=True)
    hidden_parts, hidden_shares, crossing = [], [], []
    for grads in (grad_gate, grad_up):
        whole = dot(all_normed, grads, 0, 0).astype(BF16).reshape(chips, 2, layers, fetch, ff_wide)
        if crossing:
            whole, down_share = tie(whole, down_share)
        crossing.append((pick(whole, core, 1), swap(pick(whole, 1 - core, 1), 1, n)))
    for at in range(len(steps) - 2)[::-1]:
        blocks, _ = scatter_step(blocks, n, at)

    def over_layers(crossed):
        part = (crossed[0].astype(F32) + crossed[1].astype(F32)).astype(BF16).transpose(1, 0, 2, 3)
        hidden_parts.append(part)
        hidden_shares.append(lax.psum_scatter(part, "seq", scatter_dimension=0, tiled=True)[0])

    blocks, crossing[0] = tie(blocks, crossing[0])
    over_layers(crossing[0])
    grad_mlp_normed = jnp.concatenate([blocks[0, part] for part in range(2)]).astype(F32)
    grad_mid_norm, mlp_gain_part = rms_backward(middle, mlp_inverse, mlp_gain_all, grad_mlp_normed)
    grad_middle = cotangent + grad_mid_norm
    grad_attn = (depth_scale * grad_middle).astype(BF16)
    out_proj_part = dot(attended, grad_attn, 0, 0).astype(BF16)
    grad_attended = dot(grad_attn, out_proj_all, 1, 1).astype(BF16)
    grad_attended, crossing[1] = tie(grad_attended, crossing[1])
    over_layers(crossing[1])
    backward_args = (
        bounds, q_lat_normed.T, up_all, queries, kv_normed, kv_normed.T, key_rope_all, grad_attended, attended, log_total,
        *tables[3:], start_row, full_rows, mask_rows,
    )
    out_shares = core_shares(out_proj_part, n)
    out_arrived = swap(pick(out_shares, 1 - core), 1, n)
    first = attend_backward(BACK_PARTS[0], [], [*hidden_parts, out_proj_part], *backward_args)
    down_low = lax.all_gather(down_share, "seq", axis=0, tiled=True)
    first, hidden_shares, down_share, out_arrived = tie(first, hidden_shares, down_share, out_arrived)
    out_mine = (pick(out_shares, core).astype(F32) + out_arrived.astype(F32)).astype(BF16)
    first, out_mine = tie(first, out_mine)
    hidden_share = jnp.stack(hidden_shares)
    hidden_blocks = [pick(hidden_share, chip ^ (r // 2), 1) for r in range(0, n, 2)]
    hidden_blocks = [swap(block, 2 * r, n) if r else block for r, block in enumerate(hidden_blocks)]
    second = attend_backward(BACK_PARTS[1], first, [down_share], *backward_args)
    second, hidden_blocks = tie(second, hidden_blocks)
    hidden_blocks = jnp.stack(hidden_blocks)
    hidden_blocks = [pick(hidden_blocks, chip ^ c)[..., :ff_chip] for c in range(chips)]
    placed = [jnp.concatenate([block[at] for block in hidden_blocks], axis=1) for at in range(2)]
    gate_low, up_low = (lax.all_gather(v, "seq", axis=0, tiled=True) for v in placed)
    third = attend_backward(BACK_PARTS[2], second, placed, *backward_args)
    out_blocks, third = scatter_step(chip_blocks(out_mine, chip, n), n, len(steps) - 2, third)
    for at in range(len(steps) - 2)[::-1]:
        out_blocks, _ = scatter_step(out_blocks, n, at)
    out_share = jnp.concatenate([out_blocks[0, part] for part in range(2)]).astype(BF16)
    third, active_last = tie(third, active)
    q_up_part, kv_up_part, grad_kv_all, grad_rope_all, grad_q_lat = third
    grad_q_float, q_gain_part = rms_backward(q_latent, q_inverse, q_gain_all, grad_q_lat)
    grad_kv = seq_scatter(jnp.concatenate([grad_kv_all, grad_rope_all], axis=1).astype(BF16), layer, layers)
    branch = {}
    for step, at in zip(steps, first_rows):
        branch.update(zip(step, to_tokens(at, half, len(step), [active_last], [down_w], 0)))
    grad_kv, gate_low, down_low, branch = tie(grad_kv, gate_low, down_low, branch)
    up_parts = jnp.concatenate([q_up_part, kv_up_part], axis=1).reshape(-1, HEADS * LANES)
    up_share = fsdp_scatter(up_parts, core, chip, n).astype(BF16)
    grad_kv_first, kv_gain_part = rms_backward(kv_latent, kv_inverse, kv_gain_all, grad_kv[:, :rank_kv])
    grad_rope = rotate(grad_kv[:, rank_kv + NOPE : rank_kv + NOPE + ROPE], cosine, -sine)
    grad_latent = jnp.concatenate([grad_q_float, grad_kv_first, grad_rope], axis=1).astype(BF16)
    down_all_part = dot(normed, grad_latent, 0, 0)
    grad_normed = dot(grad_latent, down_all, 1, 1)
    grad_in_norm, attn_gain_part = rms_backward(token_rows, attn_inverse, attn_gain_all, grad_normed)
    grad_input = (grad_middle + grad_in_norm).reshape(block_input.shape)

    gain_parts = [v.reshape(n, -1) for v in (attn_gain_part, mlp_gain_part, q_gain_part, kv_gain_part)]
    gain_rows = jnp.concatenate(gain_parts, axis=1)
    gain_rows = jnp.pad(gain_rows[:, None], ((0, 0), (0, 15), (0, latent.shape[1] - gain_rows.shape[1])))
    down_rows = D // n
    down_all_part = jnp.concatenate([down_all_part.reshape(n, down_rows, -1), gain_rows], axis=1)
    down_all_share = fsdp_scatter(down_all_part.reshape(-1, latent.shape[1]), core, chip, n).astype(BF16)
    up_share, out_share, down_all_share, up_low, branch = tie(up_share, out_share, down_all_share, up_low, branch)
    up_grad, out_proj_grad, down_all_grad = (v.astype(F32) for v in lax.psum((up_share, out_share, down_all_share), "seq"))
    down_grad = down_low.astype(F32)
    gate_up_grad = jnp.concatenate([gate_low, up_low], axis=1).astype(F32)
    output = (middle + depth_scale * chip_scatter(branch, n)).astype(BF16).reshape(block_input.shape)
    gain_sum = down_all_grad[down_rows]
    down_all_grad = down_all_grad[:down_rows]
    q_up_grad = up_grad[:q_rows].reshape(-1, HEADS, LANES)[..., : NOPE + ROPE].reshape(-1, HEADS * (NOPE + ROPE))
    kv_up_grad = up_grad[q_rows:]
    ends = [sum(widths[: i + 1]) for i in range(4)]
    attn_gain_grad, mlp_gain_grad, q_gain_grad, kv_gain_grad = jnp.split(gain_sum[: ends[3]], ends[:3])
    return (
        output,
        grad_input,
        attn_gain_grad,
        down_all_grad[:, :rank_q],
        q_gain_grad,
        q_up_grad,
        down_all_grad[:, rank_q:],
        kv_gain_grad,
        kv_up_grad,
        out_proj_grad,
        mlp_gain_grad,
        gate_up_grad,
        down_grad,
    )


def solution(mesh):
    tokens, matrix, vector = P("fsdp", "seq", None), P("fsdp", None), P("fsdp")
    return jax.shard_map(
        functools.partial(body, mesh.shape["fsdp"]),
        mesh=mesh,
        in_specs=(tokens, matrix, vector, matrix, vector, matrix, matrix, vector, matrix, matrix, vector, matrix, matrix, tokens),
        out_specs=(tokens, tokens, vector, matrix, vector, matrix, matrix, vector, matrix, matrix, vector, matrix, matrix),
        check_vma=False,
    )
```

```python
import functools, math
import jax
import jax.numpy as jnp
from jax import lax
from jax.experimental import pallas as pl
from jax.experimental.pallas import tpu as pltpu
from jax.sharding import PartitionSpec as P

HEADS = 40
NOPE = 64
ROPE = 32
PROMPT = 1024
LANES = 128
NEG = -1e30
SCALE = (NOPE + ROPE) ** -0.5
LOG2E = math.log2(math.e)
LN2 = math.log(2.0)


LIGHT = pl.CostEstimate(flops=1 << 20, bytes_accessed=1 << 16, transcendentals=0)


def dot(a, b, ca, cb):
    return lax.dot_general(a, b, (((ca,), (cb,)), ((), ())), preferred_element_type=jnp.float32)


def flat(ref):
    return ref[...].reshape(-1, ref.shape[-1])


def fwd_kernel(bounds, qlat, qup_ref, kvn, kvup_ref, krope, cos, sin_r, sin_l, start, *rest, full_rows, mask_rows):
    out, q_out, lse_out, m_scr, acc_scr = rest[-5:]
    rows = qlat.shape[0]
    lane = lax.broadcasted_iota(jnp.int32, (1, LANES), 1)
    low_half = lane < NOPE
    raw = dot(qlat[...], flat(qup_ref), 1, 0)
    kvup = flat(kvup_ref)
    for h in range(2):
        u = raw[:, h * LANES:(h + 1) * LANES]
        turned = u * cos[...] + pltpu.roll(u, 16, 1) * sin_r[...] + pltpu.roll(u, LANES - 16, 1) * sin_l[...]
        q_out[:, h * LANES:(h + 1) * LANES] = turned.astype(jnp.bfloat16)
    m_scr[...] = jnp.full_like(m_scr, NEG)
    acc_scr[...] = jnp.zeros_like(acc_scr)

    def block(first, size, masked):
        span = pl.ds(first, size)
        kv = dot(kvn[span, :], kvup, 1, 0).astype(jnp.bfloat16)
        rope_rows = krope[span, :]
        if masked:
            key_index = first + lax.broadcasted_iota(jnp.int32, (size, rows), 0)
            own = bounds[3] + lax.broadcasted_iota(jnp.int32, (size, rows), 1)
            allowed = (key_index <= own) & ((key_index >= start[...]) | (key_index < PROMPT))
        scores, vals = [], []
        for h in range(2):
            kv_h = kv[:, h * LANES:(h + 1) * LANES]
            key = jnp.where(low_half, kv_h, rope_rows)
            vals.append(jnp.where(low_half, jnp.ones_like(kv_h), kv_h))
            s = dot(key, q_out[:, h * LANES:(h + 1) * LANES], 1, 1)
            scores.append(jnp.where(allowed, s, NEG) if masked else s)
        for h in range(2):
            m_old = m_scr[h:h + 1, :]
            m_new = jnp.maximum(m_old, jnp.max(scores[h], axis=0, keepdims=True))
            m_scr[h:h + 1, :] = m_new
            p = jnp.exp2(scores[h] - m_new).astype(jnp.bfloat16)
            acc_scr[h] = acc_scr[h] * jnp.exp2(m_old - m_new) + dot(vals[h], p, 0, 0)

    lax.fori_loop(0, bounds[0], lambda i, c: (block(pl.multiple_of(i * full_rows, full_rows), full_rows, False), c)[1], 0)
    lax.fori_loop(bounds[1], bounds[2], lambda i, c: (block(pl.multiple_of(i * mask_rows, mask_rows), mask_rows, True), c)[1], 0)
    parts = []
    for h in range(2):
        total = acc_scr[h, 0:1, :]
        parts.append(acc_scr[h, NOPE:, :] / total)
        lse_out[h:h + 1, :] = m_scr[h:h + 1, :] + jnp.log2(total)
    out[...] = jnp.concatenate(parts, axis=0).T.astype(jnp.bfloat16)


def attend_forward(part, prev, deps, bounds, qlat, up, kvn, krope, cos, sin_r, sin_l, start, full_rows, mask_rows):
    rows, rank = qlat.shape
    q_rows, kv_rows = rank // up.shape[0], kvn.shape[1] // up.shape[0]
    whole = lambda *_: (0, 0)
    first_pair, pairs = part
    col = lambda i, b: (0, i + first_pair)
    return pl.pallas_call(
        functools.partial(fwd_kernel, full_rows=full_rows, mask_rows=mask_rows),
        grid_spec=pltpu.PrefetchScalarGridSpec(
            num_scalar_prefetch=1,
            grid=(pairs,),
            in_specs=[
                pl.BlockSpec((rows, rank), whole),
                pl.BlockSpec((up.shape[0], q_rows, 2 * LANES), lambda i, b: (0, 0, i + first_pair)),
                pl.BlockSpec(kvn.shape, whole),
                pl.BlockSpec((up.shape[0], kv_rows, 2 * LANES), lambda i, b: (0, q_rows // kv_rows, i + first_pair)),
                pl.BlockSpec(krope.shape, whole),
                pl.BlockSpec(cos.shape, whole),
                pl.BlockSpec(cos.shape, whole),
                pl.BlockSpec(cos.shape, whole),
                pl.BlockSpec((1, rows), whole),
            ] + [pl.BlockSpec(memory_space=pl.ANY)] * (len(prev) + len(deps)),
            out_specs=[
                pl.BlockSpec((rows, LANES), col),
                pl.BlockSpec((rows, 2 * LANES), col),
                pl.BlockSpec((8, rows), lambda i, b: (i + first_pair, 0)),
            ],
            scratch_shapes=[pltpu.VMEM((8, rows), jnp.float32), pltpu.VMEM((2, LANES, rows), jnp.float32)],
        ),
        out_shape=[
            jax.ShapeDtypeStruct((rows, HEADS * NOPE), jnp.bfloat16),
            jax.ShapeDtypeStruct((rows, HEADS * LANES), jnp.bfloat16),
            jax.ShapeDtypeStruct((HEADS // 2 * 8, rows), jnp.float32),
        ],
        compiler_params=pltpu.CompilerParams(vmem_limit_bytes=48 << 20),
        cost_estimate=LIGHT,
        input_output_aliases={10 + i: i for i in range(len(prev))},
        name="attend_forward",
    )(bounds, qlat, up, kvn, up, krope, cos, sin_r, sin_l, start, *prev, *deps)


def bwd_kernel(bounds, qlat_t, qup_ref, q, kvn, kvn_t, kvup_ref, krope, grad_out, out, lse, cos, sin_r, sin_l, start, *rest, full_rows, mask_rows, resumes):
    dqup_out, dkvup_out, dkvn, drope, dqlat, go_scr, dq_scr, delta_scr, dkvup = rest[-9:]
    kvup = flat(kvup_ref)
    rows = q.shape[0]
    lane = lax.broadcasted_iota(jnp.int32, (1, LANES), 1)
    low_half = lane < NOPE

    @pl.when(pl.program_id(0) == 0)
    def _():
        dkvn[...] = rest[-12][...] if resumes else jnp.zeros_like(dkvn)
        drope[...] = rest[-11][...] if resumes else jnp.zeros_like(drope)
        dqlat[...] = rest[-10][...] if resumes else jnp.zeros_like(dqlat)

    go = grad_out[...].astype(jnp.float32)
    prod_t = (go * out[...].astype(jnp.float32)).T
    delta_scr[0:1, :] = jnp.sum(prod_t[:NOPE], axis=0, keepdims=True)
    delta_scr[1:2, :] = jnp.sum(prod_t[NOPE:], axis=0, keepdims=True)
    zero = jnp.zeros_like(go)
    go_scr[0] = jnp.where(low_half, zero, pltpu.roll(go, NOPE, 1)).astype(jnp.bfloat16)
    go_scr[1] = jnp.where(low_half, zero, go).astype(jnp.bfloat16)
    dq_scr[...] = jnp.zeros_like(dq_scr)
    dkvup[...] = jnp.zeros_like(dkvup)

    def block(first, size, masked):
        span = pl.ds(first, size)
        kv = dot(kvn[span, :], kvup, 1, 0).astype(jnp.bfloat16)
        rope_rows = krope[span, :]
        if masked:
            key_index = first + lax.broadcasted_iota(jnp.int32, (size, rows), 0)
            own = bounds[3] + lax.broadcasted_iota(jnp.int32, (size, rows), 1)
            allowed = (key_index <= own) & ((key_index >= start[...]) | (key_index < PROMPT))
        pieces = []
        rope_sum = None
        for h in range(2):
            kv_h = kv[:, h * LANES:(h + 1) * LANES]
            q_h = q[:, h * LANES:(h + 1) * LANES]
            key = jnp.where(low_half, kv_h, rope_rows)
            p = jnp.exp2(dot(key, q_h, 1, 1) - lse[h:h + 1, :])
            if masked:
                p = jnp.where(allowed, p, 0.0)
            ds = (p * (dot(kv_h, go_scr[h], 1, 1) - delta_scr[h:h + 1, :])).astype(jnp.bfloat16)
            dk = dot(ds, q_h, 1, 0) * LN2
            dv = dot(p.astype(jnp.bfloat16), go_scr[h], 1, 0)
            dq_scr[h] += dot(key, ds, 0, 0)
            pieces.append(jnp.where(low_half, dk, dv).astype(jnp.bfloat16))
            rope_sum = dk if rope_sum is None else rope_sum + dk
        dkv = jnp.concatenate(pieces, axis=1)
        drope[span, :] += rope_sum
        dkvn[span, :] += dot(dkv, kvup, 1, 1)
        dkvup[...] += dot(kvn_t[:, span], dkv, 1, 0)

    lax.fori_loop(0, bounds[0], lambda i, c: (block(pl.multiple_of(i * full_rows, full_rows), full_rows, False), c)[1], 0)
    lax.fori_loop(bounds[1], bounds[2], lambda i, c: (block(pl.multiple_of(i * mask_rows, mask_rows), mask_rows, True), c)[1], 0)
    turned = []
    for h in range(2):
        u = dq_scr[h].T * SCALE
        turned.append(u * cos[...] - pltpu.roll(u, 16, 1) * sin_r[...] - pltpu.roll(u, LANES - 16, 1) * sin_l[...])
    dq = jnp.concatenate(turned, axis=1).astype(jnp.bfloat16)
    dqlat[...] += dot(dq, flat(qup_ref), 1, 1)
    dqup_out[...] = dot(qlat_t[...], dq, 1, 0).astype(jnp.bfloat16).reshape(dqup_out.shape)
    dkvup_out[...] = dkvup[...].astype(jnp.bfloat16).reshape(dkvup_out.shape)


def attend_backward(part, prev, deps, bounds, qlat_t, up, q, kvn, kvn_t, krope, grad_out, out, lse, cos, sin_r, sin_l, start, full_rows, mask_rows):
    rows = q.shape[0]
    keys, rank = kvn.shape
    devices = up.shape[0]
    q_rows, kv_rows = qlat_t.shape[0] // devices, rank // devices
    up_block = lambda i, b: (0, 0, i + first_pair)
    whole = lambda *_: (0, 0)
    first_pair, pairs = part
    col = lambda i, b: (0, i + first_pair)
    return pl.pallas_call(
        functools.partial(bwd_kernel, full_rows=full_rows, mask_rows=mask_rows, resumes=bool(prev)),
        grid_spec=pltpu.PrefetchScalarGridSpec(
            num_scalar_prefetch=1,
            grid=(pairs,),
            in_specs=[
                pl.BlockSpec(qlat_t.shape, whole),
                pl.BlockSpec((devices, q_rows, 2 * LANES), up_block),
                pl.BlockSpec((rows, 2 * LANES), col),
                pl.BlockSpec(kvn.shape, whole),
                pl.BlockSpec(kvn_t.shape, whole),
                pl.BlockSpec((devices, kv_rows, 2 * LANES), lambda i, b: (0, q_rows // kv_rows, i + first_pair)),
                pl.BlockSpec(krope.shape, whole),
                pl.BlockSpec((rows, LANES), col),
                pl.BlockSpec((rows, LANES), col),
                pl.BlockSpec((8, rows), lambda i, b: (i + first_pair, 0)),
                pl.BlockSpec(cos.shape, whole),
                pl.BlockSpec(cos.shape, whole),
                pl.BlockSpec(cos.shape, whole),
                pl.BlockSpec((1, rows), whole),
            ] + [pl.BlockSpec(memory_space=pl.ANY)] * (len(prev[:2]) + len(deps)) + [pl.BlockSpec(v.shape, whole) for v in prev[2:]],
            out_specs=[
                pl.BlockSpec((devices, q_rows, 2 * LANES), up_block),
                pl.BlockSpec((devices, kv_rows, 2 * LANES), up_block),
                pl.BlockSpec((keys, rank), whole),
                pl.BlockSpec((keys, LANES), whole),
                pl.BlockSpec((rows, qlat_t.shape[0]), whole),
            ],
            scratch_shapes=[
                pltpu.VMEM((2, rows, LANES), jnp.bfloat16),
                pltpu.VMEM((2, LANES, rows), jnp.float32),
                pltpu.VMEM((8, rows), jnp.float32),
                pltpu.VMEM((rank, 2 * LANES), jnp.float32),
            ],
        ),
        out_shape=[
            jax.ShapeDtypeStruct((devices, q_rows, HEADS * LANES), jnp.bfloat16),
            jax.ShapeDtypeStruct((devices, kv_rows, HEADS * LANES), jnp.bfloat16),
            jax.ShapeDtypeStruct((keys, rank), jnp.float32),
            jax.ShapeDtypeStruct((keys, LANES), jnp.float32),
            jax.ShapeDtypeStruct((rows, qlat_t.shape[0]), jnp.float32),
        ],
        compiler_params=pltpu.CompilerParams(vmem_limit_bytes=48 << 20),
        cost_estimate=LIGHT,
        input_output_aliases={15 + i: i for i in range(len(prev[:2]))},
        name="attend_backward",
    )(bounds, qlat_t, up, q, kvn, kvn_t, up, krope, grad_out, out, lse, cos, sin_r, sin_l, start, *prev[:2], *deps, *prev[2:])


def hidden_kernel(*refs, count):
    normed, grads, (gate_w, up_w, down_w) = refs[:count], refs[count : 2 * count], refs[2 * count : 2 * count + 3]
    active, grad_gate, grad_up = refs[-3:]
    height = normed[0].shape[0]
    for i in range(count):
        rows = slice(i * height, (i + 1) * height)
        x = normed[i][...]
        gate = dot(x, gate_w[...], 1, 0)
        upper = dot(x, up_w[...], 1, 0)
        grad = dot(grads[i][...], down_w[...], 1, 1)
        sigmoid = jax.nn.sigmoid(gate)
        silu = gate * sigmoid
        active[rows, :] = (silu * upper).astype(jnp.bfloat16)
        grad_gate[rows, :] = (grad * upper * sigmoid * (1.0 + gate * (1.0 - sigmoid))).astype(jnp.bfloat16)
        grad_up[rows, :] = (grad * silu).astype(jnp.bfloat16)


def hidden_units(first_row, all_rows, prev, normed, grads, gate_w, up_w, down_w):
    count = len(normed)
    height, width = normed[0].shape
    rows, hidden = count * height, gate_w.shape[1]
    tile = 2 * LANES
    whole = lambda j: (0, 0)
    at = first_row // rows
    return pl.pallas_call(
        functools.partial(hidden_kernel, count=count),
        grid=(pl.cdiv(hidden, tile),),
        in_specs=[pl.BlockSpec((height, width), whole)] * (2 * count)
        + [pl.BlockSpec((width, tile), lambda j: (0, j))] * 2
        + [pl.BlockSpec((tile, width), lambda j: (j, 0))]
        + [pl.BlockSpec(memory_space=pl.ANY)] * len(prev),
        out_specs=[pl.BlockSpec((rows, tile), lambda j: (at, j))] * 3,
        out_shape=[jax.ShapeDtypeStruct((all_rows, hidden), jnp.bfloat16)] * 3,
        input_output_aliases={2 * count + 3 + i: i for i in range(len(prev))},
        compiler_params=pltpu.CompilerParams(vmem_limit_bytes=48 << 20),
        cost_estimate=pl.CostEstimate(
            flops=6 * rows * width * hidden, bytes_accessed=6 * width * hidden + 8 * rows * width, transcendentals=0
        ),
        name="hidden_units",
    )(*normed, *grads, gate_w, up_w, down_w, *prev)


def back_kernel(*refs, terms, contract):
    left, right, outs = refs[:terms], refs[terms : 2 * terms], refs[2 * terms :]
    height = outs[0].shape[0]
    for i, out in enumerate(outs):
        rows = slice(i * height, (i + 1) * height)
        total = dot(left[0][rows, :], right[0][...], 1, contract)
        for a, b in zip(left[1:], right[1:]):
            total = total + dot(a[rows, :], b[...], 1, contract)
        out[...] = total.astype(jnp.bfloat16)


def to_tokens(first_row, height, count, left, right, contract):
    hidden = left[0].shape[1]
    width = right[0].shape[1 - contract]
    rows = height * count
    tile = 2 * LANES
    at = first_row // rows
    if contract:
        right_spec = pl.BlockSpec((tile, hidden), lambda j: (j, 0))
    else:
        right_spec = pl.BlockSpec((hidden, tile), lambda j: (0, j))
    return pl.pallas_call(
        functools.partial(back_kernel, terms=len(left), contract=contract),
        grid=(width // tile,),
        in_specs=[pl.BlockSpec((rows, hidden), lambda j: (at, 0))] * len(left) + [right_spec] * len(left),
        out_specs=[pl.BlockSpec((height, tile), lambda j: (0, j))] * count,
        out_shape=[jax.ShapeDtypeStruct((height, width), jnp.bfloat16)] * count,
        compiler_params=pltpu.CompilerParams(vmem_limit_bytes=48 << 20),
        cost_estimate=LIGHT,
        name="to_tokens",
    )(*left, *right)


def blank(shape):
    return pl.pallas_call(
        lambda out: None,
        out_specs=pl.BlockSpec(memory_space=pl.ANY),
        out_shape=jax.ShapeDtypeStruct(shape, jnp.bfloat16),
        cost_estimate=LIGHT,
        name="blank",
    )()


D = 2560
FF = 6400
CONTS = 4
variance_eps = 1e-05
depth_scale = 1.4 / math.sqrt(62.0)
BF16 = jnp.bfloat16
F32 = jnp.float32


def rms_forward(values, gain_vector):
    inverse = lax.rsqrt(jnp.mean(values * values, axis=-1, keepdims=True) + variance_eps)
    return (values * inverse * gain_vector, inverse)


def rms_backward(values, inverse, gain_vector, upstream):
    scaled = upstream * gain_vector
    inner_mean = jnp.mean(scaled * values, axis=-1, keepdims=True)
    grad_values = inverse * scaled - values * inverse * inverse * inverse * inner_mean
    grad_gain = jnp.sum(upstream * values * inverse, axis=0)
    return (grad_values, grad_gain)


def segment_starts(lengths, index):
    own = jnp.zeros_like(index)
    begin = jnp.int32(PROMPT)
    for c in range(CONTS):
        own = jnp.where(index >= begin, begin, own)
        begin = begin + lengths[c]
    return own


def rope_tables(position):
    frequency = jnp.exp(jnp.arange(ROPE // 2, dtype=F32) * (-2.0 * math.log(10000.0) / ROPE))
    angles = position.astype(F32)[:, None] * frequency[None, :]
    cosine, sine = jnp.cos(angles), jnp.sin(angles)
    rows = position.shape[0]
    zeros = lambda n: jnp.zeros((rows, n), F32)
    return (
        jnp.concatenate([jnp.ones((rows, NOPE), F32), cosine, cosine, zeros(32)], axis=1),
        jnp.concatenate([zeros(80), sine, zeros(32)], axis=1),
        jnp.concatenate([zeros(64), -sine, zeros(48)], axis=1),
        cosine,
        sine,
    )


def rotate(values, cosine, sine):
    first, second = values[:, : ROPE // 2], values[:, ROPE // 2 :]
    return jnp.concatenate([first * cosine - second * sine, second * cosine + first * sine], axis=1)


def swap(tensor, bit, n):
    return lax.ppermute(tensor, "fsdp", [(i, i ^ bit) for i in range(n)])


def bit_orders(n):
    bits = []
    bit = 2
    while bit < n:
        bits.append(bit)
        bit *= 2
    return [bits, bits[::-1]]


def arrivals(n):
    orders = bit_orders(n)
    steps = [[(0, part) for part in range(2)]]
    for at in range(len(orders[0])):
        steps.append([
            (r | order[at], part)
            for part, order in enumerate(orders)
            for r in range(0, n, 2)
            if not r & ~sum(order[:at])
        ])
    return steps


BACK_PARTS = ((0, 12), (12, 4), (16, HEADS // 2 - 16))
ATTEND_PARTS = ((0, 4), (4, 7), (11, 5), (16, HEADS // 2 - 16))


def own_blocks(tensor):
    half = tensor.shape[0] // 2
    return {(0, part): tensor[part * half : (part + 1) * half] for part in range(2)}


def gather_step(blocks, n, at):
    return {
        (r | order[at], p): swap(block, order[at], n)
        for part, order in enumerate(bit_orders(n))
        for (r, p), block in blocks.items()
        if p == part
    }


def scatter_step(blocks, n, at, hold=None):
    arrived = {}
    for part, order in enumerate(bit_orders(n)):
        bit = order[at]
        for r, p in blocks:
            if p == part and not r & bit:
                arrived[r, p] = swap(blocks[r | bit, p].astype(BF16), bit, n)
    if hold is not None:
        hold, arrived = tie(hold, arrived)
    return {key: blocks[key].astype(F32) + block.astype(F32) for key, block in arrived.items()}, hold


def chip_scatter(blocks, n):
    for at in range(len(bit_orders(n)[0]))[::-1]:
        blocks, _ = scatter_step(blocks, n, at)
    return jnp.concatenate([blocks[0, part] for part in range(2)])


def tie(*trees):
    return lax.optimization_barrier(trees)


def ring(shift, count):
    return [(i, (i + shift) % count) for i in range(count)]


def seq_gather(share, layer, layers):
    whole = jnp.zeros((layers, *share.shape), share.dtype)
    for shift in range(layers):
        block = lax.ppermute(share, "seq", ring(shift, layers)) if shift else share
        whole = lax.dynamic_update_index_in_dim(whole, block, (layer - shift) % layers, 0)
    return whole.reshape(-1, *share.shape[1:])


def seq_scatter(whole, layer, layers):
    shares = whole.reshape(layers, -1, *whole.shape[1:])
    total = pick(shares, layer).astype(F32)
    for shift in range(1, layers):
        total = total + lax.ppermute(pick(shares, (layer + shift) % layers), "seq", ring(shift, layers)).astype(F32)
    return total


def pick(tensor, at, axis=0):
    return lax.dynamic_index_in_dim(tensor, at, axis, keepdims=False)


def core_scatter(split, core, n, axis=0):
    arrived = swap(pick(split, 1 - core, axis).astype(BF16), 1, n)
    return pick(split, core, axis).astype(F32) + arrived.astype(F32)


def core_shares(part, n):
    return jnp.swapaxes(part.astype(BF16).reshape(n // 2, 2, part.shape[0] // n, part.shape[1]), 0, 1)


def chip_blocks(mine, chip, n):
    half = mine.shape[1] // 2
    blocks = {}
    for r in range(0, n, 2):
        own = pick(mine, chip ^ (r // 2))
        for p in range(2):
            blocks[r, p] = own[p * half : (p + 1) * half]
    return blocks


def fsdp_scatter(part, core, chip, n):
    return chip_scatter(chip_blocks(core_scatter(core_shares(part, n), core, n).astype(BF16), chip, n), n)


def body(
    n,
    block_input,
    cont_lengths,
    attn_gain,
    q_down,
    q_gain,
    q_up,
    kv_down,
    kv_gain,
    kv_up,
    out_proj,
    mlp_gain,
    gate_up,
    down_proj,
    out_cotangent,
):
    rows = block_input.shape[1]
    chips = n // 2
    ff_chip = FF // chips
    ff_sent = -(-ff_chip // LANES) * LANES
    ff_wide = ff_sent
    group_len = rows * lax.axis_size("seq")
    device = lax.axis_index("fsdp")
    core, chip = device % 2, device // 2
    layers = lax.axis_size("seq")
    layer = lax.axis_index("seq")
    rank_q, rank_kv = q_up.shape[0] * n, kv_up.shape[0] * n
    first_row = lax.axis_index("seq") * rows
    index = first_row + jnp.arange(rows, dtype=jnp.int32)
    own_start = segment_starts(cont_lengths[0], index)
    position = jnp.where(own_start > 0, PROMPT + index - own_start, index)
    cos, sin_r, sin_l, cosine, sine = rope_tables(position)
    fold = SCALE * LOG2E
    start_row = own_start[None, :]
    full_rows, mask_rows = 1024, 512
    full_blocks = jnp.minimum(first_row, PROMPT) // full_rows
    bounds = jnp.stack([
        full_blocks,
        jnp.where(first_row < PROMPT, full_blocks * (full_rows // mask_rows), own_start[0] // mask_rows),
        (first_row + rows + mask_rows - 1) // mask_rows,
        first_row,
    ]).astype(jnp.int32)

    gains = lax.all_gather(jnp.concatenate([attn_gain, mlp_gain, q_gain, kv_gain]), "fsdp", axis=0)
    widths = [v.shape[0] for v in (attn_gain, mlp_gain, q_gain, kv_gain)]
    gain_list = []
    at = 0
    for width in widths:
        gain_list.append(gains[:, at : at + width].reshape(-1).astype(F32))
        at += width
    attn_gain_all, mlp_gain_all, q_gain_all, kv_gain_all = gain_list

    down_all = lax.all_gather(jnp.concatenate([q_down, kv_down], axis=1), "fsdp", axis=0, tiled=True)
    q_up_wide = jnp.pad(q_up.reshape(-1, HEADS, NOPE + ROPE), ((0, 0), (0, 0), (0, ROPE))).reshape(-1, HEADS * LANES)
    q_rows = q_up.shape[0]
    up_all = lax.all_gather(jnp.concatenate([q_up_wide, kv_up], axis=0), "fsdp", axis=0)
    out_proj_all = lax.all_gather(out_proj, "fsdp", axis=0, tiled=True)

    steps = arrivals(n)
    fetch = (D // n) // layers
    half_down = swap(down_proj, 1, n)
    down_w = jnp.concatenate([
        jnp.where(core == 0, down_proj, half_down),
        jnp.where(core == 0, half_down, down_proj),
        jnp.zeros((ff_wide - ff_chip, D), BF16),
    ])
    own_fetch = lax.dynamic_slice_in_dim(gate_up, layer * fetch, fetch, 0)
    widen = lambda v: jnp.pad(v, ((0, 0), (0, ff_sent - ff_chip)))
    own_fetch = jnp.stack([
        jnp.stack([widen(own_fetch[:, at + c * ff_chip : at + (c + 1) * ff_chip]) for at in (0, FF)]) for c in range(chips)
    ])
    own_fetch = [pick(own_fetch, chip ^ (r // 2)) for r in range(0, n, 2)]
    tables = (cos * fold, sin_r * fold, sin_l * fold, cos, sin_r, sin_l)
    down_all, tables, down_w, own_fetch = tie(down_all, tables, down_w, own_fetch)

    token_rows = block_input[0].astype(F32)
    normed_float, attn_inverse = rms_forward(token_rows, attn_gain_all)
    normed = normed_float.astype(BF16)
    latent = jnp.dot(normed, down_all, preferred_element_type=F32)
    q_latent, kv_latent, rope_latent = jnp.split(latent, [rank_q, rank_q + rank_kv], axis=1)
    q_lat_float, q_inverse = rms_forward(q_latent, q_gain_all)
    q_lat_normed = q_lat_float.astype(BF16)
    kv_float, kv_inverse = rms_forward(kv_latent, kv_gain_all)
    key_rope = jnp.pad(rotate(rope_latent, cosine, sine), ((0, 0), (NOPE, LANES - NOPE - ROPE)))
    kv_own = jnp.concatenate([kv_float, key_rope], axis=1).astype(BF16)
    kv_all = seq_gather(kv_own, layer, layers)
    cotangent = out_cotangent[0].astype(F32)
    grad_low = (depth_scale * cotangent).astype(BF16)
    up_all, kv_all, own_fetch, grad_low = tie(up_all, kv_all, own_fetch, grad_low)
    kv_normed, key_rope_all = kv_all[:, :rank_kv], kv_all[:, rank_kv:]
    forward_args = (
        bounds, q_lat_normed, up_all, kv_normed, key_rope_all,
        *tables[:3], start_row, full_rows, mask_rows,
    )

    fetched_blocks = [swap(block, 2 * r, n) if r else block for r, block in enumerate(own_fetch)]
    outputs = attend_forward(ATTEND_PARTS[0], [], [], *forward_args)
    grad_blocks = own_blocks(grad_low)
    moved = gather_step(grad_blocks, n, 0)
    outputs, fetched_blocks = tie(outputs, fetched_blocks)
    fetched = blank((2, chips, fetch, ff_sent))
    for r, block in enumerate(fetched_blocks):
        fetched = lax.dynamic_update_slice(fetched, block[:, None], (0, chip ^ r, 0, 0))
    passed = [(fetched, fetched)]
    for step in range(1, layers):
        link = (
            lax.ppermute(passed[-1][0], "seq", [(i, i + 1) for i in range(layers - 1)]),
            lax.ppermute(passed[-1][1], "seq", [(i + 1, i) for i in range(layers - 1)]),
        )
        if step < len(ATTEND_PARTS):
            outputs = attend_forward(ATTEND_PARTS[step], outputs, [], *forward_args)
            if step < layers - 1:
                outputs, link = tie(outputs, link)
            if step == 1:
                outputs, moved = tie(outputs, moved)
                grad_blocks = {**grad_blocks, **moved}
        passed.append(link)
    for part in ATTEND_PARTS[layers:]:
        outputs = attend_forward(part, outputs, [], *forward_args)
    attended, queries, log_total = outputs
    for at in range(1, len(steps) - 1):
        grad_blocks = {**grad_blocks, **gather_step(grad_blocks, n, at)}
    attn_branch = jnp.dot(attended, out_proj_all, preferred_element_type=F32)
    attn_branch, grad_blocks, passed = tie(attn_branch, grad_blocks, passed)
    middle = token_rows + depth_scale * attn_branch
    mlp_float, mlp_inverse = rms_forward(middle, mlp_gain_all)
    normed_blocks = own_blocks(mlp_float.astype(BF16))
    normed_blocks = {**normed_blocks, **gather_step(normed_blocks, n, 0)}
    layer_blocks = [jnp.where(layer >= shift, passed[shift][0], passed[layers - shift][1]) for shift in range(1, layers)]
    for at in range(1, len(steps) - 1):
        normed_blocks = {**normed_blocks, **gather_step(normed_blocks, n, at)}
    hidden = [blank((chips, 2, layers, fetch, ff_wide)) for _ in range(2)]
    for shift in range(layers):
        block = layer_blocks[shift - 1] if shift else fetched
        source = (layer - shift) % layers
        for owner, arrived in ((core, block), (1 - core, swap(block, 1, n))):
            hidden = [
                lax.dynamic_update_slice(whole, v[:, None, None], (0, owner, source, 0, 0)) for whole, v in zip(hidden, arrived)
            ]
    gate_w, up_w = (v.reshape(D, ff_wide) for v in hidden)
    half = rows // 2
    first_rows = [sum(len(step) for step in steps[:i]) * half for i in range(len(steps))]
    kept = []
    for step, at in zip(steps, first_rows):
        kept = hidden_units(
            at, n * half, kept, [normed_blocks[key] for key in step], [grad_blocks[key] for key in step], gate_w, up_w, down_w
        )
    active, grad_gate, grad_up = kept
    all_normed = jnp.concatenate([normed_blocks[key] for step in steps for key in step])
    all_grad = jnp.concatenate([grad_blocks[key] for step in steps for key in step])

    back = lambda i, hidden: dict(zip(steps[i], to_tokens(first_rows[i], half, len(steps[i]), hidden, [gate_w, up_w], 1)))
    last_blocks = back(-1, [grad_gate, grad_up])
    last_blocks, active_late, earlier = tie(last_blocks, active, [grad_gate, grad_up])
    down_whole = dot(active_late, all_grad, 0, 0).astype(BF16)
    last_blocks, earlier = tie(last_blocks, [grad_gate, grad_up])
    half_ff = ff_chip // 2
    half_of = lambda at: lax.dynamic_slice_in_dim(down_whole, at * half_ff, half_ff, 0)
    down_part = (half_of(core).astype(F32) + swap(half_of(1 - core), 1, n).astype(F32)).astype(BF16)
    early_blocks = {}
    for i in range(len(steps) - 1)[::-1]:
        early_blocks.update(back(i, earlier))
    blocks, _ = scatter_step({**last_blocks, **early_blocks}, n, len(steps) - 2)
    blocks, all_normed, down_part = tie(blocks, all_normed, down_part)
    down_share = lax.psum_scatter(down_part, "seq", scatter_dimension=0, tiled=True)
    hidden_parts, hidden_shares, crossing = [], [], []
    for grads in (grad_gate, grad_up):
        whole = dot(all_normed, grads, 0, 0).astype(BF16).reshape(chips, 2, layers, fetch, ff_wide)
        if crossing:
            for at in range(len(steps) - 2)[::-1]:
                blocks, (whole, down_share, crossing[0]) = scatter_step(blocks, n, at, (whole, down_share, crossing[0]))
        crossing.append((pick(whole, core, 1), swap(pick(whole, 1 - core, 1), 1, n)))

    def over_layers(crossed):
        part = (crossed[0].astype(F32) + crossed[1].astype(F32)).astype(BF16).transpose(1, 0, 2, 3)
        hidden_parts.append(part)
        hidden_shares.append(lax.psum_scatter(part, "seq", scatter_dimension=0, tiled=True)[0])

    over_layers(crossing[0])
    grad_mlp_normed = jnp.concatenate([blocks[0, part] for part in range(2)]).astype(F32)
    grad_mid_norm, mlp_gain_part = rms_backward(middle, mlp_inverse, mlp_gain_all, grad_mlp_normed)
    grad_middle = cotangent + grad_mid_norm
    grad_attn = (depth_scale * grad_middle).astype(BF16)
    out_proj_part = dot(attended, grad_attn, 0, 0).astype(BF16)
    grad_attended = dot(grad_attn, out_proj_all, 1, 1).astype(BF16)
    grad_attended, crossing[1] = tie(grad_attended, crossing[1])
    over_layers(crossing[1])
    backward_args = (
        bounds, q_lat_normed.T, up_all, queries, kv_normed, kv_normed.T, key_rope_all, grad_attended, attended, log_total,
        *tables[3:], start_row, full_rows, mask_rows,
    )
    out_shares = core_shares(out_proj_part, n)
    out_arrived = swap(pick(out_shares, 1 - core), 1, n)
    first = attend_backward(BACK_PARTS[0], [], [*hidden_parts, out_proj_part], *backward_args)
    down_low = lax.all_gather(down_share, "seq", axis=0, tiled=True)
    first, hidden_shares, down_share, out_arrived = tie(first, hidden_shares, down_share, out_arrived)
    out_mine = (pick(out_shares, core).astype(F32) + out_arrived.astype(F32)).astype(BF16)
    first, out_mine = tie(first, out_mine)
    hidden_share = jnp.stack(hidden_shares)
    hidden_blocks = [pick(hidden_share, chip ^ (r // 2), 1) for r in range(0, n, 2)]
    hidden_blocks = [swap(block, 2 * r, n) if r else block for r, block in enumerate(hidden_blocks)]
    second = attend_backward(BACK_PARTS[1], first, [down_share], *backward_args)
    second, hidden_blocks = tie(second, hidden_blocks)
    hidden_blocks = jnp.stack(hidden_blocks)
    hidden_blocks = [pick(hidden_blocks, chip ^ c)[..., :ff_chip] for c in range(chips)]
    placed = [jnp.concatenate([block[at] for block in hidden_blocks], axis=1) for at in range(2)]
    gate_low, up_low = (lax.all_gather(v, "seq", axis=0, tiled=True) for v in placed)
    third = attend_backward(BACK_PARTS[2], second, placed, *backward_args)
    out_blocks, third = scatter_step(chip_blocks(out_mine, chip, n), n, len(steps) - 2, third)
    for at in range(len(steps) - 2)[::-1]:
        out_blocks, _ = scatter_step(out_blocks, n, at)
    out_share = jnp.concatenate([out_blocks[0, part] for part in range(2)]).astype(BF16)
    third, active_last = tie(third, active)
    q_up_part, kv_up_part, grad_kv_all, grad_rope_all, grad_q_lat = third
    grad_q_float, q_gain_part = rms_backward(q_latent, q_inverse, q_gain_all, grad_q_lat)
    grad_kv = seq_scatter(jnp.concatenate([grad_kv_all, grad_rope_all], axis=1).astype(BF16), layer, layers)
    branch = {}
    for step, at in zip(steps, first_rows):
        branch.update(zip(step, to_tokens(at, half, len(step), [active_last], [down_w], 0)))
    grad_kv, gate_low, down_low, branch = tie(grad_kv, gate_low, down_low, branch)
    up_parts = jnp.concatenate([q_up_part, kv_up_part], axis=1).reshape(-1, HEADS * LANES)
    up_share = fsdp_scatter(up_parts, core, chip, n).astype(BF16)
    grad_kv_first, kv_gain_part = rms_backward(kv_latent, kv_inverse, kv_gain_all, grad_kv[:, :rank_kv])
    grad_rope = rotate(grad_kv[:, rank_kv + NOPE : rank_kv + NOPE + ROPE], cosine, -sine)
    grad_latent = jnp.concatenate([grad_q_float, grad_kv_first, grad_rope], axis=1).astype(BF16)
    down_all_part = dot(normed, grad_latent, 0, 0)
    grad_normed = dot(grad_latent, down_all, 1, 1)
    grad_in_norm, attn_gain_part = rms_backward(token_rows, attn_inverse, attn_gain_all, grad_normed)
    grad_input = (grad_middle + grad_in_norm).reshape(block_input.shape)

    gain_parts = [v.reshape(n, -1) for v in (attn_gain_part, mlp_gain_part, q_gain_part, kv_gain_part)]
    gain_rows = jnp.concatenate(gain_parts, axis=1)
    gain_rows = jnp.pad(gain_rows[:, None], ((0, 0), (0, 15), (0, latent.shape[1] - gain_rows.shape[1])))
    down_rows = D // n
    down_all_part = jnp.concatenate([down_all_part.reshape(n, down_rows, -1), gain_rows], axis=1)
    down_all_share = fsdp_scatter(down_all_part.reshape(-1, latent.shape[1]), core, chip, n).astype(BF16)
    up_share, out_share, down_all_share, up_low, branch = tie(up_share, out_share, down_all_share, up_low, branch)
    up_grad, out_proj_grad, down_all_grad = (v.astype(F32) for v in lax.psum((up_share, out_share, down_all_share), "seq"))
    down_grad = down_low.astype(F32)
    gate_up_grad = jnp.concatenate([gate_low, up_low], axis=1).astype(F32)
    output = (middle + depth_scale * chip_scatter(branch, n)).astype(BF16).reshape(block_input.shape)
    gain_sum = down_all_grad[down_rows]
    down_all_grad = down_all_grad[:down_rows]
    q_up_grad = up_grad[:q_rows].reshape(-1, HEADS, LANES)[..., : NOPE + ROPE].reshape(-1, HEADS * (NOPE + ROPE))
    kv_up_grad = up_grad[q_rows:]
    ends = [sum(widths[: i + 1]) for i in range(4)]
    attn_gain_grad, mlp_gain_grad, q_gain_grad, kv_gain_grad = jnp.split(gain_sum[: ends[3]], ends[:3])
    return (
        output,
        grad_input,
        attn_gain_grad,
        down_all_grad[:, :rank_q],
        q_gain_grad,
        q_up_grad,
        down_all_grad[:, rank_q:],
        kv_gain_grad,
        kv_up_grad,
        out_proj_grad,
        mlp_gain_grad,
        gate_up_grad,
        down_grad,
    )


def solution(mesh):
    tokens, matrix, vector = P("fsdp", "seq", None), P("fsdp", None), P("fsdp")
    return jax.shard_map(
        functools.partial(body, mesh.shape["fsdp"]),
        mesh=mesh,
        in_specs=(tokens, matrix, vector, matrix, vector, matrix, matrix, vector, matrix, matrix, vector, matrix, matrix, tokens),
        out_specs=(tokens, tokens, vector, matrix, vector, matrix, matrix, vector, matrix, matrix, vector, matrix, matrix),
        check_vma=False,
    )
```

```python
import functools, math
import jax
import jax.numpy as jnp
from jax import lax
from jax.experimental import pallas as pl
from jax.experimental.pallas import tpu as pltpu
from jax.sharding import PartitionSpec as P

HEADS = 40
NOPE = 64
ROPE = 32
PROMPT = 1024
LANES = 128
NEG = -1e30
SCALE = (NOPE + ROPE) ** -0.5
LOG2E = math.log2(math.e)
LN2 = math.log(2.0)


LIGHT = pl.CostEstimate(flops=1 << 20, bytes_accessed=1 << 16, transcendentals=0)


def dot(a, b, ca, cb):
    return lax.dot_general(a, b, (((ca,), (cb,)), ((), ())), preferred_element_type=jnp.float32)


def flat(ref):
    return ref[...].reshape(-1, ref.shape[-1])


def fwd_kernel(bounds, qlat, qup_ref, kvn, kvup_ref, krope, cos, sin_r, sin_l, start, *rest, full_rows, mask_rows):
    out, q_out, lse_out, m_scr, acc_scr = rest[-5:]
    rows = qlat.shape[0]
    lane = lax.broadcasted_iota(jnp.int32, (1, LANES), 1)
    low_half = lane < NOPE
    raw = dot(qlat[...], flat(qup_ref), 1, 0)
    kvup = flat(kvup_ref)
    for h in range(2):
        u = raw[:, h * LANES:(h + 1) * LANES]
        turned = u * cos[...] + pltpu.roll(u, 16, 1) * sin_r[...] + pltpu.roll(u, LANES - 16, 1) * sin_l[...]
        q_out[:, h * LANES:(h + 1) * LANES] = turned.astype(jnp.bfloat16)
    m_scr[...] = jnp.full_like(m_scr, NEG)
    acc_scr[...] = jnp.zeros_like(acc_scr)

    def block(first, size, masked):
        span = pl.ds(first, size)
        kv = dot(kvn[span, :], kvup, 1, 0).astype(jnp.bfloat16)
        rope_rows = krope[span, :]
        if masked:
            key_index = first + lax.broadcasted_iota(jnp.int32, (size, rows), 0)
            own = bounds[3] + lax.broadcasted_iota(jnp.int32, (size, rows), 1)
            allowed = (key_index <= own) & ((key_index >= start[...]) | (key_index < PROMPT))
        scores, vals = [], []
        for h in range(2):
            kv_h = kv[:, h * LANES:(h + 1) * LANES]
            key = jnp.where(low_half, kv_h, rope_rows)
            vals.append(jnp.where(low_half, jnp.ones_like(kv_h), kv_h))
            s = dot(key, q_out[:, h * LANES:(h + 1) * LANES], 1, 1)
            scores.append(jnp.where(allowed, s, NEG) if masked else s)
        for h in range(2):
            m_old = m_scr[h:h + 1, :]
            m_new = jnp.maximum(m_old, jnp.max(scores[h], axis=0, keepdims=True))
            m_scr[h:h + 1, :] = m_new
            p = jnp.exp2(scores[h] - m_new).astype(jnp.bfloat16)
            acc_scr[h] = acc_scr[h] * jnp.exp2(m_old - m_new) + dot(vals[h], p, 0, 0)

    lax.fori_loop(0, bounds[0], lambda i, c: (block(pl.multiple_of(i * full_rows, full_rows), full_rows, False), c)[1], 0)
    lax.fori_loop(bounds[1], bounds[2], lambda i, c: (block(pl.multiple_of(i * mask_rows, mask_rows), mask_rows, True), c)[1], 0)
    parts = []
    for h in range(2):
        total = acc_scr[h, 0:1, :]
        parts.append(acc_scr[h, NOPE:, :] / total)
        lse_out[h:h + 1, :] = m_scr[h:h + 1, :] + jnp.log2(total)
    out[...] = jnp.concatenate(parts, axis=0).T.astype(jnp.bfloat16)


def attend_forward(part, prev, deps, bounds, qlat, up, kvn, krope, cos, sin_r, sin_l, start, full_rows, mask_rows):
    rows, rank = qlat.shape
    q_rows, kv_rows = rank // up.shape[0], kvn.shape[1] // up.shape[0]
    whole = lambda *_: (0, 0)
    first_pair, pairs = part
    col = lambda i, b: (0, i + first_pair)
    return pl.pallas_call(
        functools.partial(fwd_kernel, full_rows=full_rows, mask_rows=mask_rows),
        grid_spec=pltpu.PrefetchScalarGridSpec(
            num_scalar_prefetch=1,
            grid=(pairs,),
            in_specs=[
                pl.BlockSpec((rows, rank), whole),
                pl.BlockSpec((up.shape[0], q_rows, 2 * LANES), lambda i, b: (0, 0, i + first_pair)),
                pl.BlockSpec(kvn.shape, whole),
                pl.BlockSpec((up.shape[0], kv_rows, 2 * LANES), lambda i, b: (0, q_rows // kv_rows, i + first_pair)),
                pl.BlockSpec(krope.shape, whole),
                pl.BlockSpec(cos.shape, whole),
                pl.BlockSpec(cos.shape, whole),
                pl.BlockSpec(cos.shape, whole),
                pl.BlockSpec((1, rows), whole),
            ] + [pl.BlockSpec(memory_space=pl.ANY)] * (len(prev) + len(deps)),
            out_specs=[
                pl.BlockSpec((rows, LANES), col),
                pl.BlockSpec((rows, 2 * LANES), col),
                pl.BlockSpec((8, rows), lambda i, b: (i + first_pair, 0)),
            ],
            scratch_shapes=[pltpu.VMEM((8, rows), jnp.float32), pltpu.VMEM((2, LANES, rows), jnp.float32)],
        ),
        out_shape=[
            jax.ShapeDtypeStruct((rows, HEADS * NOPE), jnp.bfloat16),
            jax.ShapeDtypeStruct((rows, HEADS * LANES), jnp.bfloat16),
            jax.ShapeDtypeStruct((HEADS // 2 * 8, rows), jnp.float32),
        ],
        compiler_params=pltpu.CompilerParams(vmem_limit_bytes=48 << 20),
        cost_estimate=LIGHT,
        input_output_aliases={10 + i: i for i in range(len(prev))},
        name="attend_forward",
    )(bounds, qlat, up, kvn, up, krope, cos, sin_r, sin_l, start, *prev, *deps)


def bwd_kernel(bounds, qlat_t, qup_ref, q, kvn, kvn_t, kvup_ref, krope, grad_out, out, lse, cos, sin_r, sin_l, start, *rest, full_rows, mask_rows, resumes):
    dqup_out, dkvup_out, dkvn, drope, dqlat, go_scr, dq_scr, delta_scr, dkvup = rest[-9:]
    kvup = flat(kvup_ref)
    rows = q.shape[0]
    lane = lax.broadcasted_iota(jnp.int32, (1, LANES), 1)
    low_half = lane < NOPE

    @pl.when(pl.program_id(0) == 0)
    def _():
        dkvn[...] = rest[-12][...] if resumes else jnp.zeros_like(dkvn)
        drope[...] = rest[-11][...] if resumes else jnp.zeros_like(drope)
        dqlat[...] = rest[-10][...] if resumes else jnp.zeros_like(dqlat)

    go = grad_out[...].astype(jnp.float32)
    prod_t = (go * out[...].astype(jnp.float32)).T
    delta_scr[0:1, :] = jnp.sum(prod_t[:NOPE], axis=0, keepdims=True)
    delta_scr[1:2, :] = jnp.sum(prod_t[NOPE:], axis=0, keepdims=True)
    zero = jnp.zeros_like(go)
    go_scr[0] = jnp.where(low_half, zero, pltpu.roll(go, NOPE, 1)).astype(jnp.bfloat16)
    go_scr[1] = jnp.where(low_half, zero, go).astype(jnp.bfloat16)
    dq_scr[...] = jnp.zeros_like(dq_scr)
    dkvup[...] = jnp.zeros_like(dkvup)

    def block(first, size, masked):
        span = pl.ds(first, size)
        kv = dot(kvn[span, :], kvup, 1, 0).astype(jnp.bfloat16)
        rope_rows = krope[span, :]
        if masked:
            key_index = first + lax.broadcasted_iota(jnp.int32, (size, rows), 0)
            own = bounds[3] + lax.broadcasted_iota(jnp.int32, (size, rows), 1)
            allowed = (key_index <= own) & ((key_index >= start[...]) | (key_index < PROMPT))
        pieces = []
        rope_sum = None
        for h in range(2):
            kv_h = kv[:, h * LANES:(h + 1) * LANES]
            q_h = q[:, h * LANES:(h + 1) * LANES]
            key = jnp.where(low_half, kv_h, rope_rows)
            p = jnp.exp2(dot(key, q_h, 1, 1) - lse[h:h + 1, :])
            if masked:
                p = jnp.where(allowed, p, 0.0)
            ds = (p * (dot(kv_h, go_scr[h], 1, 1) - delta_scr[h:h + 1, :])).astype(jnp.bfloat16)
            dk = dot(ds, q_h, 1, 0) * LN2
            dv = dot(p.astype(jnp.bfloat16), go_scr[h], 1, 0)
            dq_scr[h] += dot(key, ds, 0, 0)
            pieces.append(jnp.where(low_half, dk, dv).astype(jnp.bfloat16))
            rope_sum = dk if rope_sum is None else rope_sum + dk
        dkv = jnp.concatenate(pieces, axis=1)
        drope[span, :] += rope_sum
        dkvn[span, :] += dot(dkv, kvup, 1, 1)
        dkvup[...] += dot(kvn_t[:, span], dkv, 1, 0)

    lax.fori_loop(0, bounds[0], lambda i, c: (block(pl.multiple_of(i * full_rows, full_rows), full_rows, False), c)[1], 0)
    lax.fori_loop(bounds[1], bounds[2], lambda i, c: (block(pl.multiple_of(i * mask_rows, mask_rows), mask_rows, True), c)[1], 0)
    turned = []
    for h in range(2):
        u = dq_scr[h].T * SCALE
        turned.append(u * cos[...] - pltpu.roll(u, 16, 1) * sin_r[...] - pltpu.roll(u, LANES - 16, 1) * sin_l[...])
    dq = jnp.concatenate(turned, axis=1).astype(jnp.bfloat16)
    dqlat[...] += dot(dq, flat(qup_ref), 1, 1)
    dqup_out[...] = dot(qlat_t[...], dq, 1, 0).astype(jnp.bfloat16).reshape(dqup_out.shape)
    dkvup_out[...] = dkvup[...].astype(jnp.bfloat16).reshape(dkvup_out.shape)


def attend_backward(part, prev, deps, bounds, qlat_t, up, q, kvn, kvn_t, krope, grad_out, out, lse, cos, sin_r, sin_l, start, full_rows, mask_rows):
    rows = q.shape[0]
    keys, rank = kvn.shape
    devices = up.shape[0]
    q_rows, kv_rows = qlat_t.shape[0] // devices, rank // devices
    up_block = lambda i, b: (0, 0, i + first_pair)
    whole = lambda *_: (0, 0)
    first_pair, pairs = part
    col = lambda i, b: (0, i + first_pair)
    return pl.pallas_call(
        functools.partial(bwd_kernel, full_rows=full_rows, mask_rows=mask_rows, resumes=bool(prev)),
        grid_spec=pltpu.PrefetchScalarGridSpec(
            num_scalar_prefetch=1,
            grid=(pairs,),
            in_specs=[
                pl.BlockSpec(qlat_t.shape, whole),
                pl.BlockSpec((devices, q_rows, 2 * LANES), up_block),
                pl.BlockSpec((rows, 2 * LANES), col),
                pl.BlockSpec(kvn.shape, whole),
                pl.BlockSpec(kvn_t.shape, whole),
                pl.BlockSpec((devices, kv_rows, 2 * LANES), lambda i, b: (0, q_rows // kv_rows, i + first_pair)),
                pl.BlockSpec(krope.shape, whole),
                pl.BlockSpec((rows, LANES), col),
                pl.BlockSpec((rows, LANES), col),
                pl.BlockSpec((8, rows), lambda i, b: (i + first_pair, 0)),
                pl.BlockSpec(cos.shape, whole),
                pl.BlockSpec(cos.shape, whole),
                pl.BlockSpec(cos.shape, whole),
                pl.BlockSpec((1, rows), whole),
            ] + [pl.BlockSpec(memory_space=pl.ANY)] * (len(prev[:2]) + len(deps)) + [pl.BlockSpec(v.shape, whole) for v in prev[2:]],
            out_specs=[
                pl.BlockSpec((devices, q_rows, 2 * LANES), up_block),
                pl.BlockSpec((devices, kv_rows, 2 * LANES), up_block),
                pl.BlockSpec((keys, rank), whole),
                pl.BlockSpec((keys, LANES), whole),
                pl.BlockSpec((rows, qlat_t.shape[0]), whole),
            ],
            scratch_shapes=[
                pltpu.VMEM((2, rows, LANES), jnp.bfloat16),
                pltpu.VMEM((2, LANES, rows), jnp.float32),
                pltpu.VMEM((8, rows), jnp.float32),
                pltpu.VMEM((rank, 2 * LANES), jnp.float32),
            ],
        ),
        out_shape=[
            jax.ShapeDtypeStruct((devices, q_rows, HEADS * LANES), jnp.bfloat16),
            jax.ShapeDtypeStruct((devices, kv_rows, HEADS * LANES), jnp.bfloat16),
            jax.ShapeDtypeStruct((keys, rank), jnp.float32),
            jax.ShapeDtypeStruct((keys, LANES), jnp.float32),
            jax.ShapeDtypeStruct((rows, qlat_t.shape[0]), jnp.float32),
        ],
        compiler_params=pltpu.CompilerParams(vmem_limit_bytes=48 << 20),
        cost_estimate=LIGHT,
        input_output_aliases={15 + i: i for i in range(len(prev[:2]))},
        name="attend_backward",
    )(bounds, qlat_t, up, q, kvn, kvn_t, up, krope, grad_out, out, lse, cos, sin_r, sin_l, start, *prev[:2], *deps, *prev[2:])


def hidden_kernel(*refs, count):
    normed, grads, (gate_w, up_w, down_w) = refs[:count], refs[count : 2 * count], refs[2 * count : 2 * count + 3]
    active, grad_gate, grad_up = refs[-3:]
    height = normed[0].shape[0]
    for i in range(count):
        rows = slice(i * height, (i + 1) * height)
        x = normed[i][...]
        gate = dot(x, gate_w[...], 1, 0)
        upper = dot(x, up_w[...], 1, 0)
        grad = dot(grads[i][...], down_w[...], 1, 1)
        sigmoid = jax.nn.sigmoid(gate)
        silu = gate * sigmoid
        active[rows, :] = (silu * upper).astype(jnp.bfloat16)
        grad_gate[rows, :] = (grad * upper * sigmoid * (1.0 + gate * (1.0 - sigmoid))).astype(jnp.bfloat16)
        grad_up[rows, :] = (grad * silu).astype(jnp.bfloat16)


def hidden_units(first_row, all_rows, prev, normed, grads, gate_w, up_w, down_w):
    count = len(normed)
    height, width = normed[0].shape
    rows, hidden = count * height, gate_w.shape[1]
    tile = 2 * LANES
    whole = lambda j: (0, 0)
    at = first_row // rows
    return pl.pallas_call(
        functools.partial(hidden_kernel, count=count),
        grid=(pl.cdiv(hidden, tile),),
        in_specs=[pl.BlockSpec((height, width), whole)] * (2 * count)
        + [pl.BlockSpec((width, tile), lambda j: (0, j))] * 2
        + [pl.BlockSpec((tile, width), lambda j: (j, 0))]
        + [pl.BlockSpec(memory_space=pl.ANY)] * len(prev),
        out_specs=[pl.BlockSpec((rows, tile), lambda j: (at, j))] * 3,
        out_shape=[jax.ShapeDtypeStruct((all_rows, hidden), jnp.bfloat16)] * 3,
        input_output_aliases={2 * count + 3 + i: i for i in range(len(prev))},
        compiler_params=pltpu.CompilerParams(vmem_limit_bytes=48 << 20),
        cost_estimate=pl.CostEstimate(
            flops=6 * rows * width * hidden, bytes_accessed=6 * width * hidden + 8 * rows * width, transcendentals=0
        ),
        name="hidden_units",
    )(*normed, *grads, gate_w, up_w, down_w, *prev)


def back_kernel(*refs, terms, contract):
    left, right, outs = refs[:terms], refs[terms : 2 * terms], refs[2 * terms :]
    height = outs[0].shape[0]
    for i, out in enumerate(outs):
        rows = slice(i * height, (i + 1) * height)
        total = dot(left[0][rows, :], right[0][...], 1, contract)
        for a, b in zip(left[1:], right[1:]):
            total = total + dot(a[rows, :], b[...], 1, contract)
        out[...] = total.astype(jnp.bfloat16)


def to_tokens(first_row, height, count, left, right, contract):
    hidden = left[0].shape[1]
    width = right[0].shape[1 - contract]
    rows = height * count
    tile = 2 * LANES
    at = first_row // rows
    if contract:
        right_spec = pl.BlockSpec((tile, hidden), lambda j: (j, 0))
    else:
        right_spec = pl.BlockSpec((hidden, tile), lambda j: (0, j))
    return pl.pallas_call(
        functools.partial(back_kernel, terms=len(left), contract=contract),
        grid=(width // tile,),
        in_specs=[pl.BlockSpec((rows, hidden), lambda j: (at, 0))] * len(left) + [right_spec] * len(left),
        out_specs=[pl.BlockSpec((height, tile), lambda j: (0, j))] * count,
        out_shape=[jax.ShapeDtypeStruct((height, width), jnp.bfloat16)] * count,
        compiler_params=pltpu.CompilerParams(vmem_limit_bytes=48 << 20),
        cost_estimate=LIGHT,
        name="to_tokens",
    )(*left, *right)


def blank(shape):
    return pl.pallas_call(
        lambda out: None,
        out_specs=pl.BlockSpec(memory_space=pl.ANY),
        out_shape=jax.ShapeDtypeStruct(shape, jnp.bfloat16),
        cost_estimate=LIGHT,
        name="blank",
    )()


D = 2560
FF = 6400
CONTS = 4
variance_eps = 1e-05
depth_scale = 1.4 / math.sqrt(62.0)
BF16 = jnp.bfloat16
F32 = jnp.float32


def rms_forward(values, gain_vector):
    inverse = lax.rsqrt(jnp.mean(values * values, axis=-1, keepdims=True) + variance_eps)
    return (values * inverse * gain_vector, inverse)


def rms_backward(values, inverse, gain_vector, upstream):
    scaled = upstream * gain_vector
    inner_mean = jnp.mean(scaled * values, axis=-1, keepdims=True)
    grad_values = inverse * scaled - values * inverse * inverse * inverse * inner_mean
    grad_gain = jnp.sum(upstream * values * inverse, axis=0)
    return (grad_values, grad_gain)


def segment_starts(lengths, index):
    own = jnp.zeros_like(index)
    begin = jnp.int32(PROMPT)
    for c in range(CONTS):
        own = jnp.where(index >= begin, begin, own)
        begin = begin + lengths[c]
    return own


def rope_tables(position):
    frequency = jnp.exp(jnp.arange(ROPE // 2, dtype=F32) * (-2.0 * math.log(10000.0) / ROPE))
    angles = position.astype(F32)[:, None] * frequency[None, :]
    cosine, sine = jnp.cos(angles), jnp.sin(angles)
    rows = position.shape[0]
    zeros = lambda n: jnp.zeros((rows, n), F32)
    return (
        jnp.concatenate([jnp.ones((rows, NOPE), F32), cosine, cosine, zeros(32)], axis=1),
        jnp.concatenate([zeros(80), sine, zeros(32)], axis=1),
        jnp.concatenate([zeros(64), -sine, zeros(48)], axis=1),
        cosine,
        sine,
    )


def rotate(values, cosine, sine):
    first, second = values[:, : ROPE // 2], values[:, ROPE // 2 :]
    return jnp.concatenate([first * cosine - second * sine, second * cosine + first * sine], axis=1)


def swap(tensor, bit, n):
    return lax.ppermute(tensor, "fsdp", [(i, i ^ bit) for i in range(n)])


def bit_orders(n):
    bits = []
    bit = 2
    while bit < n:
        bits.append(bit)
        bit *= 2
    return [bits, bits[::-1]]


def arrivals(n):
    orders = bit_orders(n)
    steps = [[(0, part) for part in range(2)]]
    for at in range(len(orders[0])):
        steps.append([
            (r | order[at], part)
            for part, order in enumerate(orders)
            for r in range(0, n, 2)
            if not r & ~sum(order[:at])
        ])
    return steps


BACK_PARTS = ((0, 12), (12, 4), (16, HEADS // 2 - 16))
ATTEND_PARTS = ((0, 4), (4, 7), (11, 5), (16, HEADS // 2 - 16))


def own_blocks(tensor):
    half = tensor.shape[0] // 2
    return {(0, part): tensor[part * half : (part + 1) * half] for part in range(2)}


def gather_step(blocks, n, at):
    return {
        (r | order[at], p): swap(block, order[at], n)
        for part, order in enumerate(bit_orders(n))
        for (r, p), block in blocks.items()
        if p == part
    }


def scatter_step(blocks, n, at, hold=None):
    arrived = {}
    for part, order in enumerate(bit_orders(n)):
        bit = order[at]
        for r, p in blocks:
            if p == part and not r & bit:
                arrived[r, p] = swap(blocks[r | bit, p].astype(BF16), bit, n)
    if hold is not None:
        hold, arrived = tie(hold, arrived)
    return {key: blocks[key].astype(F32) + block.astype(F32) for key, block in arrived.items()}, hold


def chip_scatter(blocks, n):
    for at in range(len(bit_orders(n)[0]))[::-1]:
        blocks, _ = scatter_step(blocks, n, at)
    return jnp.concatenate([blocks[0, part] for part in range(2)])


def tie(*trees):
    return lax.optimization_barrier(trees)


def ring(shift, count):
    return [(i, (i + shift) % count) for i in range(count)]


def seq_gather(share, layer, layers):
    whole = jnp.zeros((layers, *share.shape), share.dtype)
    for shift in range(layers):
        block = lax.ppermute(share, "seq", ring(shift, layers)) if shift else share
        whole = lax.dynamic_update_index_in_dim(whole, block, (layer - shift) % layers, 0)
    return whole.reshape(-1, *share.shape[1:])


def seq_scatter(whole, layer, layers):
    shares = whole.reshape(layers, -1, *whole.shape[1:])
    total = pick(shares, layer).astype(F32)
    for shift in range(1, layers):
        total = total + lax.ppermute(pick(shares, (layer + shift) % layers), "seq", ring(shift, layers)).astype(F32)
    return total


def pick(tensor, at, axis=0):
    return lax.dynamic_index_in_dim(tensor, at, axis, keepdims=False)


def core_scatter(split, core, n, axis=0):
    arrived = swap(pick(split, 1 - core, axis).astype(BF16), 1, n)
    return pick(split, core, axis).astype(F32) + arrived.astype(F32)


def core_shares(part, n):
    return jnp.swapaxes(part.astype(BF16).reshape(n // 2, 2, part.shape[0] // n, part.shape[1]), 0, 1)


def chip_blocks(mine, chip, n):
    half = mine.shape[1] // 2
    blocks = {}
    for r in range(0, n, 2):
        own = pick(mine, chip ^ (r // 2))
        for p in range(2):
            blocks[r, p] = own[p * half : (p + 1) * half]
    return blocks


def fsdp_scatter(part, core, chip, n):
    return chip_scatter(chip_blocks(core_scatter(core_shares(part, n), core, n).astype(BF16), chip, n), n)


def body(
    n,
    block_input,
    cont_lengths,
    attn_gain,
    q_down,
    q_gain,
    q_up,
    kv_down,
    kv_gain,
    kv_up,
    out_proj,
    mlp_gain,
    gate_up,
    down_proj,
    out_cotangent,
):
    rows = block_input.shape[1]
    chips = n // 2
    ff_chip = FF // chips
    ff_sent = -(-ff_chip // LANES) * LANES
    ff_wide = ff_sent
    group_len = rows * lax.axis_size("seq")
    device = lax.axis_index("fsdp")
    core, chip = device % 2, device // 2
    layers = lax.axis_size("seq")
    layer = lax.axis_index("seq")
    rank_q, rank_kv = q_up.shape[0] * n, kv_up.shape[0] * n
    first_row = lax.axis_index("seq") * rows
    index = first_row + jnp.arange(rows, dtype=jnp.int32)
    own_start = segment_starts(cont_lengths[0], index)
    position = jnp.where(own_start > 0, PROMPT + index - own_start, index)
    cos, sin_r, sin_l, cosine, sine = rope_tables(position)
    fold = SCALE * LOG2E
    start_row = own_start[None, :]
    full_rows, mask_rows = 1024, 512
    full_blocks = jnp.minimum(first_row, PROMPT) // full_rows
    bounds = jnp.stack([
        full_blocks,
        jnp.where(first_row < PROMPT, full_blocks * (full_rows // mask_rows), own_start[0] // mask_rows),
        (first_row + rows + mask_rows - 1) // mask_rows,
        first_row,
    ]).astype(jnp.int32)

    gains = lax.all_gather(jnp.concatenate([attn_gain, mlp_gain, q_gain, kv_gain]), "fsdp", axis=0)
    widths = [v.shape[0] for v in (attn_gain, mlp_gain, q_gain, kv_gain)]
    gain_list = []
    at = 0
    for width in widths:
        gain_list.append(gains[:, at : at + width].reshape(-1).astype(F32))
        at += width
    attn_gain_all, mlp_gain_all, q_gain_all, kv_gain_all = gain_list

    down_all = lax.all_gather(jnp.concatenate([q_down, kv_down], axis=1), "fsdp", axis=0, tiled=True)
    q_up_wide = jnp.pad(q_up.reshape(-1, HEADS, NOPE + ROPE), ((0, 0), (0, 0), (0, ROPE))).reshape(-1, HEADS * LANES)
    q_rows = q_up.shape[0]
    up_all = lax.all_gather(jnp.concatenate([q_up_wide, kv_up], axis=0), "fsdp", axis=0)
    out_proj_all = lax.all_gather(out_proj, "fsdp", axis=0, tiled=True)

    steps = arrivals(n)
    fetch = (D // n) // layers
    half_down = swap(down_proj, 1, n)
    down_w = jnp.concatenate([
        jnp.where(core == 0, down_proj, half_down),
        jnp.where(core == 0, half_down, down_proj),
        jnp.zeros((ff_wide - ff_chip, D), BF16),
    ])
    own_fetch = lax.dynamic_slice_in_dim(gate_up, layer * fetch, fetch, 0)
    widen = lambda v: jnp.pad(v, ((0, 0), (0, ff_sent - ff_chip)))
    own_fetch = jnp.stack([
        jnp.stack([widen(own_fetch[:, at + c * ff_chip : at + (c + 1) * ff_chip]) for at in (0, FF)]) for c in range(chips)
    ])
    own_fetch = [pick(own_fetch, chip ^ (r // 2)) for r in range(0, n, 2)]
    tables = (cos * fold, sin_r * fold, sin_l * fold, cos, sin_r, sin_l)
    down_all, tables, down_w, own_fetch = tie(down_all, tables, down_w, own_fetch)

    token_rows = block_input[0].astype(F32)
    normed_float, attn_inverse = rms_forward(token_rows, attn_gain_all)
    normed = normed_float.astype(BF16)
    latent = jnp.dot(normed, down_all, preferred_element_type=F32)
    q_latent, kv_latent, rope_latent = jnp.split(latent, [rank_q, rank_q + rank_kv], axis=1)
    q_lat_float, q_inverse = rms_forward(q_latent, q_gain_all)
    q_lat_normed = q_lat_float.astype(BF16)
    kv_float, kv_inverse = rms_forward(kv_latent, kv_gain_all)
    key_rope = jnp.pad(rotate(rope_latent, cosine, sine), ((0, 0), (NOPE, LANES - NOPE - ROPE)))
    kv_own = jnp.concatenate([kv_float, key_rope], axis=1).astype(BF16)
    kv_all = seq_gather(kv_own, layer, layers)
    cotangent = out_cotangent[0].astype(F32)
    grad_low = (depth_scale * cotangent).astype(BF16)
    up_all, kv_all, own_fetch, grad_low = tie(up_all, kv_all, own_fetch, grad_low)
    kv_normed, key_rope_all = kv_all[:, :rank_kv], kv_all[:, rank_kv:]
    forward_args = (
        bounds, q_lat_normed, up_all, kv_normed, key_rope_all,
        *tables[:3], start_row, full_rows, mask_rows,
    )

    fetched_blocks = [swap(block, 2 * r, n) if r else block for r, block in enumerate(own_fetch)]
    outputs = attend_forward(ATTEND_PARTS[0], [], [], *forward_args)
    grad_blocks = own_blocks(grad_low)
    moved = gather_step(grad_blocks, n, 0)
    outputs, fetched_blocks = tie(outputs, fetched_blocks)
    fetched = blank((2, chips, fetch, ff_sent))
    for r, block in enumerate(fetched_blocks):
        fetched = lax.dynamic_update_slice(fetched, block[:, None], (0, chip ^ r, 0, 0))
    passed = [(fetched, fetched)]
    for step in range(1, layers):
        link = (
            lax.ppermute(passed[-1][0], "seq", [(i, i + 1) for i in range(layers - 1)]),
            lax.ppermute(passed[-1][1], "seq", [(i + 1, i) for i in range(layers - 1)]),
        )
        if step < len(ATTEND_PARTS):
            outputs = attend_forward(ATTEND_PARTS[step], outputs, [], *forward_args)
            if step < layers - 1:
                outputs, link = tie(outputs, link)
            if step == 1:
                outputs, moved, turned = tie(outputs, moved, (q_lat_normed.T, kv_normed.T))
                grad_blocks = {**grad_blocks, **moved}
        passed.append(link)
    for part in ATTEND_PARTS[layers:]:
        outputs = attend_forward(part, outputs, [], *forward_args)
    attended, queries, log_total = outputs
    for at in range(1, len(steps) - 1):
        grad_blocks = {**grad_blocks, **gather_step(grad_blocks, n, at)}
    attn_branch = jnp.dot(attended, out_proj_all, preferred_element_type=F32)
    attn_branch, grad_blocks, passed = tie(attn_branch, grad_blocks, passed)
    middle = token_rows + depth_scale * attn_branch
    mlp_float, mlp_inverse = rms_forward(middle, mlp_gain_all)
    normed_blocks = own_blocks(mlp_float.astype(BF16))
    normed_blocks = {**normed_blocks, **gather_step(normed_blocks, n, 0)}
    layer_blocks = [jnp.where(layer >= shift, passed[shift][0], passed[layers - shift][1]) for shift in range(1, layers)]
    for at in range(1, len(steps) - 1):
        normed_blocks = {**normed_blocks, **gather_step(normed_blocks, n, at)}
    hidden = [blank((chips, 2, layers, fetch, ff_wide)) for _ in range(2)]
    for shift in range(layers):
        block = layer_blocks[shift - 1] if shift else fetched
        source = (layer - shift) % layers
        for owner, arrived in ((core, block), (1 - core, swap(block, 1, n))):
            hidden = [
                lax.dynamic_update_slice(whole, v[:, None, None], (0, owner, source, 0, 0)) for whole, v in zip(hidden, arrived)
            ]
    gate_w, up_w = (v.reshape(D, ff_wide) for v in hidden)
    half = rows // 2
    first_rows = [sum(len(step) for step in steps[:i]) * half for i in range(len(steps))]
    kept = []
    for step, at in zip(steps, first_rows):
        kept = hidden_units(
            at, n * half, kept, [normed_blocks[key] for key in step], [grad_blocks[key] for key in step], gate_w, up_w, down_w
        )
    active, grad_gate, grad_up = kept
    all_normed = jnp.concatenate([normed_blocks[key] for step in steps for key in step])
    all_grad = jnp.concatenate([grad_blocks[key] for step in steps for key in step])

    back = lambda i, hidden: dict(zip(steps[i], to_tokens(first_rows[i], half, len(steps[i]), hidden, [gate_w, up_w], 1)))
    last_blocks = back(-1, [grad_gate, grad_up])
    last_blocks, active_late, earlier = tie(last_blocks, active, [grad_gate, grad_up])
    down_whole = dot(active_late, all_grad, 0, 0).astype(BF16)
    last_blocks, earlier = tie(last_blocks, [grad_gate, grad_up])
    half_ff = ff_chip // 2
    half_of = lambda at: lax.dynamic_slice_in_dim(down_whole, at * half_ff, half_ff, 0)
    down_part = (half_of(core).astype(F32) + swap(half_of(1 - core), 1, n).astype(F32)).astype(BF16)
    early_blocks = {}
    for i in range(len(steps) - 1)[::-1]:
        early_blocks.update(back(i, earlier))
    blocks, _ = scatter_step({**last_blocks, **early_blocks}, n, len(steps) - 2)
    blocks, all_normed, down_part = tie(blocks, all_normed, down_part)
    down_share = lax.psum_scatter(down_part, "seq", scatter_dimension=0, tiled=True)
    hidden_parts, hidden_shares, crossing = [], [], []
    for grads in (grad_gate, grad_up):
        whole = dot(all_normed, grads, 0, 0).astype(BF16).reshape(chips, 2, layers, fetch, ff_wide)
        if crossing:
            for at in range(len(steps) - 2)[::-1]:
                blocks, (whole, down_share, crossing[0]) = scatter_step(blocks, n, at, (whole, down_share, crossing[0]))
        crossing.append((pick(whole, core, 1), swap(pick(whole, 1 - core, 1), 1, n)))

    def over_layers(crossed):
        part = (crossed[0].astype(F32) + crossed[1].astype(F32)).astype(BF16).transpose(1, 0, 2, 3)
        hidden_parts.append(part)
        hidden_shares.append(lax.psum_scatter(part, "seq", scatter_dimension=0, tiled=True)[0])

    over_layers(crossing[0])
    grad_mlp_normed = jnp.concatenate([blocks[0, part] for part in range(2)]).astype(F32)
    grad_mid_norm, mlp_gain_part = rms_backward(middle, mlp_inverse, mlp_gain_all, grad_mlp_normed)
    grad_middle = cotangent + grad_mid_norm
    grad_attn = (depth_scale * grad_middle).astype(BF16)
    out_proj_part = dot(attended, grad_attn, 0, 0).astype(BF16)
    grad_attended = dot(grad_attn, out_proj_all, 1, 1).astype(BF16)
    grad_attended, crossing[1] = tie(grad_attended, crossing[1])
    over_layers(crossing[1])
    backward_args = (
        bounds, turned[0], up_all, queries, kv_normed, turned[1], key_rope_all, grad_attended, attended, log_total,
        *tables[3:], start_row, full_rows, mask_rows,
    )
    out_shares = core_shares(out_proj_part, n)
    out_arrived = swap(pick(out_shares, 1 - core), 1, n)
    first = attend_backward(BACK_PARTS[0], [], [*hidden_parts, out_proj_part], *backward_args)
    down_low = lax.all_gather(down_share, "seq", axis=0, tiled=True)
    first, hidden_shares, down_share, out_arrived = tie(first, hidden_shares, down_share, out_arrived)
    out_mine = (pick(out_shares, core).astype(F32) + out_arrived.astype(F32)).astype(BF16)
    first, out_mine = tie(first, out_mine)
    hidden_share = jnp.stack(hidden_shares)
    hidden_blocks = [pick(hidden_share, chip ^ (r // 2), 1) for r in range(0, n, 2)]
    hidden_blocks = [swap(block, 2 * r, n) if r else block for r, block in enumerate(hidden_blocks)]
    second = attend_backward(BACK_PARTS[1], first, [down_share], *backward_args)
    second, hidden_blocks = tie(second, hidden_blocks)
    hidden_blocks = jnp.stack(hidden_blocks)
    hidden_blocks = [pick(hidden_blocks, chip ^ c)[..., :ff_chip] for c in range(chips)]
    placed = [jnp.concatenate([block[at] for block in hidden_blocks], axis=1) for at in range(2)]
    gate_low, up_low = (lax.all_gather(v, "seq", axis=0, tiled=True) for v in placed)
    third = attend_backward(BACK_PARTS[2], second, placed, *backward_args)
    out_blocks, third = scatter_step(chip_blocks(out_mine, chip, n), n, len(steps) - 2, third)
    for at in range(len(steps) - 2)[::-1]:
        out_blocks, _ = scatter_step(out_blocks, n, at)
    out_share = jnp.concatenate([out_blocks[0, part] for part in range(2)]).astype(BF16)
    third, active_last = tie(third, active)
    q_up_part, kv_up_part, grad_kv_all, grad_rope_all, grad_q_lat = third
    grad_q_float, q_gain_part = rms_backward(q_latent, q_inverse, q_gain_all, grad_q_lat)
    grad_kv = seq_scatter(jnp.concatenate([grad_kv_all, grad_rope_all], axis=1).astype(BF16), layer, layers)
    branch = {}
    for step, at in zip(steps, first_rows):
        branch.update(zip(step, to_tokens(at, half, len(step), [active_last], [down_w], 0)))
    grad_kv, gate_low, down_low, branch = tie(grad_kv, gate_low, down_low, branch)
    up_parts = jnp.concatenate([q_up_part, kv_up_part], axis=1).reshape(-1, HEADS * LANES)
    up_share = fsdp_scatter(up_parts, core, chip, n).astype(BF16)
    grad_kv_first, kv_gain_part = rms_backward(kv_latent, kv_inverse, kv_gain_all, grad_kv[:, :rank_kv])
    grad_rope = rotate(grad_kv[:, rank_kv + NOPE : rank_kv + NOPE + ROPE], cosine, -sine)
    grad_latent = jnp.concatenate([grad_q_float, grad_kv_first, grad_rope], axis=1).astype(BF16)
    down_all_part = dot(normed, grad_latent, 0, 0)
    grad_normed = dot(grad_latent, down_all, 1, 1)
    grad_in_norm, attn_gain_part = rms_backward(token_rows, attn_inverse, attn_gain_all, grad_normed)
    grad_input = (grad_middle + grad_in_norm).reshape(block_input.shape)

    gain_parts = [v.reshape(n, -1) for v in (attn_gain_part, mlp_gain_part, q_gain_part, kv_gain_part)]
    gain_rows = jnp.concatenate(gain_parts, axis=1)
    gain_rows = jnp.pad(gain_rows[:, None], ((0, 0), (0, 15), (0, latent.shape[1] - gain_rows.shape[1])))
    down_rows = D // n
    down_all_part = jnp.concatenate([down_all_part.reshape(n, down_rows, -1), gain_rows], axis=1)
    down_all_share = fsdp_scatter(down_all_part.reshape(-1, latent.shape[1]), core, chip, n).astype(BF16)
    up_share, out_share, down_all_share, up_low, branch, down_grad = tie(
        up_share, out_share, down_all_share, up_low, branch, down_low.astype(F32)
    )
    up_grad, out_proj_grad, down_all_grad = (v.astype(F32) for v in lax.psum((up_share, out_share, down_all_share), "seq"))
    gate_up_grad = jnp.concatenate([gate_low, up_low], axis=1).astype(F32)
    output = (middle + depth_scale * chip_scatter(branch, n)).astype(BF16).reshape(block_input.shape)
    gain_sum = down_all_grad[down_rows]
    down_all_grad = down_all_grad[:down_rows]
    q_up_grad = up_grad[:q_rows].reshape(-1, HEADS, LANES)[..., : NOPE + ROPE].reshape(-1, HEADS * (NOPE + ROPE))
    kv_up_grad = up_grad[q_rows:]
    ends = [sum(widths[: i + 1]) for i in range(4)]
    attn_gain_grad, mlp_gain_grad, q_gain_grad, kv_gain_grad = jnp.split(gain_sum[: ends[3]], ends[:3])
    return (
        output,
        grad_input,
        attn_gain_grad,
        down_all_grad[:, :rank_q],
        q_gain_grad,
        q_up_grad,
        down_all_grad[:, rank_q:],
        kv_gain_grad,
        kv_up_grad,
        out_proj_grad,
        mlp_gain_grad,
        gate_up_grad,
        down_grad,
    )


def solution(mesh):
    tokens, matrix, vector = P("fsdp", "seq", None), P("fsdp", None), P("fsdp")
    return jax.shard_map(
        functools.partial(body, mesh.shape["fsdp"]),
        mesh=mesh,
        in_specs=(tokens, matrix, vector, matrix, vector, matrix, matrix, vector, matrix, matrix, vector, matrix, matrix, tokens),
        out_specs=(tokens, tokens, vector, matrix, vector, matrix, matrix, vector, matrix, matrix, vector, matrix, matrix),
        check_vma=False,
    )
```
